256 devices in a mesh: gx: 16 (over x_hi, y, core), gz: 16 (over z, x_lo).
Axes of the slice: x: 4 (x_hi: 2, x_lo: 2; x = x_hi * 2 + x_lo), y: 4, z: 8, core: 2. Of those that a mesh axis runs over, the one named last changes fastest.
Arguments:
- vertical_now: float32 [640, 16, 2048], P('gz', None, 'gx'), may hold values from -6 to 6
- vertical_section: float32 [640, 16, 2048], P('gz', None, 'gx'), may hold values from -6 to 6
- theta_now: float32 [640, 16, 2048], P('gz', None, 'gx'), may hold values from -6 to 6
- theta_section: float32 [640, 16, 2048], P('gz', None, 'gx'), may hold values from -6 to 6
- east_wind: bfloat16 [640, 16, 2048], P('gz', None, 'gx'), may hold values from -5 to 5
- north_wind: bfloat16 [640, 16, 2048], P('gz', None, 'gx'), may hold values from -5 to 5
- eddy_viscosity: bfloat16 [640, 16, 2048], P('gz', None, 'gx'), may hold values from 0.019897461 to 0.19921875
- density: float32 [640], P('gz'), may hold values from 0.7 to 1.4
- coupling: float32 [640], P('gz'), may hold values from 10 to 200
- cloud_top: int32 [16, 16], P(None, 'gx'), may hold values from 160 to 479
Outputs:
- vertical_next: float32 [640, 16, 2048], P('gz', None, 'gx')
- theta_next: float32 [640, 16, 2048], P('gz', None, 'gx')
The draws below stay inside these ranges and needn't reach their ends.
All inputs are finite; a program needn't handle non-finite values.
Results may differ from the reference program's by a relative error of at most 0.0003.
Values may be sent and summed in bfloat16 or wider, within the bound.
No kernel may reach another device: no remote copies, remote signals or barrier semaphores. Data moves between devices by JAX's collectives and lax.ppermute only.
A program may use at most 64 MiB of HBM per device.

```python
import math
import jax
import jax.numpy as jnp
from jax import lax

CX = 128
NY = 16
NX = 2048
NZ = 640
N_GX = 16


def touch_ends(array, key, smallest, top_value):
    dims = array.shape
    place = [jax.random.randint(jax.random.fold_in(key, axis), (), 0, dims[axis]) for axis in range(len(dims))]
    array = array.at[tuple(place)].set(smallest)
    longest = dims.index(max(dims))
    place[longest] = (place[longest] + 1) % dims[longest]
    return array.at[tuple(place)].set(top_value)


def block_levels(own_key, shape, shards, smallest, top_value):
    level, own = 1.0, jax.random.fold_in(own_key, 6)
    for dim, blocks in shards:
        draws = jnp.exp(jax.random.uniform(jax.random.fold_in(own, dim), (blocks,), jnp.float32, smallest / len(shards), top_value / len(shards)))
        level = level * jnp.repeat(draws, shape[dim] // blocks).reshape([-1 if axis == dim else 1 for axis in range(len(shape))])
    return level


def normal_values(key, extent, deviation, bound, cuts=(), kind=jnp.bfloat16):
    drawn = jax.random.normal(key, extent, jnp.float32) * deviation
    if len(cuts) > 0:
        drawn = block_levels(key, extent, cuts, -0.22, 0.18) * drawn
    return jnp.clip(drawn, min=-bound, max=bound).astype(kind)


def setup_inputs(seed: int = 0) -> dict:
    keys = jax.random.split(jax.random.key(seed), 11)
    vertical_now = normal_values(keys[0], (NZ, NY, NX), 1.0, 6.0, ((0, 16), (2, 16)), jnp.float32)
    vertical_section = normal_values(keys[1], (NZ, NY, NX), 1.0, 6.0, ((0, 16), (2, 16)), jnp.float32)
    theta_now = normal_values(keys[2], (NZ, NY, NX), 1.0, 6.0, ((0, 16), (2, 16)), jnp.float32)
    theta_section = normal_values(keys[3], (NZ, NY, NX), 1.0, 6.0, ((0, 16), (2, 16)), jnp.float32)
    east_wind = normal_values(keys[4], (NZ, NY, NX), 1.0, 5.0, ((0, 16), (2, 16)))
    north_wind = normal_values(keys[5], (NZ, NY, NX), 1.0, 5.0, ((0, 16), (2, 16)))
    eddy_viscosity = jnp.clip(jnp.exp(math.log(0.19921875) - 2.3038113 * jax.random.uniform(keys[6], (NZ, NY, NX), jnp.float32) ** block_levels(keys[6], (NZ, NY, NX), ((0, 16), (2, 16)), -0.2, 0.2)), 0.019897461, 0.19921875).astype(jnp.bfloat16)
    density = jnp.clip(jnp.exp(math.log(1.4) - 0.6931472 * jax.random.uniform(keys[7], (NZ,), jnp.float32) ** block_levels(keys[7], (NZ,), ((0, 16),), -0.2, 0.2)), 0.7, 1.4)
    coupling = jnp.clip(jnp.exp(math.log(200.0) - 2.9957323 * jax.random.uniform(keys[8], (NZ,), jnp.float32) ** block_levels(keys[8], (NZ,), ((0, 16),), -0.2, 0.2)), 10.0, 200.0)
    cloud_top = touch_ends(jax.random.randint(keys[9], (NY, N_GX), NZ // 4, 3 * NZ // 4), jax.random.fold_in(keys[9], 1), NZ // 4, (3 * NZ // 4) - 1).astype(jnp.int32)
    return dict(vertical_now=vertical_now, vertical_section=vertical_section, theta_now=theta_now, theta_section=theta_section, east_wind=east_wind, north_wind=north_wind, eddy_viscosity=eddy_viscosity, density=density, coupling=coupling, cloud_top=cloud_top)


COURANT = 0.25
MIXED_BOOST = 4.0
HEAT_RATIO = 3.0


def face_flux(shifted, face_speed, mixing):
    ahead_face = (2.0 * shifted(-2) - 13.0 * shifted(-1) + 47.0 * shifted(0) + 27.0 * shifted(1) - 3.0 * shifted(2)) / 60.0
    behind = (2.0 * shifted(3) - 13.0 * shifted(2) + 47.0 * shifted(1) + 27.0 * shifted(0) - 3.0 * shifted(-1)) / 60.0
    upwind = jnp.where(face_speed >= 0.0, ahead_face, behind)
    return COURANT * face_speed * upwind - mixing * (shifted(1) - shifted(0))


def periodic_change(values, velocity, viscous, axis_pos):
    def shifted(offset):
        return jnp.roll(values, -offset, axis=axis_pos)
    face_speed = 0.5 * (velocity + jnp.roll(velocity, -1, axis=axis_pos))
    mixing = 0.5 * (viscous + jnp.roll(viscous, -1, axis=axis_pos))
    face_fluxes = face_flux(shifted, face_speed, mixing)
    return face_fluxes - jnp.roll(face_fluxes, 1, axis=axis_pos)


def face_coef(height, coupled, ceiling, factor):
    return factor * coupled * jnp.where(height <= ceiling, MIXED_BOOST + 1.0, 1.0)


def column_solve(source, density, lower_faces, upper_faces, ceiling, factor, first_level):
    layers = source.shape[0]
    heights = first_level + jnp.arange(layers, dtype=jnp.int32)

    def forward(state_pair, member):
        ratio_prev, solved_prev = state_pair
        height, right_side, weight, low_value, high_value = member
        low_coef = face_coef(height, low_value, ceiling, factor)
        high_coef = face_coef(height + 1, high_value, ceiling, factor)
        pivot_value = weight + low_coef + high_coef - low_coef * ratio_prev
        ratio_next = high_coef / pivot_value
        solved = (right_side + low_coef * solved_prev) / pivot_value
        return (ratio_next, solved), (ratio_next, solved)

    start_state = (jnp.zeros(source.shape[-2:], jnp.float32), jnp.zeros(source.shape[1:], jnp.float32))
    final_state, (ratios, eliminated) = lax.scan(forward, start_state, (heights, source, density, lower_faces, upper_faces))

    def backward(following, member):
        ratio_here, solved = member
        current = solved + ratio_here * following
        return current, current

    final_top, result = lax.scan(backward, jnp.zeros(source.shape[1:], jnp.float32), (ratios, eliminated), reverse=True)
    return result


def reference(vertical_now, vertical_section, theta_now, theta_section, east_wind, north_wind, eddy_viscosity, density, coupling, cloud_top):
    def level_update(member):
        old_vertical, mid_vertical, old_theta, mid_theta, east_level, north_level, viscous_level = member
        section_pair = jnp.stack([mid_vertical, mid_theta])
        former = jnp.stack([old_vertical, old_theta])
        viscous = viscous_level.astype(jnp.float32)
        along_x = periodic_change(section_pair, east_level.astype(jnp.float32), viscous, -1)
        along_y = periodic_change(section_pair, north_level.astype(jnp.float32), viscous, -2)
        change = -(along_x + along_y)
        return former / 3.0 + 2.0 * (section_pair + change) / 3.0

    explicit = lax.map(level_update, (vertical_now, vertical_section, theta_now, theta_section, east_wind, north_wind, eddy_viscosity))
    heights = jnp.arange(NZ, dtype=jnp.int32)
    lower_faces = jnp.where(heights >= 1, coupling, 0.0)
    upper_faces = jnp.concatenate([coupling[1:], jnp.zeros((1,), jnp.float32)])
    ceiling = jnp.repeat(cloud_top, CX, axis=1)
    vertical_next = column_solve(density[:, None, None] * explicit[:, 0], density, lower_faces, upper_faces, ceiling, 1.0, 0)
    theta_next = column_solve(density[:, None, None] * explicit[:, 1], density, lower_faces, upper_faces, ceiling, HEAT_RATIO, 0)
    return (vertical_next, theta_next)
```

```python
import functools

import jax
import jax.numpy as jnp
from jax import lax
from jax.experimental import pallas as pl
from jax.experimental.pallas import tpu as pltpu
from jax.sharding import PartitionSpec as P

COURANT = 0.25
MIXED_BOOST = 4.0
HEAT_RATIO = 3.0
RATIOS = (1.0, HEAT_RATIO)
LEVELS = 40
ROWS = 16
LANES = 128
CELLS = LEVELS * ROWS
STATE = 5 * ROWS
VMEM = pl.BlockSpec(memory_space=pltpu.VMEM)
SMEM = pl.BlockSpec(memory_space=pltpu.SMEM)
PARAMS = pltpu.CompilerParams(vmem_limit_bytes=32 * 1024 * 1024)
F32 = jnp.float32


def iota(shape, dim):
    return lax.broadcasted_iota(jnp.int32, shape, dim)


def split3(x, axis):
    high = x.astype(jnp.bfloat16)
    rest = x - high.astype(F32)
    mid = rest.astype(jnp.bfloat16)
    low = (rest - mid.astype(F32)).astype(jnp.bfloat16)
    return jnp.concatenate([high, mid, low], axis=axis)


def flux(qs, speed_sum, mixing_sum):
    qm2, qm1, q0, q1, q2, q3 = qs
    speed = speed_sum * (0.5 * COURANT / 60.0)
    step = q0 - q1
    mean = (qm2 + q3) - 8.0 * (qm1 + q2) + 37.0 * (q0 + q1)
    skew = (qm2 - q3) - 5.0 * (qm1 - q2) + 10.0 * step
    return speed * mean + jnp.abs(speed) * skew + (0.5 * mixing_sum) * step


def strip_selectors():
    rows = [[-1] * 64 for _ in range(4)]
    for field in range(2):
        for cell in range(3):
            rows[field][3 * field + cell] = cell
            rows[field][8 + 3 * field + cell] = LANES - 3 + cell
        for cell in range(5):
            rows[field][16 + 16 * field + 3 + cell] = cell
            rows[field][24 + 16 * field + cell] = LANES - 5 + cell
    for kind in range(2):
        rows[2 + kind][6 + kind] = 0
        rows[2 + kind][14 + kind] = LANES - 1
        for cell in range(3):
            rows[2 + kind][48 + 8 * kind + 1 + cell] = cell
            rows[2 + kind][48 + 8 * kind + 4 + cell] = LANES - 3 + cell
    return rows


def lane_selector(lanes):
    row = iota((len(lanes), LANES), 0)
    lane = iota((len(lanes), LANES), 1)
    hit = jnp.zeros((len(lanes), LANES), jnp.bool_)
    start = 0
    while start < len(lanes):
        if lanes[start] < 0:
            start += 1
            continue
        stop = start + 1
        while stop < len(lanes) and lanes[stop] == lanes[stop - 1] + 1:
            stop += 1
        hit = hit | ((row >= start) & (row < stop) & (lane - row == lanes[start] - start))
        start = stop
    return jnp.where(hit, 1.0, 0.0).astype(jnp.bfloat16)


def pick_lanes(select, x):
    dims = (((1,), (1,)), ((), ()))
    if x.dtype == jnp.bfloat16:
        return lax.dot_general(select, x, dims, preferred_element_type=F32)
    high = x.astype(jnp.bfloat16)
    rest = x - high.astype(F32)
    mid = rest.astype(jnp.bfloat16)
    low = (rest - mid.astype(F32)).astype(jnp.bfloat16)
    parts = [lax.dot_general(select, p, dims, preferred_element_type=F32) for p in (high, mid, low)]
    return parts[0] + (parts[1] + parts[2])


def pack_kernel(w_ref, t_ref, east_ref, visc_ref, near_ref, far_ref, own_ref):
    odd = lax.rem(lax.axis_index("gx"), 2)
    rows = strip_selectors()
    total = None
    for ref, lanes in zip((w_ref, t_ref, east_ref, visc_ref), rows):
        part = pick_lanes(lane_selector(lanes), ref[...].reshape(CELLS, LANES))
        total = part if total is None else total + part
    left, right = total[0:8], total[8:16]
    is_odd = odd == 1
    near_ref[...] = jnp.where(is_odd, left, right)
    far_ref[...] = jnp.where(is_odd, right, left)
    own_ref[...] = total[16:]


def main_kernel(
    wn_ref, ws_ref, tn_ref, ts_ref, east_ref, north_ref, visc_ref, dens_ref, coup_ref, top_ref,
    rhs_ref, up_ref, down_ref, sums_ref, dense_ref, packed_ref,
):
    first = lax.axis_index("gz") * LEVELS
    tile = (ROWS, LANES)
    top = jnp.broadcast_to(top_ref[...], tile)
    lane = iota(tile, 1)
    one = jnp.ones(tile, F32)

    def resist(k):
        boost = jnp.where(first + k <= top, 1.0 / (1.0 + MIXED_BOOST), 1.0)
        return boost / (one * coup_ref[k])

    u = [one, one]
    v = [one, one]
    n = [one * dens_ref[0]] * 2
    m = [one * dens_ref[LEVELS - 1]] * 2
    for f in range(2):
        up_ref[f, 0] = u[f]
        down_ref[f, LEVELS - 1] = v[f]
    for k in range(1, LEVELS):
        j = LEVELS - 1 - k
        res_u = resist(k)
        res_v = resist(j + 1)
        for f in range(2):
            u[f] = u[f] + n[f] * (res_u * (1.0 / RATIOS[f]))
            n[f] = n[f] + dens_ref[k] * u[f]
            up_ref[f, k] = u[f]
            v[f] = v[f] + m[f] * (res_v * (1.0 / RATIOS[f]))
            m[f] = m[f] + dens_ref[j] * v[f]
            down_ref[f, j] = v[f]
    inv = [1.0 / n[f] for f in range(2)]

    for k in range(LEVELS):
        packed = jnp.where(lane < 16, up_ref[0, k] * inv[0], down_ref[0, k] * inv[0])
        packed = jnp.where(lane < 32, packed, up_ref[1, k] * inv[1])
        packed = jnp.where(lane < 48, packed, down_ref[1, k] * inv[1])
        packed = jnp.where(lane < 64, packed, one * dens_ref[k])
        packed_ref[k] = packed
    dense_ref[...] = pick_lanes(
        lane_selector([0, 16, 32, 48, 64, -1, -1, -1]), packed_ref[...].reshape(CELLS, LANES)
    )

    inside = (lane >= 2) & (lane <= LANES - 4)

    def level(k, carry):
        east = east_ref[k].astype(F32)
        north = north_ref[k].astype(F32)
        visc = visc_ref[k].astype(F32)
        east_sum = jnp.where(inside, east + pltpu.roll(east, LANES - 1, 1), 0.0)
        visc_x = jnp.where(inside, visc + pltpu.roll(visc, LANES - 1, 1), 0.0)
        north_sum = north + pltpu.roll(north, ROWS - 1, 0)
        visc_y = visc + pltpu.roll(visc, ROWS - 1, 0)
        weight = dens_ref[k]
        out = []
        for f, (now_ref, sec_ref) in enumerate(((wn_ref, ws_ref), (tn_ref, ts_ref))):
            q = sec_ref[k]
            qx = [q if s == 0 else pltpu.roll(q, (-s) % LANES, 1) for s in range(-2, 4)]
            fx = flux(qx, east_sum, visc_x)
            qy = [q if s == 0 else pltpu.roll(q, (-s) % ROWS, 0) for s in range(-2, 4)]
            fy = flux(qy, north_sum, visc_y)
            change = (pltpu.roll(fx, 1, 1) - fx) + (pltpu.roll(fy, 1, 0) - fy)
            explicit = now_ref[k] * (1.0 / 3.0) + (q + change) * (2.0 / 3.0)
            b = explicit * weight
            rhs_ref[f, k] = b
            out.append(carry[2 * f] + down_ref[f, k] * b)
            out.append(carry[2 * f + 1] + up_ref[f, k] * b)
        return tuple(out)

    zero = jnp.zeros(tile, F32)
    sums = lax.fori_loop(0, LEVELS, level, (zero,) * 4)
    for f in range(2):
        sums_ref[f * ROWS:(f + 1) * ROWS] = sums[2 * f] * inv[f]
        sums_ref[(2 + f) * ROWS:(3 + f) * ROWS] = sums[2 * f + 1] * inv[f]
    coef = jnp.zeros(tile, F32)
    boost = jnp.where(first <= top, 1.0 + MIXED_BOOST, 1.0)
    below = jnp.where(first >= 1, 1.0, 0.0)
    for f in range(2):
        values = (
            down_ref[f, 0] * inv[f],
            inv[f],
            up_ref[f, LEVELS - 1] * inv[f],
            boost * (coup_ref[0] * RATIOS[f] * below),
        )
        for i, value in enumerate(values):
            coef = jnp.where(lane == 4 * f + i, value, coef)
    sums_ref[4 * ROWS:] = coef


def face_spread():
    row = lax.rem(iota((24, LANES), 0), 8)
    lane = iota((24, LANES), 1)
    face = jnp.where(row < 3, row - 1, LANES - 6 + row)
    spread = jnp.where(lane == face, -1.0, 0.0) + jnp.where(lane == face + 1, 1.0, 0.0)
    return jnp.where(row < 6, spread, 0.0).astype(jnp.bfloat16)


def spread_faces(faces):
    return lax.dot_general(
        split3(faces, 0), face_spread(), (((0,), (0,)), ((), ())), preferred_element_type=F32
    )


def edge_kernel(near_ref, far_ref, own_ref, sums_ref, dense_ref, state_ref, faces_ref, strip_ref):
    odd = lax.rem(lax.axis_index("gx"), 2) == 1
    near, far = near_ref[...], far_ref[...]
    left = jnp.where(odd, near, far)
    right = jnp.where(odd, far, near)
    strip_ref[...] = own_ref[...]
    for f in range(2):
        strip_ref[16 * f:16 * f + 3] = left[3 * f:3 * f + 3]
        strip_ref[16 * f + 13:16 * f + 16] = right[3 * f:3 * f + 3]
    for kind in range(2):
        strip_ref[32 + 8 * kind:33 + 8 * kind] = left[6 + kind:7 + kind]
        strip_ref[39 + 8 * kind:40 + 8 * kind] = right[6 + kind:7 + kind]
    faces_ref[...] = jnp.zeros(faces_ref.shape, F32)
    weight = dense_ref[4:5] * (2.0 / 3.0)
    for side in range(2):
        at = 32 + 4 * side
        speed = strip_ref[at:at + 3] + strip_ref[at + 1:at + 4]
        mixing = strip_ref[at + 8:at + 11] + strip_ref[at + 9:at + 12]
        for f in range(2):
            at = 16 * f + 8 * side
            qs = [strip_ref[at + s:at + s + 3] for s in range(6)]
            faces_ref[8 * f + 3 * side:8 * f + 3 * side + 3] = flux(qs, speed, mixing) * weight
    for f in range(2):
        faces = faces_ref[8 * f:8 * f + 8]
        for part in range(2):
            product = faces * dense_ref[2 * f + part:2 * f + part + 1]
            folded = product[:, :LANES]
            for i in range(1, CELLS // LANES):
                folded = folded + product[:, i * LANES:(i + 1) * LANES]
            total = jnp.sum(spread_faces(folded).reshape(LANES // ROWS, ROWS, LANES), axis=0)
            at = (2 * (1 - part) + f) * ROWS
            state_ref[at:at + ROWS] = sums_ref[at:at + ROWS] + total
    state_ref[4 * ROWS:] = sums_ref[4 * ROWS:]


def unpack(state, f):
    yf = state[f * ROWS:(f + 1) * ROWS]
    yl = state[(2 + f) * ROWS:(3 + f) * ROWS]
    coef = state[4 * ROWS:]
    z = [jnp.broadcast_to(coef[:, 4 * f + i:4 * f + i + 1], (ROWS, LANES)) for i in range(4)]
    return (yf, yl, *z)


def join(lower, upper):
    lane = iota((ROWS, LANES), 1)
    firsts, lasts = [], []
    coef = jnp.zeros((ROWS, LANES), F32)
    for f in range(2):
        yf_a, yl_a, z11_a, z12_a, z22_a, a_a = unpack(lower, f)
        yf_b, yl_b, z11_b, z12_b, z22_b, a_b = unpack(upper, f)
        g = a_b / (1.0 + a_b * (z22_a + z11_b))
        flow = g * (yl_a - yf_b)
        firsts.append(yf_a - z12_a * flow)
        lasts.append(yl_b + z12_b * flow)
        values = (z11_a - z12_a * z12_a * g, z12_a * g * z12_b, z22_b - z12_b * z12_b * g, a_a)
        for i, value in enumerate(values):
            coef = jnp.where(lane == 4 * f + i, value, coef)
    return jnp.concatenate(firsts + lasts + [coef], axis=0)


def bit(place):
    return lax.rem(lax.div(lax.axis_index("gz"), 1 << place), 2) == 1


def join_pair(own, other, place):
    high = bit(place)
    return join(jnp.where(high, other, own), jnp.where(high, own, other))


def four_kernel(own_ref, one_ref, two_ref, three_ref, pair_ref, total_ref):
    mine = join_pair(own_ref[...], one_ref[...], 0)
    other = join_pair(two_ref[...], three_ref[...], 0)
    pair_ref[...] = other
    total_ref[...] = join_pair(mine, other, 1)


def two_kernel(place, own_ref, other_ref, total_ref):
    total_ref[...] = join_pair(own_ref[...], other_ref[...], place)


def final_kernel(rhs_ref, up_ref, down_ref, faces_ref, own_ref, p0_ref, p1_ref, p2_ref, p3_ref, w_ref, t_ref, b_ref):
    zero = jnp.zeros((ROWS, LANES), F32)
    partners = [p0_ref[...], p1_ref[...], p2_ref[...], p3_ref[...]]
    own = own_ref[...]
    flows = []
    for f in range(2):
        yf_above, z_above, a_above = zero, zero, zero
        yl_below, z_below = zero, zero
        for place in (3, 2, 1, 0):
            yf, yl, z11, z12, z22, a = unpack(partners[place], f)
            below = bit(place)
            g = a_above / (1.0 + a_above * (z_above + z22))
            flow = g * (yf_above - yl)
            yf_above = jnp.where(below, yf_above, yf + z12 * flow)
            z_above = jnp.where(below, z_above, z11 - z12 * z12 * g)
            a_above = jnp.where(below, a_above, a)
            g = a / (1.0 + a * (z_below + z11))
            flow = g * (yl_below - yf)
            yl_below = jnp.where(below, yl + z12 * flow, yl_below)
            z_below = jnp.where(below, z22 - z12 * z12 * g, z_below)
        yf, yl, z11, z12, z22, a = unpack(own, f)
        p = 1.0 + a * (z_below + z11)
        q = 1.0 + a_above * (z_above + z22)
        s_below = a * (yl_below - yf)
        s_above = a_above * (yf_above - yl)
        scale = z12 / (p * q - a * a_above * z12 * z12)
        flows.append((
            (s_below * q - a * z12 * s_above) * scale,
            (s_above * p - a_above * z12 * s_below) * scale,
            z12,
        ))
    for f in range(2):
        spread = spread_faces(faces_ref[8 * f:8 * f + 8]).reshape(LEVELS, ROWS, LANES)
        b_ref[f] = (rhs_ref[f] + spread) * flows[f][2][None]
    outs = (w_ref, t_ref)

    def upward(k, carry):
        new = []
        for f in range(2):
            s = carry[f] + up_ref[f, k] * b_ref[f, k]
            outs[f][k] = s * down_ref[f, k]
            new.append(s)
        return tuple(new)

    lax.fori_loop(0, LEVELS, upward, (flows[0][0], flows[1][0]))

    def downward(i, carry):
        k = LEVELS - 1 - i
        new = []
        for f in range(2):
            outs[f][k] = outs[f][k] + up_ref[f, k] * carry[f]
            new.append(carry[f] + down_ref[f, k] * b_ref[f, k])
        return tuple(new)

    lax.fori_loop(0, LEVELS, downward, (flows[0][1], flows[1][1]))


def call(kernel, shapes, in_specs, scratch=(), flops=0):
    return pl.pallas_call(
        kernel,
        out_shape=[jax.ShapeDtypeStruct(s, F32) for s in shapes],
        in_specs=in_specs,
        out_specs=[VMEM] * len(shapes),
        scratch_shapes=list(scratch),
        compiler_params=PARAMS,
        cost_estimate=pl.CostEstimate(flops=flops, bytes_accessed=flops // 8, transcendentals=0),
    )


def shards(
    vertical_now, vertical_section, theta_now, theta_section,
    east_wind, north_wind, eddy_viscosity, density, coupling, cloud_top,
):
    strip = (8, CELLS)
    count = 16
    near, far, own = call(pack_kernel, [strip, strip, (48, CELLS)], [VMEM] * 4)(
        vertical_section, theta_section, east_wind, eddy_viscosity
    )
    far = lax.ppermute(
        far, "gx", [(i, (i + 1) % count if i % 2 else (i - 1) % count) for i in range(count)]
    )
    near = lax.ppermute(near, "gx", [(i, i ^ 1) for i in range(count)])
    block = (2, LEVELS, ROWS, LANES)
    rhs, up, down, sums, dense = call(
        main_kernel,
        [block, block, block, (STATE, LANES), strip],
        [VMEM] * 7 + [SMEM, SMEM, VMEM],
        [pltpu.VMEM((LEVELS, ROWS, LANES), F32)],
        flops=16_000_000,
    )(
        vertical_now, vertical_section, theta_now, theta_section,
        east_wind, north_wind, eddy_viscosity, density, coupling, cloud_top,
    )
    state_shape = (STATE, LANES)
    state, faces = call(
        edge_kernel, [state_shape, (16, CELLS)], [VMEM] * 5, [pltpu.VMEM((48, CELLS), F32)]
    )(near, far, own, sums, dense)

    def swap(x, partner):
        return lax.ppermute(x, "gz", [(i, partner(i)) for i in range(count)])

    three, two, one = (swap(state, lambda i, k=k: i ^ k) for k in (3, 2, 1))
    pair, four = call(four_kernel, [state_shape] * 2, [VMEM] * 4)(state, one, two, three)
    four_other = swap(four, lambda i: i ^ 4)
    (eight,) = call(functools.partial(two_kernel, 2), [state_shape], [VMEM] * 2)(four, four_other)
    eight_other = swap(eight, lambda i: (7 - i // 2) * 2 + i % 2)
    part = (LEVELS, ROWS, LANES)
    w_next, t_next = call(
        final_kernel, [part, part], [VMEM] * 9, [pltpu.VMEM(block, F32)]
    )(rhs, up, down, faces, state, one, pair, four_other, eight_other)
    return (w_next, t_next)


def solution(mesh):
    wide = P("gz", None, "gx")
    return jax.shard_map(
        shards,
        mesh=mesh,
        in_specs=(wide,) * 7 + (P("gz"), P("gz"), P(None, "gx")),
        out_specs=(wide, wide),
        check_vma=False,
    )
```

```python
import functools

import jax
import jax.numpy as jnp
from jax import lax
from jax.experimental import pallas as pl
from jax.experimental.pallas import tpu as pltpu
from jax.sharding import PartitionSpec as P

COURANT = 0.25
MIXED_BOOST = 4.0
HEAT_RATIO = 3.0
RATIOS = (1.0, HEAT_RATIO)
LEVELS = 40
ROWS = 16
LANES = 128
CELLS = LEVELS * ROWS
STATE = 5 * ROWS
PARTS = 5
UNROLL = 4
HBM = pl.BlockSpec(memory_space=pltpu.HBM)
VMEM = pl.BlockSpec(memory_space=pltpu.VMEM)
SMEM = pl.BlockSpec(memory_space=pltpu.SMEM)
PARAMS = pltpu.CompilerParams(vmem_limit_bytes=32 * 1024 * 1024)
F32 = jnp.float32


def iota(shape, dim):
    return lax.broadcasted_iota(jnp.int32, shape, dim)


def split3(x, axis):
    high = x.astype(jnp.bfloat16)
    rest = x - high.astype(F32)
    mid = rest.astype(jnp.bfloat16)
    low = (rest - mid.astype(F32)).astype(jnp.bfloat16)
    return jnp.concatenate([high, mid, low], axis=axis)


def flux(qs, speed_sum, mixing_sum):
    qm2, qm1, q0, q1, q2, q3 = qs
    speed = speed_sum * (0.5 * COURANT / 60.0)
    step = q0 - q1
    mean = (qm2 + q3) - 8.0 * (qm1 + q2) + 37.0 * (q0 + q1)
    skew = (qm2 - q3) - 5.0 * (qm1 - q2) + 10.0 * step
    return speed * mean + jnp.abs(speed) * skew + (0.5 * mixing_sum) * step


def strip_selectors():
    rows = [[-1] * 64 for _ in range(4)]
    for field in range(2):
        for cell in range(3):
            rows[field][3 * field + cell] = cell
            rows[field][8 + 3 * field + cell] = LANES - 3 + cell
        for cell in range(5):
            rows[field][16 + 16 * field + 3 + cell] = cell
            rows[field][24 + 16 * field + cell] = LANES - 5 + cell
    for kind in range(2):
        rows[2 + kind][6 + kind] = 0
        rows[2 + kind][14 + kind] = LANES - 1
        for cell in range(3):
            rows[2 + kind][48 + 8 * kind + 1 + cell] = cell
            rows[2 + kind][48 + 8 * kind + 4 + cell] = LANES - 3 + cell
    return rows


def lane_selector(lanes):
    row = iota((len(lanes), LANES), 0)
    lane = iota((len(lanes), LANES), 1)
    hit = jnp.zeros((len(lanes), LANES), jnp.bool_)
    start = 0
    while start < len(lanes):
        if lanes[start] < 0:
            start += 1
            continue
        stop = start + 1
        while stop < len(lanes) and lanes[stop] == lanes[stop - 1] + 1:
            stop += 1
        hit = hit | ((row >= start) & (row < stop) & (lane - row == lanes[start] - start))
        start = stop
    return jnp.where(hit, 1.0, 0.0).astype(jnp.bfloat16)


def pick_lanes(select, x):
    dims = (((1,), (1,)), ((), ()))
    if x.dtype == jnp.bfloat16:
        return lax.dot_general(select, x, dims, preferred_element_type=F32)
    high = x.astype(jnp.bfloat16)
    rest = x - high.astype(F32)
    mid = rest.astype(jnp.bfloat16)
    low = (rest - mid.astype(F32)).astype(jnp.bfloat16)
    parts = [lax.dot_general(select, p, dims, preferred_element_type=F32) for p in (high, mid, low)]
    return parts[0] + (parts[1] + parts[2])


def prep_kernel(
    ws_hbm, ts_hbm, east_hbm, visc_hbm, wn_hbm, tn_hbm, north_hbm, dens_hbm, coup_hbm, top_hbm,
    ws_ref, ts_ref, east_ref, visc_ref, wn_ref, tn_ref, north_ref,
    near_ref, far_ref, own_ref, up_ref, down_ref, rho_ref, dense_ref, coef_ref,
    packed_ref, dens_ref, coup_ref, top_ref, small_sem, big_sem,
):
    small = [
        pltpu.make_async_copy(src, dst, small_sem.at[i])
        for i, (src, dst) in enumerate(
            ((dens_hbm, dens_ref), (coup_hbm, coup_ref), (top_hbm, top_ref))
        )
    ]
    big = []
    for i, (src, dst) in enumerate((
        (ws_hbm, ws_ref), (ts_hbm, ts_ref), (east_hbm, east_ref), (visc_hbm, visc_ref),
        (wn_hbm, wn_ref), (tn_hbm, tn_ref), (north_hbm, north_ref),
    )):
        for part in range(PARTS):
            levels = pl.ds(part * (LEVELS // PARTS), LEVELS // PARTS)
            big.append(pltpu.make_async_copy(
                src.at[levels], dst.at[levels], big_sem.at[i * PARTS + part]
            ))
    for copy in small + big:
        copy.start()
    for copy in small:
        copy.wait()

    first = lax.axis_index("gz") * LEVELS
    tile = (ROWS, LANES)
    lane = iota(tile, 1)
    row = iota(tile, 0)
    one = jnp.ones(tile, F32)
    top = jnp.zeros(tile, jnp.int32)
    for j in range(ROWS):
        top = jnp.where(row == j, top_ref[0, j], top)

    def resist(k):
        boost = jnp.where(first + k <= top, 1.0 / (1.0 + MIXED_BOOST), 1.0)
        return boost / (one * coup_ref[k])

    u = [one, one]
    v = [one, one]
    n = [one * dens_ref[0]] * 2
    m = [one * dens_ref[LEVELS - 1]] * 2
    rho_ref[0] = n[0]
    for f in range(2):
        up_ref[f, 0] = u[f]
        down_ref[f, LEVELS - 1] = v[f]
    for k in range(1, LEVELS):
        j = LEVELS - 1 - k
        res_u = resist(k)
        res_v = resist(j + 1)
        rho_ref[k] = one * dens_ref[k]
        for f in range(2):
            u[f] = u[f] + n[f] * (res_u * (1.0 / RATIOS[f]))
            n[f] = n[f] + dens_ref[k] * u[f]
            up_ref[f, k] = u[f]
            v[f] = v[f] + m[f] * (res_v * (1.0 / RATIOS[f]))
            m[f] = m[f] + dens_ref[j] * v[f]
            down_ref[f, j] = v[f]
    inv = [1.0 / n[f] for f in range(2)]

    for k in range(LEVELS):
        packed = jnp.where(lane < 16, up_ref[0, k] * inv[0], down_ref[0, k] * inv[0])
        packed = jnp.where(lane < 32, packed, up_ref[1, k] * inv[1])
        packed = jnp.where(lane < 48, packed, down_ref[1, k] * inv[1])
        packed_ref[k] = jnp.where(lane < 64, packed, rho_ref[k])
    dense_ref[...] = pick_lanes(
        lane_selector([0, 16, 32, 48, 64, -1, -1, -1]), packed_ref[...].reshape(CELLS, LANES)
    )

    coef = jnp.zeros(tile, F32)
    boost = jnp.where(first <= top, 1.0 + MIXED_BOOST, 1.0)
    below = jnp.where(first >= 1, 1.0, 0.0)
    for f in range(2):
        values = (
            down_ref[f, 0] * inv[f],
            inv[f],
            up_ref[f, LEVELS - 1] * inv[f],
            boost * (coup_ref[0] * RATIOS[f] * below),
        )
        for i, value in enumerate(values):
            coef = jnp.where(lane == 4 * f + i, value, coef)
    coef_ref[...] = coef

    for copy in big[:4 * PARTS]:
        copy.wait()
    odd = lax.rem(lax.axis_index("gx"), 2)
    rows = strip_selectors()
    total = None
    for ref, lanes in zip((ws_ref, ts_ref, east_ref, visc_ref), rows):
        part = pick_lanes(lane_selector(lanes), ref[...].reshape(CELLS, LANES))
        total = part if total is None else total + part
    left, right = total[0:8], total[8:16]
    is_odd = odd == 1
    near_ref[...] = jnp.where(is_odd, left, right)
    far_ref[...] = jnp.where(is_odd, right, left)
    own_ref[...] = total[16:]
    for copy in big[4 * PARTS:]:
        copy.wait()


def main_kernel(
    wn_ref, ws_ref, tn_ref, ts_ref, east_ref, north_ref, visc_ref, rho_ref, up_ref, down_ref, coef_ref,
    rhs_ref, sums_ref,
):
    tile = (ROWS, LANES)
    lane = iota(tile, 1)
    inside = (lane >= 2) & (lane <= LANES - 4)

    def level(k, carry):
        east = east_ref[k].astype(F32)
        north = north_ref[k].astype(F32)
        visc = visc_ref[k].astype(F32)
        east_sum = jnp.where(inside, east + pltpu.roll(east, LANES - 1, 1), 0.0)
        visc_x = jnp.where(inside, visc + pltpu.roll(visc, LANES - 1, 1), 0.0)
        north_sum = north + pltpu.roll(north, ROWS - 1, 0)
        visc_y = visc + pltpu.roll(visc, ROWS - 1, 0)
        weight = rho_ref[k]
        out = []
        for f, (now_ref, sec_ref) in enumerate(((wn_ref, ws_ref), (tn_ref, ts_ref))):
            q = sec_ref[k]
            qx = [q if s == 0 else pltpu.roll(q, (-s) % LANES, 1) for s in range(-2, 4)]
            fx = flux(qx, east_sum, visc_x)
            qy = [q if s == 0 else pltpu.roll(q, (-s) % ROWS, 0) for s in range(-2, 4)]
            fy = flux(qy, north_sum, visc_y)
            change = (pltpu.roll(fx, 1, 1) - fx) + (pltpu.roll(fy, 1, 0) - fy)
            explicit = now_ref[k] * (1.0 / 3.0) + (q + change) * (2.0 / 3.0)
            b = explicit * weight
            rhs_ref[f, k] = b
            out.append(carry[2 * f] + down_ref[f, k] * b)
            out.append(carry[2 * f + 1] + up_ref[f, k] * b)
        return tuple(out)

    def levels(i, carry):
        for step in range(UNROLL):
            carry = level(i * UNROLL + step, carry)
        return carry

    zero = jnp.zeros(tile, F32)
    sums = lax.fori_loop(0, LEVELS // UNROLL, levels, (zero,) * 4)
    coef = coef_ref[...]
    for f in range(2):
        inv = jnp.broadcast_to(coef[:, 4 * f + 1:4 * f + 2], tile)
        sums_ref[f * ROWS:(f + 1) * ROWS] = sums[2 * f] * inv
        sums_ref[(2 + f) * ROWS:(3 + f) * ROWS] = sums[2 * f + 1] * inv
    sums_ref[4 * ROWS:] = coef


def face_spread():
    row = lax.rem(iota((24, LANES), 0), 8)
    lane = iota((24, LANES), 1)
    face = jnp.where(row < 3, row - 1, LANES - 6 + row)
    spread = jnp.where(lane == face, -1.0, 0.0) + jnp.where(lane == face + 1, 1.0, 0.0)
    return jnp.where(row < 6, spread, 0.0).astype(jnp.bfloat16)


def spread_faces(faces):
    return lax.dot_general(
        split3(faces, 0), face_spread(), (((0,), (0,)), ((), ())), preferred_element_type=F32
    )


def edge_kernel(near_ref, far_ref, own_ref, sums_ref, dense_ref, state_ref, faces_ref, strip_ref):
    odd = lax.rem(lax.axis_index("gx"), 2) == 1
    near, far = near_ref[...], far_ref[...]
    left = jnp.where(odd, near, far)
    right = jnp.where(odd, far, near)
    strip_ref[...] = own_ref[...]
    for f in range(2):
        strip_ref[16 * f:16 * f + 3] = left[3 * f:3 * f + 3]
        strip_ref[16 * f + 13:16 * f + 16] = right[3 * f:3 * f + 3]
    for kind in range(2):
        strip_ref[32 + 8 * kind:33 + 8 * kind] = left[6 + kind:7 + kind]
        strip_ref[39 + 8 * kind:40 + 8 * kind] = right[6 + kind:7 + kind]
    faces_ref[...] = jnp.zeros(faces_ref.shape, F32)
    weight = dense_ref[4:5] * (2.0 / 3.0)
    for side in range(2):
        at = 32 + 4 * side
        speed = strip_ref[at:at + 3] + strip_ref[at + 1:at + 4]
        mixing = strip_ref[at + 8:at + 11] + strip_ref[at + 9:at + 12]
        for f in range(2):
            at = 16 * f + 8 * side
            qs = [strip_ref[at + s:at + s + 3] for s in range(6)]
            faces_ref[8 * f + 3 * side:8 * f + 3 * side + 3] = flux(qs, speed, mixing) * weight
    for f in range(2):
        faces = faces_ref[8 * f:8 * f + 8]
        for part in range(2):
            product = faces * dense_ref[2 * f + part:2 * f + part + 1]
            folded = product[:, :LANES]
            for i in range(1, CELLS // LANES):
                folded = folded + product[:, i * LANES:(i + 1) * LANES]
            total = jnp.sum(spread_faces(folded).reshape(LANES // ROWS, ROWS, LANES), axis=0)
            at = (2 * (1 - part) + f) * ROWS
            state_ref[at:at + ROWS] = sums_ref[at:at + ROWS] + total
    state_ref[4 * ROWS:] = sums_ref[4 * ROWS:]


def unpack(state, f):
    yf = state[f * ROWS:(f + 1) * ROWS]
    yl = state[(2 + f) * ROWS:(3 + f) * ROWS]
    coef = state[4 * ROWS:]
    z = [jnp.broadcast_to(coef[:, 4 * f + i:4 * f + i + 1], (ROWS, LANES)) for i in range(4)]
    return (yf, yl, *z)


def join(lower, upper):
    lane = iota((ROWS, LANES), 1)
    firsts, lasts = [], []
    coef = jnp.zeros((ROWS, LANES), F32)
    for f in range(2):
        yf_a, yl_a, z11_a, z12_a, z22_a, a_a = unpack(lower, f)
        yf_b, yl_b, z11_b, z12_b, z22_b, a_b = unpack(upper, f)
        g = a_b / (1.0 + a_b * (z22_a + z11_b))
        flow = g * (yl_a - yf_b)
        firsts.append(yf_a - z12_a * flow)
        lasts.append(yl_b + z12_b * flow)
        values = (z11_a - z12_a * z12_a * g, z12_a * g * z12_b, z22_b - z12_b * z12_b * g, a_a)
        for i, value in enumerate(values):
            coef = jnp.where(lane == 4 * f + i, value, coef)
    return jnp.concatenate(firsts + lasts + [coef], axis=0)


def bit(place):
    return lax.rem(lax.div(lax.axis_index("gz"), 1 << place), 2) == 1


def join_pair(own, other, place):
    high = bit(place)
    return join(jnp.where(high, other, own), jnp.where(high, own, other))


def four_kernel(own_ref, one_ref, two_ref, three_ref, pair_ref, total_ref):
    mine = join_pair(own_ref[...], one_ref[...], 0)
    other = join_pair(two_ref[...], three_ref[...], 0)
    pair_ref[...] = other
    total_ref[...] = join_pair(mine, other, 1)


def two_kernel(place, own_ref, other_ref, total_ref):
    total_ref[...] = join_pair(own_ref[...], other_ref[...], place)


def local_kernel(rhs_ref, up_ref, down_ref, faces_ref, state_ref, y_ref, b_ref):
    zero = jnp.zeros((ROWS, LANES), F32)
    coef = state_ref[4 * ROWS:]
    for f in range(2):
        inv = jnp.broadcast_to(coef[:, 4 * f + 1:4 * f + 2], (ROWS, LANES))
        spread = spread_faces(faces_ref[8 * f:8 * f + 8]).reshape(LEVELS, ROWS, LANES)
        b_ref[f] = (rhs_ref[f] + spread) * inv[None]

    def upward(i, carry):
        carry = list(carry)
        for step in range(UNROLL):
            k = i * UNROLL + step
            for f in range(2):
                carry[f] = carry[f] + up_ref[f, k] * b_ref[f, k]
                y_ref[f, k] = carry[f] * down_ref[f, k]
        return tuple(carry)

    lax.fori_loop(0, LEVELS // UNROLL, upward, (zero, zero))

    def downward(i, carry):
        carry = list(carry)
        for step in range(UNROLL):
            k = LEVELS - 1 - (i * UNROLL + step)
            for f in range(2):
                y_ref[f, k] = y_ref[f, k] + up_ref[f, k] * carry[f]
                carry[f] = carry[f] + down_ref[f, k] * b_ref[f, k]
        return tuple(carry)

    lax.fori_loop(0, LEVELS // UNROLL, downward, (zero, zero))


def final_kernel(y_ref, up_ref, down_ref, own_ref, p0_ref, p1_ref, p2_ref, p3_ref, w_hbm, t_hbm, out_ref, sem):
    zero = jnp.zeros((ROWS, LANES), F32)
    partners = [p0_ref[...], p1_ref[...], p2_ref[...], p3_ref[...]]
    own = own_ref[...]
    flows = []
    for f in range(2):
        yf_above, z_above, a_above = zero, zero, zero
        yl_below, z_below = zero, zero
        for place in (3, 2, 1, 0):
            yf, yl, z11, z12, z22, a = unpack(partners[place], f)
            below = bit(place)
            g = a_above / (1.0 + a_above * (z_above + z22))
            flow = g * (yf_above - yl)
            yf_above = jnp.where(below, yf_above, yf + z12 * flow)
            z_above = jnp.where(below, z_above, z11 - z12 * z12 * g)
            a_above = jnp.where(below, a_above, a)
            g = a / (1.0 + a * (z_below + z11))
            flow = g * (yl_below - yf)
            yl_below = jnp.where(below, yl + z12 * flow, yl_below)
            z_below = jnp.where(below, z22 - z12 * z12 * g, z_below)
        yf, yl, z11, z12, z22, a = unpack(own, f)
        p = 1.0 + a * (z_below + z11)
        q = 1.0 + a_above * (z_above + z22)
        s_below = a * (yl_below - yf)
        s_above = a_above * (yf_above - yl)
        scale = z12 / (p * q - a * a_above * z12 * z12)
        flows.append((
            (s_below * q - a * z12 * s_above) * scale,
            (s_above * p - a_above * z12 * s_below) * scale,
        ))
    chunk = LEVELS // PARTS
    copies = []
    for part in range(PARTS):
        for f, out in enumerate((w_hbm, t_hbm)):
            for k in range(part * chunk, (part + 1) * chunk):
                out_ref[f, k] = y_ref[f, k] + (down_ref[f, k] * flows[f][0] + up_ref[f, k] * flows[f][1])
            levels = pl.ds(part * chunk, chunk)
            copies.append(pltpu.make_async_copy(
                out_ref.at[f, levels], out.at[levels], sem.at[2 * part + f]
            ))
            copies[-1].start()
    for copy in copies:
        copy.wait()


def call(kernel, shapes, in_specs, scratch=(), out_specs=None, flops=0):
    shapes = [s if isinstance(s, jax.ShapeDtypeStruct) else jax.ShapeDtypeStruct(s, F32) for s in shapes]
    return pl.pallas_call(
        kernel,
        out_shape=shapes,
        in_specs=in_specs,
        out_specs=out_specs or [VMEM] * len(shapes),
        scratch_shapes=list(scratch),
        compiler_params=PARAMS,
        cost_estimate=pl.CostEstimate(flops=flops, bytes_accessed=flops // 8, transcendentals=0),
    )


def shards(
    vertical_now, vertical_section, theta_now, theta_section,
    east_wind, north_wind, eddy_viscosity, density, coupling, cloud_top,
):
    strip = (8, CELLS)
    count = 16
    part = (LEVELS, ROWS, LANES)
    block = (2, *part)
    tile = (ROWS, LANES)
    state_shape = (STATE, LANES)
    wide = jax.ShapeDtypeStruct(part, F32)
    half = jax.ShapeDtypeStruct(part, jnp.bfloat16)
    (ws, ts, east, visc, wn, tn, north, near, far, own, up, down, rho, dense, coef) = call(
        prep_kernel,
        [wide, wide, half, half, wide, wide, half, strip, strip, (48, CELLS), block, block, part, strip, tile],
        [HBM] * 10,
        [
            pltpu.VMEM(part, F32),
            pltpu.SMEM((LEVELS,), F32),
            pltpu.SMEM((LEVELS,), F32),
            pltpu.SMEM((1, ROWS), jnp.int32),
            pltpu.SemaphoreType.DMA((3,)),
            pltpu.SemaphoreType.DMA((7 * PARTS,)),
        ],
    )(*(
        pltpu.with_memory_space_constraint(x, pltpu.HBM) for x in (
            vertical_section, theta_section, east_wind, eddy_viscosity,
            vertical_now, theta_now, north_wind,
            density, coupling, cloud_top.reshape(1, ROWS),
        )
    ))
    far = lax.ppermute(
        far, "gx", [(i, (i + 1) % count if i % 2 else (i - 1) % count) for i in range(count)]
    )
    near = lax.ppermute(near, "gx", [(i, i ^ 1) for i in range(count)])
    rhs, sums = call(main_kernel, [block, state_shape], [VMEM] * 11, flops=16_000_000)(
        wn, ws, tn, ts, east, north, visc, rho, up, down, coef
    )
    state, faces = call(
        edge_kernel, [state_shape, (16, CELLS)], [VMEM] * 5, [pltpu.VMEM((48, CELLS), F32)]
    )(near, far, own, sums, dense)

    def swap(x, partner):
        return lax.ppermute(x, "gz", [(i, partner(i)) for i in range(count)])

    three, two, one = (swap(state, lambda i, k=k: i ^ k) for k in (3, 2, 1))
    (y,) = call(
        local_kernel, [block], [VMEM] * 5, [pltpu.VMEM(block, F32)], flops=4_000_000
    )(rhs, up, down, faces, state)
    pair, four = call(four_kernel, [state_shape] * 2, [VMEM] * 4)(state, one, two, three)
    four_other = swap(four, lambda i: i ^ 4)
    (eight,) = call(functools.partial(two_kernel, 2), [state_shape], [VMEM] * 2)(four, four_other)
    eight_other = swap(eight, lambda i: (7 - i // 2) * 2 + i % 2)
    return tuple(call(
        final_kernel,
        [part, part],
        [VMEM] * 8,
        [pltpu.VMEM(block, F32), pltpu.SemaphoreType.DMA((2 * PARTS,))],
        [HBM] * 2,
    )(y, up, down, state, one, pair, four_other, eight_other))


def solution(mesh):
    wide = P("gz", None, "gx")
    return jax.shard_map(
        shards,
        mesh=mesh,
        in_specs=(wide,) * 7 + (P("gz"), P("gz"), P(None, "gx")),
        out_specs=(wide, wide),
        check_vma=False,
    )
```

```python
import jax
import jax.numpy as jnp
from jax import lax
from jax.experimental import pallas as pl
from jax.experimental.pallas import tpu as pltpu
from jax.sharding import PartitionSpec as P

COURANT = 0.25
MIXED_BOOST = 4.0
HEAT_RATIO = 3.0
RATIOS = (1.0, HEAT_RATIO)
LEVELS = 40
ROWS = 16
LANES = 128
CELLS = LEVELS * ROWS
COEF = 8
STATE = 4 * ROWS + COEF
PAD = 8
PARTS = 5
UNROLL = 5
HBM = pl.BlockSpec(memory_space=pltpu.HBM)
VMEM = pl.BlockSpec(memory_space=pltpu.VMEM)
SMEM = pl.BlockSpec(memory_space=pltpu.SMEM)
PARAMS = pltpu.CompilerParams(vmem_limit_bytes=32 * 1024 * 1024)
F32 = jnp.float32


def iota(shape, dim):
    return lax.broadcasted_iota(jnp.int32, shape, dim)


def split3(x, axis):
    high = x.astype(jnp.bfloat16)
    rest = x - high.astype(F32)
    mid = rest.astype(jnp.bfloat16)
    low = (rest - mid.astype(F32)).astype(jnp.bfloat16)
    return jnp.concatenate([high, mid, low], axis=axis)


def flux(qs, speed_sum, mixing_sum):
    qm2, qm1, q0, q1, q2, q3 = qs
    speed = speed_sum * (0.5 * COURANT / 60.0)
    step = q0 - q1
    mean = (qm2 + q3) - 8.0 * (qm1 + q2) + 37.0 * (q0 + q1)
    skew = (qm2 - q3) - 5.0 * (qm1 - q2) + 10.0 * step
    return speed * mean + jnp.abs(speed) * skew + (0.5 * mixing_sum) * step


def strip_selectors():
    rows = [[-1] * 64 for _ in range(4)]
    for field in range(2):
        for cell in range(3):
            rows[field][3 * field + cell] = cell
            rows[field][8 + 3 * field + cell] = LANES - 3 + cell
        for cell in range(5):
            rows[field][16 + 16 * field + 3 + cell] = cell
            rows[field][24 + 16 * field + cell] = LANES - 5 + cell
    for kind in range(2):
        rows[2 + kind][6 + kind] = 0
        rows[2 + kind][14 + kind] = LANES - 1
        for cell in range(3):
            rows[2 + kind][48 + 8 * kind + 1 + cell] = cell
            rows[2 + kind][48 + 8 * kind + 4 + cell] = LANES - 3 + cell
    return rows


def lane_selector(lanes):
    row = iota((len(lanes), LANES), 0)
    lane = iota((len(lanes), LANES), 1)
    hit = jnp.zeros((len(lanes), LANES), jnp.bool_)
    start = 0
    while start < len(lanes):
        if lanes[start] < 0:
            start += 1
            continue
        stop = start + 1
        while stop < len(lanes) and lanes[stop] == lanes[stop - 1] + 1:
            stop += 1
        hit = hit | ((row >= start) & (row < stop) & (lane - row == lanes[start] - start))
        start = stop
    return jnp.where(hit, 1.0, 0.0).astype(jnp.bfloat16)


def pick_lanes(select, x):
    dims = (((1,), (1,)), ((), ()))
    if x.dtype == jnp.bfloat16:
        return lax.dot_general(select, x, dims, preferred_element_type=F32)
    high = x.astype(jnp.bfloat16)
    rest = x - high.astype(F32)
    mid = rest.astype(jnp.bfloat16)
    low = (rest - mid.astype(F32)).astype(jnp.bfloat16)
    parts = [lax.dot_general(select, p, dims, preferred_element_type=F32) for p in (high, mid, low)]
    return parts[0] + (parts[1] + parts[2])


def pack_kernel(
    ws_hbm, ts_hbm, east_hbm, visc_hbm, wn_hbm, tn_hbm, north_hbm, dens_hbm, coup_hbm, top_hbm,
    ws_ref, ts_ref, east_ref, visc_ref, wn_ref, tn_ref, north_ref, far_ref, near_ref, own_ref,
    up_ref, down_ref, rho_ref, inv_ref, coef_ref,
    dens_ref, coup_ref, top_ref, small_sem, sem,
):
    small = [
        pltpu.make_async_copy(src, dst, small_sem.at[i])
        for i, (src, dst) in enumerate(
            ((dens_hbm, dens_ref), (coup_hbm, coup_ref), (top_hbm, top_ref))
        )
    ]
    for copy in small:
        copy.start()
    refs = (ws_ref, ts_ref, east_ref, visc_ref)
    sources = (ws_hbm, ts_hbm, east_hbm, visc_hbm, wn_hbm, tn_hbm, north_hbm)
    targets = (*refs, wn_ref, tn_ref, north_ref)
    pairs = [
        (src, dst.at[:, PAD:PAD + ROWS] if i < 2 else dst) for i, (src, dst) in enumerate(zip(sources, targets))
    ]
    for src, dst in zip(sources[:2], targets):
        pairs.append((src.at[:, ROWS - PAD:], dst.at[:, :PAD]))
        pairs.append((src.at[:, :PAD], dst.at[:, PAD + ROWS:]))
    copies = [pltpu.make_async_copy(src, dst, sem.at[i]) for i, (src, dst) in enumerate(pairs)]
    for copy in copies:
        copy.start()
    selects = [lane_selector(lanes) for lanes in strip_selectors()]
    is_odd = lax.rem(lax.axis_index("gx"), 2) == 1
    for copy in small:
        copy.wait()

    first = lax.axis_index("gz") * LEVELS
    tile = (ROWS, LANES)
    row = iota(tile, 0)
    one = jnp.ones(tile, F32)
    top = jnp.zeros(tile, jnp.int32)
    for j in range(ROWS):
        top = jnp.where(row == j, top_ref[0, j], top)

    def resist(k):
        boost = jnp.where(first + k <= top, 1.0 / (1.0 + MIXED_BOOST), 1.0)
        return boost / (one * coup_ref[k])

    u = [one, one]
    v = [one, one]
    n = [one * dens_ref[0]] * 2
    m = [one * dens_ref[LEVELS - 1]] * 2
    rho_ref[0] = n[0]
    for f in range(2):
        up_ref[f, 0] = u[f]
        down_ref[f, LEVELS - 1] = v[f]
    for k in range(1, LEVELS):
        j = LEVELS - 1 - k
        res_u = resist(k)
        res_v = resist(j + 1)
        rho_ref[k] = one * dens_ref[k]
        for f in range(2):
            u[f] = u[f] + n[f] * (res_u * (1.0 / RATIOS[f]))
            n[f] = n[f] + dens_ref[k] * u[f]
            up_ref[f, k] = u[f]
            v[f] = v[f] + m[f] * (res_v * (1.0 / RATIOS[f]))
            m[f] = m[f] + dens_ref[j] * v[f]
            down_ref[f, j] = v[f]
    inv = [1.0 / n[f] for f in range(2)]

    boost = jnp.where(first <= top, 1.0 + MIXED_BOOST, 1.0)
    below = jnp.where(first >= 1, 1.0, 0.0)
    values = []
    for f in range(2):
        values += [
            down_ref[f, 0] * inv[f],
            inv[f],
            up_ref[f, LEVELS - 1] * inv[f],
            boost * (coup_ref[0] * RATIOS[f] * below),
        ]
    coef_ref[...] = pack_coef(values)
    for f in range(2):
        inv_ref[f] = inv[f]
    for copy in copies[:4]:
        copy.wait()
    left_parts, right_parts = [], []
    for ref, select in zip(refs, selects):
        x = ref[:, PAD:PAD + ROWS] if ref.shape[1] > ROWS else ref[...]
        x = x.reshape(CELLS, LANES)
        parts = [x]
        if x.dtype == F32:
            high = x.astype(jnp.bfloat16)
            rest = x - high.astype(F32)
            mid = rest.astype(jnp.bfloat16)
            parts = [high, mid, (rest - mid.astype(F32)).astype(jnp.bfloat16)]
        left_parts += [select] * len(parts)
        right_parts += parts
    total = lax.dot_general(
        jnp.concatenate(left_parts, axis=1), jnp.concatenate(right_parts, axis=1),
        (((1,), (1,)), ((), ())), preferred_element_type=F32,
    )
    left, right = total[0:8], total[8:16]
    far_ref[...] = jnp.where(is_odd, right, left)
    near_ref[...] = jnp.where(is_odd, left, right)
    own_ref[...] = total[16:]
    for copy in copies[4:]:
        copy.wait()


def main_kernel(
    wn_ref, tn_ref, north_ref, ws_ref, ts_ref, east_ref, visc_ref, up_ref, down_ref, rho_ref, inv_ref, coef_ref,
    rhs_ref, sums_ref, dense_ref, packed_ref,
):
    tile = (ROWS, LANES)
    lane = iota(tile, 1)
    inv = [inv_ref[f] for f in range(2)]

    for k in range(LEVELS):
        packed = jnp.where(lane < 16, up_ref[0, k] * inv[0], down_ref[0, k] * inv[0])
        packed = jnp.where(lane < 32, packed, up_ref[1, k] * inv[1])
        packed = jnp.where(lane < 48, packed, down_ref[1, k] * inv[1])
        packed_ref[k] = jnp.where(lane < 64, packed, rho_ref[k])
    dense_ref[...] = pick_lanes(
        lane_selector([0, 16, 32, 48, 64, -1, -1, -1]), packed_ref[...].reshape(CELLS, LANES)
    )

    inside = (lane >= 2) & (lane <= LANES - 4)

    def level(k, carry):
        east = east_ref[k].astype(F32)
        north = north_ref[k].astype(F32)
        visc = visc_ref[k].astype(F32)
        east_sum = jnp.where(inside, east + pltpu.roll(east, LANES - 1, 1), 0.0)
        visc_x = jnp.where(inside, visc + pltpu.roll(visc, LANES - 1, 1), 0.0)
        north_sum = north + pltpu.roll(north, ROWS - 1, 0)
        visc_y = visc + pltpu.roll(visc, ROWS - 1, 0)
        weight = rho_ref[k]
        out = []
        for f, (now_ref, sec_ref) in enumerate(((wn_ref, ws_ref), (tn_ref, ts_ref))):
            q = sec_ref[k, PAD:PAD + ROWS]
            qx = [q if s == 0 else pltpu.roll(q, (-s) % LANES, 1) for s in range(-2, 4)]
            fx = flux(qx, east_sum, visc_x)
            qy = [q if s == 0 else sec_ref[k, PAD + s:PAD + s + ROWS] for s in range(-2, 4)]
            fy = flux(qy, north_sum, visc_y)
            change = (pltpu.roll(fx, 1, 1) - fx) + (pltpu.roll(fy, 1, 0) - fy)
            explicit = now_ref[k] * (1.0 / 3.0) + (q + change) * (2.0 / 3.0)
            b = explicit * weight
            rhs_ref[f, k] = b
            out.append(carry[2 * f] + down_ref[f, k] * b)
            out.append(carry[2 * f + 1] + up_ref[f, k] * b)
        return tuple(out)

    def levels(i, carry):
        for step in range(UNROLL):
            carry = level(i * UNROLL + step, carry)
        return carry

    zero = jnp.zeros(tile, F32)
    sums = lax.fori_loop(0, LEVELS // UNROLL, levels, (zero,) * 4)
    for f in range(2):
        sums_ref[f * ROWS:(f + 1) * ROWS] = sums[2 * f] * inv[f]
        sums_ref[(2 + f) * ROWS:(3 + f) * ROWS] = sums[2 * f + 1] * inv[f]
    sums_ref[4 * ROWS:] = coef_ref[...]


def face_spread():
    row = lax.rem(iota((24, LANES), 0), 8)
    lane = iota((24, LANES), 1)
    face = jnp.where(row < 3, row - 1, LANES - 6 + row)
    spread = jnp.where(lane == face, -1.0, 0.0) + jnp.where(lane == face + 1, 1.0, 0.0)
    return jnp.where(row < 6, spread, 0.0).astype(jnp.bfloat16)


def spread_faces(faces):
    return lax.dot_general(
        split3(faces, 0), face_spread(), (((0,), (0,)), ((), ())), preferred_element_type=F32
    )


def edge_kernel(far_ref, near_ref, own_ref, sums_ref, dense_ref, state_ref, faces_ref, strip_ref):
    odd = lax.rem(lax.axis_index("gx"), 2) == 1
    near, far = near_ref[...], far_ref[...]
    left = jnp.where(odd, near, far)
    right = jnp.where(odd, far, near)
    strip_ref[...] = own_ref[...]
    for f in range(2):
        strip_ref[16 * f:16 * f + 3] = left[3 * f:3 * f + 3]
        strip_ref[16 * f + 13:16 * f + 16] = right[3 * f:3 * f + 3]
    for kind in range(2):
        strip_ref[32 + 8 * kind:33 + 8 * kind] = left[6 + kind:7 + kind]
        strip_ref[39 + 8 * kind:40 + 8 * kind] = right[6 + kind:7 + kind]
    faces_ref[...] = jnp.zeros(faces_ref.shape, F32)
    weight = dense_ref[4:5] * (2.0 / 3.0)
    for side in range(2):
        at = 32 + 4 * side
        speed = strip_ref[at:at + 3] + strip_ref[at + 1:at + 4]
        mixing = strip_ref[at + 8:at + 11] + strip_ref[at + 9:at + 12]
        for f in range(2):
            at = 16 * f + 8 * side
            qs = [strip_ref[at + s:at + s + 3] for s in range(6)]
            faces_ref[8 * f + 3 * side:8 * f + 3 * side + 3] = flux(qs, speed, mixing) * weight
    for f in range(2):
        faces = faces_ref[8 * f:8 * f + 8]
        for part in range(2):
            product = faces * dense_ref[2 * f + part:2 * f + part + 1]
            folded = product[:, :LANES]
            for i in range(1, CELLS // LANES):
                folded = folded + product[:, i * LANES:(i + 1) * LANES]
            total = jnp.sum(spread_faces(folded).reshape(LANES // ROWS, ROWS, LANES), axis=0)
            at = (2 * (1 - part) + f) * ROWS
            state_ref[at:at + ROWS] = sums_ref[at:at + ROWS] + total
    state_ref[4 * ROWS:] = sums_ref[4 * ROWS:]


def spread_coef(coef, f, i):
    at = 4 * f + i
    return jnp.concatenate([
        jnp.broadcast_to(coef[:, at:at + 1], (COEF, LANES)),
        jnp.broadcast_to(coef[:, at + LANES // 2:at + LANES // 2 + 1], (COEF, LANES)),
    ], axis=0)


def pack_coef(values):
    lane = iota((COEF, LANES), 1)
    coef = jnp.zeros((COEF, LANES), F32)
    for i, value in enumerate(values):
        coef = jnp.where(lane == i, value[:COEF], coef)
        coef = jnp.where(lane == i + LANES // 2, value[COEF:], coef)
    return coef


def unpack(state, f):
    yf = state[f * ROWS:(f + 1) * ROWS]
    yl = state[(2 + f) * ROWS:(3 + f) * ROWS]
    coef = state[4 * ROWS:]
    return (yf, yl, *(spread_coef(coef, f, i) for i in range(4)))


def join(lower, upper):
    firsts, lasts, values = [], [], []
    for f in range(2):
        yf_a, yl_a, z11_a, z12_a, z22_a, a_a = unpack(lower, f)
        yf_b, yl_b, z11_b, z12_b, z22_b, a_b = unpack(upper, f)
        g = a_b / (1.0 + a_b * (z22_a + z11_b))
        flow = g * (yl_a - yf_b)
        firsts.append(yf_a - z12_a * flow)
        lasts.append(yl_b + z12_b * flow)
        values += [z11_a - z12_a * z12_a * g, z12_a * g * z12_b, z22_b - z12_b * z12_b * g, a_a]
    return jnp.concatenate(firsts + lasts + [pack_coef(values)], axis=0)


def bit(place):
    return lax.rem(lax.div(lax.axis_index("gz"), 1 << place), 2) == 1


def join_pair(own, other, place):
    high = bit(place)
    return join(jnp.where(high, other, own), jnp.where(high, own, other))


def four_kernel(own_ref, one_ref, two_ref, three_ref, pair_ref, total_ref):
    mine = join_pair(own_ref[...], one_ref[...], 0)
    other = join_pair(two_ref[...], three_ref[...], 0)
    pair_ref[...] = other
    total_ref[...] = join_pair(mine, other, 1)


def half_kernel(own_ref, other_ref, send_ref):
    total = join_pair(own_ref[...], other_ref[...], 2)
    send_ref[:2 * ROWS] = jnp.where(bit(3), total[:2 * ROWS], total[2 * ROWS:4 * ROWS])
    send_ref[2 * ROWS:] = total[4 * ROWS:]


def local_kernel(rhs_ref, up_ref, down_ref, faces_ref, state_ref, y_ref, b_ref):
    zero = jnp.zeros((ROWS, LANES), F32)
    coef = state_ref[4 * ROWS:]
    for f in range(2):
        inv = spread_coef(coef, f, 1)
        spread = spread_faces(faces_ref[8 * f:8 * f + 8]).reshape(LEVELS, ROWS, LANES)
        b_ref[f] = (rhs_ref[f] + spread) * inv[None]

    def upward(i, carry):
        carry = list(carry)
        for step in range(UNROLL):
            k = i * UNROLL + step
            for f in range(2):
                carry[f] = carry[f] + up_ref[f, k] * b_ref[f, k]
                y_ref[f, k] = carry[f] * down_ref[f, k]
        return tuple(carry)

    lax.fori_loop(0, LEVELS // UNROLL, upward, (zero, zero))

    def downward(i, carry):
        carry = list(carry)
        for step in range(UNROLL):
            k = LEVELS - 1 - (i * UNROLL + step)
            for f in range(2):
                y_ref[f, k] = y_ref[f, k] + up_ref[f, k] * carry[f]
                carry[f] = carry[f] + down_ref[f, k] * b_ref[f, k]
        return tuple(carry)

    lax.fori_loop(0, LEVELS // UNROLL, downward, (zero, zero))


def final_kernel(y_ref, up_ref, down_ref, own_ref, p0_ref, p1_ref, p2_ref, p3_ref, w_hbm, t_hbm, out_ref, sem):
    zero = jnp.zeros((ROWS, LANES), F32)
    partners = [p0_ref[...], p1_ref[...], p2_ref[...]]
    half = p3_ref[...]
    upper = bit(3)
    own = own_ref[...]
    flows = []
    for f in range(2):
        y = half[f * ROWS:(f + 1) * ROWS]
        z11, z22, a = (
            spread_coef(half[2 * ROWS:], f, i) for i in (0, 2, 3)
        )
        yf_above, z_above, a_above = (jnp.where(upper, zero, x) for x in (y, z11, a))
        yl_below, z_below = (jnp.where(upper, x, zero) for x in (y, z22))
        for place in (2, 1, 0):
            yf, yl, z11, z12, z22, a = unpack(partners[place], f)
            below = bit(place)
            g = a_above / (1.0 + a_above * (z_above + z22))
            flow = g * (yf_above - yl)
            yf_above = jnp.where(below, yf_above, yf + z12 * flow)
            z_above = jnp.where(below, z_above, z11 - z12 * z12 * g)
            a_above = jnp.where(below, a_above, a)
            g = a / (1.0 + a * (z_below + z11))
            flow = g * (yl_below - yf)
            yl_below = jnp.where(below, yl + z12 * flow, yl_below)
            z_below = jnp.where(below, z22 - z12 * z12 * g, z_below)
        yf, yl, z11, z12, z22, a = unpack(own, f)
        p = 1.0 + a * (z_below + z11)
        q = 1.0 + a_above * (z_above + z22)
        s_below = a * (yl_below - yf)
        s_above = a_above * (yf_above - yl)
        scale = z12 / (p * q - a * a_above * z12 * z12)
        flows.append((
            (s_below * q - a * z12 * s_above) * scale,
            (s_above * p - a_above * z12 * s_below) * scale,
        ))
    chunk = LEVELS // PARTS
    copies = []
    for part in range(PARTS):
        for f, out in enumerate((w_hbm, t_hbm)):
            for k in range(part * chunk, (part + 1) * chunk):
                out_ref[f, k] = y_ref[f, k] + (down_ref[f, k] * flows[f][0] + up_ref[f, k] * flows[f][1])
            levels = pl.ds(part * chunk, chunk)
            copies.append(pltpu.make_async_copy(
                out_ref.at[f, levels], out.at[levels], sem.at[2 * part + f]
            ))
            copies[-1].start()
    for copy in copies:
        copy.wait()


def call(kernel, shapes, in_specs, scratch=(), out_specs=None, flops=0):
    shapes = [s if isinstance(s, jax.ShapeDtypeStruct) else jax.ShapeDtypeStruct(s, F32) for s in shapes]
    return pl.pallas_call(
        kernel,
        out_shape=shapes,
        in_specs=in_specs,
        out_specs=out_specs or [VMEM] * len(shapes),
        scratch_shapes=list(scratch),
        compiler_params=PARAMS,
        cost_estimate=pl.CostEstimate(flops=flops, bytes_accessed=flops // 8, transcendentals=0),
    )


def shards(
    vertical_now, vertical_section, theta_now, theta_section,
    east_wind, north_wind, eddy_viscosity, density, coupling, cloud_top,
):
    strip = (8, CELLS)
    count = 16
    part = (LEVELS, ROWS, LANES)
    block = (2, *part)
    state_shape = (STATE, LANES)
    wide = jax.ShapeDtypeStruct(part, F32)
    half = jax.ShapeDtypeStruct(part, jnp.bfloat16)
    tall = jax.ShapeDtypeStruct((LEVELS, ROWS + 2 * PAD, LANES), F32)

    def in_hbm(*arrays):
        return [pltpu.with_memory_space_constraint(x, pltpu.HBM) for x in arrays]

    tile = (ROWS, LANES)
    ws, ts, east, visc, wn, tn, north, far, near, own, up, down, rho, inv, coef = call(
        pack_kernel,
        [tall, tall, half, half, wide, wide, half, strip, strip, (48, CELLS), block, block, part, (2, *tile), (COEF, LANES)],
        [HBM] * 10,
        [
            pltpu.SMEM((LEVELS,), F32),
            pltpu.SMEM((LEVELS,), F32),
            pltpu.SMEM((1, ROWS), jnp.int32),
            pltpu.SemaphoreType.DMA((3,)),
            pltpu.SemaphoreType.DMA((11,)),
        ],
    )(*in_hbm(
        vertical_section, theta_section, east_wind, eddy_viscosity, vertical_now, theta_now, north_wind,
        density, coupling, cloud_top.reshape(1, ROWS),
    ))
    far = lax.ppermute(
        far, "gx", [(i, (i + 1) % count if i % 2 else (i - 1) % count) for i in range(count)]
    )
    near = lax.ppermute(near, "gx", [(i, i ^ 1) for i in range(count)])
    rhs, sums, dense = call(
        main_kernel,
        [block, state_shape, strip],
        [VMEM] * 12,
        [
            pltpu.VMEM(part, F32),
        ],
        flops=16_000_000,
    )(
        wn, tn, north, ws, ts, east, visc, up, down, rho, inv, coef,
    )
    state, faces = call(
        edge_kernel, [state_shape, (16, CELLS)], [VMEM] * 5, [pltpu.VMEM((48, CELLS), F32)]
    )(far, near, own, sums, dense)

    def swap(x, partner):
        return lax.ppermute(x, "gz", [(i, partner(i)) for i in range(count)])

    three, two, one = (swap(state, lambda i, k=k: i ^ k) for k in (3, 2, 1))
    (y,) = call(
        local_kernel, [block], [VMEM] * 5, [pltpu.VMEM(block, F32)], flops=4_000_000
    )(rhs, up, down, faces, state)
    pair, four = call(four_kernel, [state_shape] * 2, [VMEM] * 4)(state, one, two, three)
    four_other = swap(four, lambda i: i ^ 4)
    (eight,) = call(half_kernel, [(2 * ROWS + COEF, LANES)], [VMEM] * 2)(four, four_other)
    eight_other = swap(eight, lambda i: (i + 4 if i & 4 else i - 4) % count)
    return tuple(call(
        final_kernel,
        [part, part],
        [VMEM] * 8,
        [pltpu.VMEM(block, F32), pltpu.SemaphoreType.DMA((2 * PARTS,))],
        [HBM] * 2,
    )(y, up, down, state, one, pair, four_other, eight_other))


def solution(mesh):
    wide = P("gz", None, "gx")
    return jax.shard_map(
        shards,
        mesh=mesh,
        in_specs=(wide,) * 7 + (P("gz"), P("gz"), P(None, "gx")),
        out_specs=(wide, wide),
        check_vma=False,
    )
```

```python
import jax
import jax.numpy as jnp
from jax import lax
from jax.experimental import pallas as pl
from jax.experimental.pallas import tpu as pltpu
from jax.sharding import PartitionSpec as P

COURANT = 0.25
MIXED_BOOST = 4.0
HEAT_RATIO = 3.0
RATIOS = (1.0, HEAT_RATIO)
LEVELS = 40
ROWS = 16
LANES = 128
CELLS = LEVELS * ROWS
COEF = 8
STATE = 4 * ROWS + COEF
PAD = 8
FAR_GROUP = (5, 4, 7, 6, 1, 0, 3, 2)
PARTS = 2
UNROLL = 8
HBM = pl.BlockSpec(memory_space=pltpu.HBM)
VMEM = pl.BlockSpec(memory_space=pltpu.VMEM)
SMEM = pl.BlockSpec(memory_space=pltpu.SMEM)
PARAMS = pltpu.CompilerParams(vmem_limit_bytes=32 * 1024 * 1024)
F32 = jnp.float32


def iota(shape, dim):
    return lax.broadcasted_iota(jnp.int32, shape, dim)


def split3(x, axis):
    high = x.astype(jnp.bfloat16)
    rest = x - high.astype(F32)
    mid = rest.astype(jnp.bfloat16)
    low = (rest - mid.astype(F32)).astype(jnp.bfloat16)
    return jnp.concatenate([high, mid, low], axis=axis)


MEAN = (1.0, -8.0, 37.0, 37.0, -8.0, 1.0)
SKEW = (1.0, -5.0, 10.0, -10.0, 5.0, -1.0)
STEP = (0.0, 0.0, 1.0, -1.0, 0.0, 0.0)


def face_flux(mean, skew, step, speed_sum, mixing_sum):
    speed = speed_sum * (0.5 * COURANT / 60.0)
    return speed * mean + jnp.abs(speed) * skew + (0.5 * mixing_sum) * step


def flux(qs, speed_sum, mixing_sum):
    qm2, qm1, q0, q1, q2, q3 = qs
    step = q0 - q1
    mean = (qm2 + q3) - 8.0 * (qm1 + q2) + 37.0 * (q0 + q1)
    skew = (qm2 - q3) - 5.0 * (qm1 - q2) + 10.0 * step
    return face_flux(mean, skew, step, speed_sum, mixing_sum)


def stencil(coefs, first):
    offset = iota((LANES, LANES), 0) - iota((LANES, LANES), 1) - first
    out = jnp.zeros((LANES, LANES), F32)
    for s, coef in enumerate(coefs):
        if coef:
            out = jnp.where(offset == s, coef, out)
    return out


def dot(x, y):
    return lax.dot_general(x, y, (((1,), (0,)), ((), ())), preferred_element_type=F32)


def strip_selectors():
    rows = [[-1] * 64 for _ in range(4)]
    for field in range(2):
        for cell in range(3):
            rows[field][3 * field + cell] = cell
            rows[field][8 + 3 * field + cell] = LANES - 3 + cell
        for cell in range(5):
            rows[field][16 + 16 * field + 3 + cell] = cell
            rows[field][24 + 16 * field + cell] = LANES - 5 + cell
    for kind in range(2):
        rows[2 + kind][6 + kind] = 0
        rows[2 + kind][14 + kind] = LANES - 1
        for cell in range(3):
            rows[2 + kind][48 + 8 * kind + 1 + cell] = cell
            rows[2 + kind][48 + 8 * kind + 4 + cell] = LANES - 3 + cell
    return rows


def lane_selector(lanes):
    row = iota((len(lanes), LANES), 0)
    lane = iota((len(lanes), LANES), 1)
    hit = jnp.zeros((len(lanes), LANES), jnp.bool_)
    start = 0
    while start < len(lanes):
        if lanes[start] < 0:
            start += 1
            continue
        stop = start + 1
        while stop < len(lanes) and lanes[stop] == lanes[stop - 1] + 1:
            stop += 1
        hit = hit | ((row >= start) & (row < stop) & (lane - row == lanes[start] - start))
        start = stop
    return jnp.where(hit, 1.0, 0.0).astype(jnp.bfloat16)


def pick_lanes(select, x):
    dims = (((1,), (1,)), ((), ()))
    if x.dtype == jnp.bfloat16:
        return lax.dot_general(select, x, dims, preferred_element_type=F32)
    high = x.astype(jnp.bfloat16)
    rest = x - high.astype(F32)
    mid = rest.astype(jnp.bfloat16)
    low = (rest - mid.astype(F32)).astype(jnp.bfloat16)
    parts = [lax.dot_general(select, p, dims, preferred_element_type=F32) for p in (high, mid, low)]
    return parts[0] + (parts[1] + parts[2])


def pack_kernel(
    ws_hbm, ts_hbm, east_hbm, visc_hbm, wn_hbm, tn_hbm, north_hbm, dens_hbm, coup_hbm, top_hbm,
    ws_ref, ts_ref, east_ref, visc_ref, wn_ref, tn_ref, north_ref, parts_ref, far_ref, near_ref, own_ref,
    up_ref, down_ref, rho_ref, inv_ref, coef_ref,
    dens_ref, coup_ref, top_ref, small_sem, sem,
):
    small = [
        pltpu.make_async_copy(src, dst, small_sem.at[i])
        for i, (src, dst) in enumerate(
            ((dens_hbm, dens_ref), (coup_hbm, coup_ref), (top_hbm, top_ref))
        )
    ]
    for copy in small:
        copy.start()
    refs = (ws_ref, ts_ref, east_ref, visc_ref)
    sources = (ws_hbm, ts_hbm, east_hbm, visc_hbm, wn_hbm, tn_hbm, north_hbm)
    targets = (*refs, wn_ref, tn_ref, north_ref)
    pairs = [
        (src, dst.at[:, PAD:PAD + ROWS] if i < 2 else dst) for i, (src, dst) in enumerate(zip(sources, targets))
    ]
    for src, dst in zip(sources[:2], targets):
        pairs.append((src.at[:, ROWS - PAD:], dst.at[:, :PAD]))
        pairs.append((src.at[:, :PAD], dst.at[:, PAD + ROWS:]))
    copies = [pltpu.make_async_copy(src, dst, sem.at[i]) for i, (src, dst) in enumerate(pairs)]
    for copy in copies:
        copy.start()
    selects = [lane_selector(lanes) for lanes in strip_selectors()]
    is_odd = lax.rem(lax.axis_index("gx"), 2) == 1
    for copy in small:
        copy.wait()

    first = lax.axis_index("gz") * LEVELS
    tile = (ROWS, LANES)
    row = iota(tile, 0)
    one = jnp.ones(tile, F32)
    top = jnp.zeros(tile, jnp.int32)
    for j in range(ROWS):
        top = jnp.where(row == j, top_ref[0, j], top)

    def resist(k):
        boost = jnp.where(first + k <= top, 1.0 / (1.0 + MIXED_BOOST), 1.0)
        return boost / (one * coup_ref[k])

    u = [one, one]
    v = [one, one]
    n = [one * dens_ref[0]] * 2
    m = [one * dens_ref[LEVELS - 1]] * 2
    rho_ref[0] = n[0]
    for f in range(2):
        up_ref[f, 0] = u[f]
        down_ref[f, LEVELS - 1] = v[f]
    for k in range(1, LEVELS):
        j = LEVELS - 1 - k
        res_u = resist(k)
        res_v = resist(j + 1)
        rho_ref[k] = one * dens_ref[k]
        for f in range(2):
            u[f] = u[f] + n[f] * (res_u * (1.0 / RATIOS[f]))
            n[f] = n[f] + dens_ref[k] * u[f]
            up_ref[f, k] = u[f]
            v[f] = v[f] + m[f] * (res_v * (1.0 / RATIOS[f]))
            m[f] = m[f] + dens_ref[j] * v[f]
            down_ref[f, j] = v[f]
    inv = [1.0 / n[f] for f in range(2)]

    boost = jnp.where(first <= top, 1.0 + MIXED_BOOST, 1.0)
    below = jnp.where(first >= 1, 1.0, 0.0)
    values = []
    for f in range(2):
        values += [
            down_ref[f, 0] * inv[f],
            inv[f],
            up_ref[f, LEVELS - 1] * inv[f],
            boost * (coup_ref[0] * RATIOS[f] * below),
        ]
    coef_ref[...] = pack_coef(values)
    for f in range(2):
        inv_ref[f] = inv[f]
    for copy in copies[:4]:
        copy.wait()
    left_parts, right_parts = [], []
    for index, (ref, select) in enumerate(zip(refs, selects)):
        x = ref[:, PAD:PAD + ROWS] if ref.shape[1] > ROWS else ref[...]
        x = x.reshape(CELLS, LANES)
        parts = [x]
        if x.dtype == F32:
            high = x.astype(jnp.bfloat16)
            rest = x - high.astype(F32)
            mid = rest.astype(jnp.bfloat16)
            parts = [high, mid, (rest - mid.astype(F32)).astype(jnp.bfloat16)]
            for j, value in enumerate(parts):
                parts_ref[index, :, j * LANES:(j + 1) * LANES] = value
        left_parts += [select] * len(parts)
        right_parts += parts
    total = lax.dot_general(
        jnp.concatenate(left_parts, axis=1), jnp.concatenate(right_parts, axis=1),
        (((1,), (1,)), ((), ())), preferred_element_type=F32,
    )
    left, right = total[0:8], total[8:16]
    far_ref[...] = jnp.where(is_odd, right, left)
    near_ref[...] = jnp.where(is_odd, left, right)
    own_ref[...] = total[16:]
    for copy in copies[4:]:
        copy.wait()


def main_kernel(
    wn_ref, tn_ref, north_ref, ws_ref, ts_ref, east_ref, visc_ref, parts_ref,
    up_ref, down_ref, rho_ref, inv_ref, coef_ref,
    rhs_ref, sums_ref, dense_ref, packed_ref, face_ref, stencil_ref,
):
    tile = (ROWS, LANES)
    lane = iota(tile, 1)
    inv = [inv_ref[f] for f in range(2)]

    for k in range(LEVELS):
        packed = jnp.where(lane < 16, up_ref[0, k] * inv[0], down_ref[0, k] * inv[0])
        packed = jnp.where(lane < 32, packed, up_ref[1, k] * inv[1])
        packed = jnp.where(lane < 48, packed, down_ref[1, k] * inv[1])
        packed_ref[k] = jnp.where(lane < 64, packed, rho_ref[k])
    dense_ref[...] = pick_lanes(
        lane_selector([0, 16, 32, 48, 64, -1, -1, -1]), packed_ref[...].reshape(CELLS, LANES)
    )

    column = iota((LANES, LANES), 1)
    pair = jnp.where((column >= 2) & (column <= LANES - 4), stencil((1.0, 1.0), 0), 0.0).astype(jnp.bfloat16)
    row, column = iota((LANES, LANES), 0), iota((LANES, LANES), 1)
    near = (row == column) | ((row // ROWS == column // ROWS) & (lax.rem(row + 1, ROWS) == lax.rem(column, ROWS)))
    pair_y = jnp.where(near, 1.0, 0.0).astype(jnp.bfloat16)
    chunk = LANES // ROWS
    face_ref[0] = dot(east_ref[...].reshape(CELLS, LANES), pair).reshape(LEVELS, ROWS, LANES)
    face_ref[1] = dot(visc_ref[...].reshape(CELLS, LANES), pair).reshape(LEVELS, ROWS, LANES)
    for i, ref in enumerate((north_ref, visc_ref)):
        for k in range(0, LEVELS, chunk):
            x = ref[k:k + chunk].reshape(LANES, LANES)
            face_ref[2 + i, k:k + chunk] = dot(pair_y, x).reshape(chunk, ROWS, LANES)
    weights = jnp.concatenate([stencil(c, -2) for c in (MEAN, SKEW, STEP)], axis=1).astype(jnp.bfloat16)
    weights = jnp.concatenate([weights] * 3, axis=0)
    for f in range(2):
        product = dot(parts_ref[f], weights)
        for j in range(3):
            stencil_ref[f, j] = product[:, j * LANES:(j + 1) * LANES].reshape(LEVELS, ROWS, LANES)

    def level(k, carry):
        weight = rho_ref[k]
        out = []
        for f, (now_ref, sec_ref) in enumerate(((wn_ref, ws_ref), (tn_ref, ts_ref))):
            fx = face_flux(*(stencil_ref[f, j, k] for j in range(3)), face_ref[0, k], face_ref[1, k])
            qy = [sec_ref[k, PAD + s:PAD + s + ROWS] for s in range(-2, 4)]
            fy = flux(qy, face_ref[2, k], face_ref[3, k])
            change = (pltpu.roll(fx, 1, 1) - fx) + (pltpu.roll(fy, 1, 0) - fy)
            explicit = now_ref[k] * (1.0 / 3.0) + (qy[2] + change) * (2.0 / 3.0)
            b = explicit * weight
            rhs_ref[f, k] = b
            out.append(carry[2 * f] + down_ref[f, k] * b)
            out.append(carry[2 * f + 1] + up_ref[f, k] * b)
        return tuple(out)

    def levels(i, carry):
        for step in range(UNROLL):
            carry = level(i * UNROLL + step, carry)
        return carry

    zero = jnp.zeros(tile, F32)
    sums = lax.fori_loop(0, LEVELS // UNROLL, levels, (zero,) * 4)
    for f in range(2):
        sums_ref[f * ROWS:(f + 1) * ROWS] = sums[2 * f] * inv[f]
        sums_ref[(2 + f) * ROWS:(3 + f) * ROWS] = sums[2 * f + 1] * inv[f]
    sums_ref[4 * ROWS:] = coef_ref[...]


def face_spread():
    row = lax.rem(iota((24, LANES), 0), 8)
    lane = iota((24, LANES), 1)
    face = jnp.where(row < 3, row - 1, LANES - 6 + row)
    spread = jnp.where(lane == face, -1.0, 0.0) + jnp.where(lane == face + 1, 1.0, 0.0)
    return jnp.where(row < 6, spread, 0.0).astype(jnp.bfloat16)


def spread_faces(faces):
    return lax.dot_general(
        split3(faces, 0), face_spread(), (((0,), (0,)), ((), ())), preferred_element_type=F32
    )


def edge_kernel(far_ref, near_ref, own_ref, sums_ref, dense_ref, state_ref, faces_ref, strip_ref):
    odd = lax.rem(lax.axis_index("gx"), 2) == 1
    near, far = near_ref[...], far_ref[...]
    left = jnp.where(odd, near, far)
    right = jnp.where(odd, far, near)
    strip_ref[...] = own_ref[...]
    for f in range(2):
        strip_ref[16 * f:16 * f + 3] = left[3 * f:3 * f + 3]
        strip_ref[16 * f + 13:16 * f + 16] = right[3 * f:3 * f + 3]
    for kind in range(2):
        strip_ref[32 + 8 * kind:33 + 8 * kind] = left[6 + kind:7 + kind]
        strip_ref[39 + 8 * kind:40 + 8 * kind] = right[6 + kind:7 + kind]
    faces_ref[...] = jnp.zeros(faces_ref.shape, F32)
    weight = dense_ref[4:5] * (2.0 / 3.0)
    for side in range(2):
        at = 32 + 4 * side
        speed = strip_ref[at:at + 3] + strip_ref[at + 1:at + 4]
        mixing = strip_ref[at + 8:at + 11] + strip_ref[at + 9:at + 12]
        for f in range(2):
            at = 16 * f + 8 * side
            qs = [strip_ref[at + s:at + s + 3] for s in range(6)]
            faces_ref[8 * f + 3 * side:8 * f + 3 * side + 3] = flux(qs, speed, mixing) * weight
    folds = []
    for part in range(2):
        for f in range(2):
            product = faces_ref[8 * f:8 * f + 8] * dense_ref[2 * f + 1 - part:2 * f + 2 - part]
            folded = product[:, :LANES]
            for i in range(1, CELLS // LANES):
                folded = folded + product[:, i * LANES:(i + 1) * LANES]
            folds.append(folded)
    total = spread_faces(jnp.concatenate(folds, axis=1)).reshape(4, LANES // ROWS, ROWS, LANES)
    state_ref[:4 * ROWS] = sums_ref[:4 * ROWS] + jnp.sum(total, axis=1).reshape(4 * ROWS, LANES)
    state_ref[4 * ROWS:] = sums_ref[4 * ROWS:]


def spread_coef(coef, f, i):
    at = 4 * f + i
    return jnp.concatenate([
        jnp.broadcast_to(coef[:, at:at + 1], (COEF, LANES)),
        jnp.broadcast_to(coef[:, at + LANES // 2:at + LANES // 2 + 1], (COEF, LANES)),
    ], axis=0)


def pack_coef(values):
    lane = iota((COEF, LANES), 1)
    coef = jnp.zeros((COEF, LANES), F32)
    for i, value in enumerate(values):
        coef = jnp.where(lane == i, value[:COEF], coef)
        coef = jnp.where(lane == i + LANES // 2, value[COEF:], coef)
    return coef


def unpack(state, f):
    yf = state[f * ROWS:(f + 1) * ROWS]
    yl = state[(2 + f) * ROWS:(3 + f) * ROWS]
    coef = state[4 * ROWS:]
    return (yf, yl, *(spread_coef(coef, f, i) for i in range(4)))


def join(lower, upper):
    yf_a, yl_a, z11_a, z12_a, z22_a, a_a = lower
    yf_b, yl_b, z11_b, z12_b, z22_b, a_b = upper
    g = a_b / (1.0 + a_b * (z22_a + z11_b))
    flow = g * (yl_a - yf_b)
    step_a, step_b = z12_a * g, z12_b * g
    return (
        yf_a - z12_a * flow, yl_b + z12_b * flow,
        z11_a - z12_a * step_a, z12_a * step_b, z22_b - z12_b * step_b, a_a,
    )


def bit(place):
    return lax.rem(lax.div(lax.axis_index("gz"), 1 << place), 2) == 1


def join_pair(own, other, place):
    high = bit(place)
    lower = tuple(jnp.where(high, y, x) for x, y in zip(own, other))
    upper = tuple(jnp.where(high, x, y) for x, y in zip(own, other))
    return join(lower, upper)


def store(state_ref, blocks):
    values = []
    for f, (yf, yl, *coefs) in enumerate(blocks):
        state_ref[f * ROWS:(f + 1) * ROWS] = yf
        state_ref[(2 + f) * ROWS:(3 + f) * ROWS] = yl
        values += coefs
    state_ref[4 * ROWS:] = pack_coef(values)


def four_kernel(own_ref, one_ref, two_ref, three_ref, pair_ref, total_ref):
    pairs, totals = [], []
    for f in range(2):
        own, one, two, three = (unpack(ref[...], f) for ref in (own_ref, one_ref, two_ref, three_ref))
        pairs.append(join_pair(two, three, 0))
        totals.append(join_pair(join_pair(own, one, 0), pairs[f], 1))
    store(total_ref, totals)
    store(pair_ref, pairs)


def local_kernel(
    rhs_ref, up_ref, down_ref, faces_ref, state_ref, one_ref, pair_ref, y_ref, above_ref, below_ref, b_ref
):
    aboves, belows = [], []
    for f in range(2):
        one, pair = unpack(one_ref[...], f), unpack(pair_ref[...], f)
        near, outer = bit(0), bit(1)
        both = join(one, pair)
        aboves.append(tuple(
            jnp.where(near, y, jnp.where(outer, x, z)) for x, y, z in zip(one, pair, both)
        ))
        both = join(pair, one)
        belows.append(tuple(
            jnp.where(near, jnp.where(outer, z, x), y) for x, y, z in zip(one, pair, both)
        ))
    store(above_ref, aboves)
    store(below_ref, belows)
    zero = jnp.zeros((ROWS, LANES), F32)
    coef = state_ref[4 * ROWS:]
    for f in range(2):
        inv = spread_coef(coef, f, 1)
        spread = spread_faces(faces_ref[8 * f:8 * f + 8]).reshape(LEVELS, ROWS, LANES)
        b_ref[f] = (rhs_ref[f] + spread) * inv[None]

    def upward(i, carry):
        carry = list(carry)
        for step in range(UNROLL):
            k = i * UNROLL + step
            for f in range(2):
                carry[f] = carry[f] + up_ref[f, k] * b_ref[f, k]
                y_ref[f, k] = carry[f] * down_ref[f, k]
        return tuple(carry)

    lax.fori_loop(0, LEVELS // UNROLL, upward, (zero, zero))

    def downward(i, carry):
        carry = list(carry)
        for step in range(UNROLL):
            k = LEVELS - 1 - (i * UNROLL + step)
            for f in range(2):
                y_ref[f, k] = y_ref[f, k] + up_ref[f, k] * carry[f]
                carry[f] = carry[f] + down_ref[f, k] * b_ref[f, k]
        return tuple(carry)

    lax.fori_loop(0, LEVELS // UNROLL, downward, (zero, zero))


def above(chain, block, here):
    y, z, a = chain
    yf, yl, z11, z12, z22, a_block = block
    g = a / (1.0 + a * (z + z22))
    new = (yf + z12 * (g * (y - yl)), z11 - z12 * z12 * g, a_block)
    return tuple(jnp.where(here, x, old) for x, old in zip(new, chain))


def below(chain, block, here):
    y, z = chain
    yf, yl, z11, z12, z22, a = block
    g = a / (1.0 + a * (z + z11))
    new = (yl + z12 * (g * (y - yf)), z22 - z12 * z12 * g)
    return tuple(jnp.where(here, x, old) for x, old in zip(new, chain))


def final_kernel(
    y_ref, up_ref, down_ref, own_ref, above_ref, below_ref, a_ref, b_ref, c_ref, w_hbm, t_hbm, out_ref, sem
):
    zero = jnp.zeros((ROWS, LANES), F32)
    own = own_ref[...]
    group = lax.div(lax.axis_index("gz"), 4)
    place = lax.rem(lax.axis_index("gz"), 4)
    others = (a_ref[...], c_ref[...], b_ref[...])
    groups = []
    for j in range(4):
        slot = lax.rem(group, 2) * (1 - 2 * (j % 2)) + j % 2
        slot = slot + 2 * (lax.div(group, 2) * (1 - 2 * (j // 2)) + j // 2)
        groups.append(jnp.where(slot == 1, others[0], jnp.where(slot == 2, others[1], others[2])))
    flows = []
    for f in range(2):
        blocks = [unpack(g, f) for g in groups]
        inner_above, inner_below = unpack(above_ref[...], f), unpack(below_ref[...], f)
        upper, lower = (zero, zero, zero), (zero, zero)
        for j in (3, 2, 1):
            upper = above(upper, blocks[j], j > group)
        for j in (0, 1, 2):
            lower = below(lower, blocks[j], j < group)
        upper = above(upper, inner_above, place < 3)
        lower = below(lower, inner_below, place > 0)
        yf_above, z_above, a_above = upper
        yl_below, z_below = lower
        yf, yl, z11, z12, z22, a = unpack(own, f)
        p = 1.0 + a * (z_below + z11)
        q = 1.0 + a_above * (z_above + z22)
        s_below = a * (yl_below - yf)
        s_above = a_above * (yf_above - yl)
        scale = z12 / (p * q - a * a_above * z12 * z12)
        flows.append((
            (s_below * q - a * z12 * s_above) * scale,
            (s_above * p - a_above * z12 * s_below) * scale,
        ))
    chunk = LEVELS // PARTS
    copies = []
    for part in range(PARTS):
        for f, out in enumerate((w_hbm, t_hbm)):
            for k in range(part * chunk, (part + 1) * chunk):
                out_ref[f, k] = y_ref[f, k] + (down_ref[f, k] * flows[f][0] + up_ref[f, k] * flows[f][1])
            levels = pl.ds(part * chunk, chunk)
            copies.append(pltpu.make_async_copy(
                out_ref.at[f, levels], out.at[levels], sem.at[2 * part + f]
            ))
            copies[-1].start()
    for copy in copies:
        copy.wait()


def call(kernel, shapes, in_specs, scratch=(), out_specs=None, flops=0):
    shapes = [s if isinstance(s, jax.ShapeDtypeStruct) else jax.ShapeDtypeStruct(s, F32) for s in shapes]
    return pl.pallas_call(
        kernel,
        out_shape=shapes,
        in_specs=in_specs,
        out_specs=out_specs or [VMEM] * len(shapes),
        scratch_shapes=list(scratch),
        compiler_params=PARAMS,
        cost_estimate=pl.CostEstimate(flops=flops, bytes_accessed=flops // 8, transcendentals=0),
    )


def shards(
    vertical_now, vertical_section, theta_now, theta_section,
    east_wind, north_wind, eddy_viscosity, density, coupling, cloud_top,
):
    strip = (8, CELLS)
    count = 16
    part = (LEVELS, ROWS, LANES)
    block = (2, *part)
    state_shape = (STATE, LANES)
    wide = jax.ShapeDtypeStruct(part, F32)
    half = jax.ShapeDtypeStruct(part, jnp.bfloat16)
    split = jax.ShapeDtypeStruct((2, CELLS, 3 * LANES), jnp.bfloat16)
    tall = jax.ShapeDtypeStruct((LEVELS, ROWS + 2 * PAD, LANES), F32)

    def in_hbm(*arrays):
        return [pltpu.with_memory_space_constraint(x, pltpu.HBM) for x in arrays]

    tile = (ROWS, LANES)
    ws, ts, east, visc, wn, tn, north, parts, far, near, own, up, down, rho, inv, coef = call(
        pack_kernel,
        [tall, tall, half, half, wide, wide, half, split, strip, strip, (48, CELLS), block, block, part, (2, *tile), (COEF, LANES)],
        [HBM] * 10,
        [
            pltpu.SMEM((LEVELS,), F32),
            pltpu.SMEM((LEVELS,), F32),
            pltpu.SMEM((1, ROWS), jnp.int32),
            pltpu.SemaphoreType.DMA((3,)),
            pltpu.SemaphoreType.DMA((11,)),
        ],
    )(*in_hbm(
        vertical_section, theta_section, east_wind, eddy_viscosity, vertical_now, theta_now, north_wind,
        density, coupling, cloud_top.reshape(1, ROWS),
    ))
    far = lax.ppermute(
        far, "gx", [(i, (i + 1) % count if i % 2 else (i - 1) % count) for i in range(count)]
    )
    near = lax.ppermute(near, "gx", [(i, i ^ 1) for i in range(count)])
    rhs, sums, dense = call(
        main_kernel,
        [block, state_shape, strip],
        [VMEM] * 13,
        [pltpu.VMEM(part, F32), pltpu.VMEM((4, *part), F32), pltpu.VMEM((2, 3, *part), F32)],
        flops=16_000_000,
    )(
        wn, tn, north, ws, ts, east, visc, parts, up, down, rho, inv, coef,
    )
    state, faces = call(
        edge_kernel, [state_shape, (16, CELLS)], [VMEM] * 5, [pltpu.VMEM((48, CELLS), F32)]
    )(far, near, own, sums, dense)

    def swap(x, partner):
        return lax.ppermute(x, "gz", [(i, partner(i)) for i in range(count)])

    three, two, one = (swap(state, lambda i, k=k: i ^ k) for k in (3, 2, 1))
    pair, four = call(four_kernel, [state_shape] * 2, [VMEM] * 4)(state, one, two, three)
    y, inner_above, inner_below = call(
        local_kernel, [block, state_shape, state_shape], [VMEM] * 7, [pltpu.VMEM(block, F32)], flops=4_000_000
    )(rhs, up, down, faces, state, one, pair)
    side_a = swap(four, lambda i: i ^ 4)
    side_b = swap(four, lambda i: (i + 4 if i & 4 else i - 4) % count)
    side_c = swap(four, lambda i: FAR_GROUP[i // 2] * 2 + i % 2)
    return tuple(call(
        final_kernel,
        [part, part],
        [VMEM] * 9,
        [pltpu.VMEM(block, F32), pltpu.SemaphoreType.DMA((2 * PARTS,))],
        [HBM] * 2,
    )(y, up, down, state, inner_above, inner_below, side_a, side_b, side_c))


def solution(mesh):
    wide = P("gz", None, "gx")
    return jax.shard_map(
        shards,
        mesh=mesh,
        in_specs=(wide,) * 7 + (P("gz"), P("gz"), P(None, "gx")),
        out_specs=(wide, wide),
        check_vma=False,
    )
```

```python
import jax
import jax.numpy as jnp
from jax import lax
from jax.experimental import pallas as pl
from jax.experimental.pallas import tpu as pltpu
from jax.sharding import PartitionSpec as P

COURANT = 0.25
MIXED_BOOST = 4.0
HEAT_RATIO = 3.0
RATIOS = (1.0, HEAT_RATIO)
LEVELS = 40
ROWS = 16
LANES = 128
CELLS = LEVELS * ROWS
COEF = 8
STATE = 4 * ROWS + COEF
PAD = 8
FAR_GROUP = (5, 4, 7, 6, 1, 0, 3, 2)
PARTS = 2
UNROLL = 8
HBM = pl.BlockSpec(memory_space=pltpu.HBM)
VMEM = pl.BlockSpec(memory_space=pltpu.VMEM)
SMEM = pl.BlockSpec(memory_space=pltpu.SMEM)
PARAMS = pltpu.CompilerParams(vmem_limit_bytes=32 * 1024 * 1024)
F32 = jnp.float32


def iota(shape, dim):
    return lax.broadcasted_iota(jnp.int32, shape, dim)


def split3(x, axis):
    high = x.astype(jnp.bfloat16)
    rest = x - high.astype(F32)
    mid = rest.astype(jnp.bfloat16)
    low = (rest - mid.astype(F32)).astype(jnp.bfloat16)
    return jnp.concatenate([high, mid, low], axis=axis)


MEAN = (1.0, -8.0, 37.0, 37.0, -8.0, 1.0)
SKEW = (1.0, -5.0, 10.0, -10.0, 5.0, -1.0)
STEP = (0.0, 0.0, 1.0, -1.0, 0.0, 0.0)


def face_flux(mean, skew, step, speed_sum, mixing_sum):
    speed = speed_sum * (0.5 * COURANT / 60.0)
    return speed * mean + jnp.abs(speed) * skew + (0.5 * mixing_sum) * step


def flux(qs, speed_sum, mixing_sum):
    qm2, qm1, q0, q1, q2, q3 = qs
    step = q0 - q1
    mean = (qm2 + q3) - 8.0 * (qm1 + q2) + 37.0 * (q0 + q1)
    skew = (qm2 - q3) - 5.0 * (qm1 - q2) + 10.0 * step
    return face_flux(mean, skew, step, speed_sum, mixing_sum)


def stencil(coefs, first):
    offset = iota((LANES, LANES), 0) - iota((LANES, LANES), 1) - first
    out = jnp.zeros((LANES, LANES), F32)
    for s, coef in enumerate(coefs):
        if coef:
            out = jnp.where(offset == s, coef, out)
    return out


def dot(x, y):
    return lax.dot_general(x, y, (((1,), (0,)), ((), ())), preferred_element_type=F32)


def strip_selectors():
    rows = [[-1] * 64 for _ in range(4)]
    for field in range(2):
        for cell in range(3):
            rows[field][3 * field + cell] = cell
            rows[field][8 + 3 * field + cell] = LANES - 3 + cell
        for cell in range(5):
            rows[field][16 + 16 * field + 3 + cell] = cell
            rows[field][24 + 16 * field + cell] = LANES - 5 + cell
    for kind in range(2):
        rows[2 + kind][6 + kind] = 0
        rows[2 + kind][14 + kind] = LANES - 1
        for cell in range(3):
            rows[2 + kind][48 + 8 * kind + 1 + cell] = cell
            rows[2 + kind][48 + 8 * kind + 4 + cell] = LANES - 3 + cell
    return rows


def lane_selector(lanes):
    row = iota((len(lanes), LANES), 0)
    lane = iota((len(lanes), LANES), 1)
    hit = jnp.zeros((len(lanes), LANES), jnp.bool_)
    start = 0
    while start < len(lanes):
        if lanes[start] < 0:
            start += 1
            continue
        stop = start + 1
        while stop < len(lanes) and lanes[stop] == lanes[stop - 1] + 1:
            stop += 1
        hit = hit | ((row >= start) & (row < stop) & (lane - row == lanes[start] - start))
        start = stop
    return jnp.where(hit, 1.0, 0.0).astype(jnp.bfloat16)


def pick_lanes(select, x):
    dims = (((1,), (1,)), ((), ()))
    if x.dtype == jnp.bfloat16:
        return lax.dot_general(select, x, dims, preferred_element_type=F32)
    high = x.astype(jnp.bfloat16)
    rest = x - high.astype(F32)
    mid = rest.astype(jnp.bfloat16)
    low = (rest - mid.astype(F32)).astype(jnp.bfloat16)
    parts = [lax.dot_general(select, p, dims, preferred_element_type=F32) for p in (high, mid, low)]
    return parts[0] + (parts[1] + parts[2])


def pack_kernel(
    ws_hbm, ts_hbm, east_hbm, visc_hbm, wn_hbm, tn_hbm, north_hbm, dens_hbm, coup_hbm, top_hbm,
    ws_ref, ts_ref, east_ref, visc_ref, wn_ref, tn_ref, north_ref, parts_ref, far_ref, near_ref, own_ref,
    up_ref, down_ref, rho_ref, inv_ref, coef_ref,
    dens_ref, coup_ref, top_ref, small_sem, sem,
):
    small = [
        pltpu.make_async_copy(src, dst, small_sem.at[i])
        for i, (src, dst) in enumerate(
            ((dens_hbm, dens_ref), (coup_hbm, coup_ref), (top_hbm, top_ref))
        )
    ]
    for copy in small:
        copy.start()
    refs = (ws_ref, ts_ref, east_ref, visc_ref)
    sources = (ws_hbm, ts_hbm, east_hbm, visc_hbm, wn_hbm, tn_hbm, north_hbm)
    targets = (*refs, wn_ref, tn_ref, north_ref)
    pairs = [
        (src, dst.at[:, PAD:PAD + ROWS] if i < 2 else dst) for i, (src, dst) in enumerate(zip(sources, targets))
    ]
    for src, dst in zip(sources[:2], targets):
        pairs.append((src.at[:, ROWS - PAD:], dst.at[:, :PAD]))
        pairs.append((src.at[:, :PAD], dst.at[:, PAD + ROWS:]))
    copies = [pltpu.make_async_copy(src, dst, sem.at[i]) for i, (src, dst) in enumerate(pairs)]
    for copy in copies:
        copy.start()
    selects = [lane_selector(lanes) for lanes in strip_selectors()]
    is_odd = lax.rem(lax.axis_index("gx"), 2) == 1
    for copy in small:
        copy.wait()

    first = lax.axis_index("gz") * LEVELS
    tile = (ROWS, LANES)
    row = iota(tile, 0)
    one = jnp.ones(tile, F32)
    top = jnp.zeros(tile, jnp.int32)
    for j in range(ROWS):
        top = jnp.where(row == j, top_ref[0, j], top)

    def resist(k):
        boost = jnp.where(first + k <= top, 1.0 / (1.0 + MIXED_BOOST), 1.0)
        return boost / (one * coup_ref[k])

    u = [one, one]
    v = [one, one]
    n = [one * dens_ref[0]] * 2
    m = [one * dens_ref[LEVELS - 1]] * 2
    rho_ref[0] = n[0]
    for f in range(2):
        up_ref[f, 0] = u[f]
        down_ref[f, LEVELS - 1] = v[f]
    for k in range(1, LEVELS):
        j = LEVELS - 1 - k
        res_u = resist(k)
        res_v = resist(j + 1)
        rho_ref[k] = one * dens_ref[k]
        for f in range(2):
            u[f] = u[f] + n[f] * (res_u * (1.0 / RATIOS[f]))
            n[f] = n[f] + dens_ref[k] * u[f]
            up_ref[f, k] = u[f]
            v[f] = v[f] + m[f] * (res_v * (1.0 / RATIOS[f]))
            m[f] = m[f] + dens_ref[j] * v[f]
            down_ref[f, j] = v[f]
    inv = [1.0 / n[f] for f in range(2)]

    boost = jnp.where(first <= top, 1.0 + MIXED_BOOST, 1.0)
    below = jnp.where(first >= 1, 1.0, 0.0)
    values = []
    for f in range(2):
        values += [
            down_ref[f, 0] * inv[f],
            inv[f],
            up_ref[f, LEVELS - 1] * inv[f],
            boost * (coup_ref[0] * RATIOS[f] * below),
        ]
    coef_ref[...] = pack_coef(values)
    for f in range(2):
        inv_ref[f] = inv[f]
    for copy in copies[:4]:
        copy.wait()
    left_parts, right_parts = [], []
    for index, (ref, select) in enumerate(zip(refs, selects)):
        x = ref[:, PAD:PAD + ROWS] if ref.shape[1] > ROWS else ref[...]
        x = x.reshape(CELLS, LANES)
        parts = [x]
        if x.dtype == F32:
            high = x.astype(jnp.bfloat16)
            rest = x - high.astype(F32)
            mid = rest.astype(jnp.bfloat16)
            parts = [high, mid]
            for j, value in enumerate(parts):
                parts_ref[index, :, j * LANES:(j + 1) * LANES] = value
        left_parts += [select] * len(parts)
        right_parts += parts
    total = lax.dot_general(
        jnp.concatenate(left_parts, axis=1), jnp.concatenate(right_parts, axis=1),
        (((1,), (1,)), ((), ())), preferred_element_type=F32,
    )
    left, right = total[0:8], total[8:16]
    far_ref[...] = jnp.where(is_odd, right, left)
    near_ref[...] = jnp.where(is_odd, left, right)
    own_ref[...] = total[16:]
    for copy in copies[4:]:
        copy.wait()


def main_kernel(
    wn_ref, tn_ref, north_ref, ws_ref, ts_ref, east_ref, visc_ref, parts_ref,
    up_ref, down_ref, rho_ref, inv_ref, coef_ref,
    rhs_ref, sums_ref, dense_ref, packed_ref, face_ref, stencil_ref,
):
    tile = (ROWS, LANES)
    lane = iota(tile, 1)
    inv = [inv_ref[f] for f in range(2)]

    for k in range(LEVELS):
        packed = jnp.where(lane < 16, up_ref[0, k] * inv[0], down_ref[0, k] * inv[0])
        packed = jnp.where(lane < 32, packed, up_ref[1, k] * inv[1])
        packed = jnp.where(lane < 48, packed, down_ref[1, k] * inv[1])
        packed_ref[k] = jnp.where(lane < 64, packed, rho_ref[k])
    dense_ref[...] = pick_lanes(
        lane_selector([0, 16, 32, 48, 64, -1, -1, -1]), packed_ref[...].reshape(CELLS, LANES)
    )

    column = iota((LANES, LANES), 1)
    pair = jnp.where((column >= 2) & (column <= LANES - 4), stencil((1.0, 1.0), 0), 0.0).astype(jnp.bfloat16)
    row, column = iota((LANES, LANES), 0), iota((LANES, LANES), 1)
    near = (row == column) | ((row // ROWS == column // ROWS) & (lax.rem(row + 1, ROWS) == lax.rem(column, ROWS)))
    pair_y = jnp.where(near, 1.0, 0.0).astype(jnp.bfloat16)
    chunk = LANES // ROWS
    face_ref[0] = dot(east_ref[...].reshape(CELLS, LANES), pair).reshape(LEVELS, ROWS, LANES)
    face_ref[1] = dot(visc_ref[...].reshape(CELLS, LANES), pair).reshape(LEVELS, ROWS, LANES)
    for i, ref in enumerate((north_ref, visc_ref)):
        for k in range(0, LEVELS, chunk):
            x = ref[k:k + chunk].reshape(LANES, LANES)
            face_ref[2 + i, k:k + chunk] = dot(pair_y, x).reshape(chunk, ROWS, LANES)
    weights = jnp.concatenate([stencil(c, -2) for c in (MEAN, SKEW, STEP)], axis=1).astype(jnp.bfloat16)
    weights = jnp.concatenate([weights] * 2, axis=0)
    for f in range(2):
        product = dot(parts_ref[f], weights)
        for j in range(3):
            stencil_ref[f, j] = product[:, j * LANES:(j + 1) * LANES].reshape(LEVELS, ROWS, LANES)

    def level(k, carry):
        weight = rho_ref[k]
        out = []
        for f, (now_ref, sec_ref) in enumerate(((wn_ref, ws_ref), (tn_ref, ts_ref))):
            fx = face_flux(*(stencil_ref[f, j, k] for j in range(3)), face_ref[0, k], face_ref[1, k])
            qy = [sec_ref[k, PAD + s:PAD + s + ROWS] for s in range(-2, 4)]
            fy = flux(qy, face_ref[2, k], face_ref[3, k])
            change = (pltpu.roll(fx, 1, 1) - fx) + (pltpu.roll(fy, 1, 0) - fy)
            explicit = now_ref[k] * (1.0 / 3.0) + (qy[2] + change) * (2.0 / 3.0)
            b = explicit * weight
            rhs_ref[f, k] = b
            out.append(carry[2 * f] + down_ref[f, k] * b)
            out.append(carry[2 * f + 1] + up_ref[f, k] * b)
        return tuple(out)

    def levels(i, carry):
        for step in range(UNROLL):
            carry = level(i * UNROLL + step, carry)
        return carry

    zero = jnp.zeros(tile, F32)
    sums = lax.fori_loop(0, LEVELS // UNROLL, levels, (zero,) * 4)
    for f in range(2):
        sums_ref[f * ROWS:(f + 1) * ROWS] = sums[2 * f] * inv[f]
        sums_ref[(2 + f) * ROWS:(3 + f) * ROWS] = sums[2 * f + 1] * inv[f]
    sums_ref[4 * ROWS:] = coef_ref[...]


def face_spread():
    row = lax.rem(iota((24, LANES), 0), 8)
    lane = iota((24, LANES), 1)
    face = jnp.where(row < 3, row - 1, LANES - 6 + row)
    spread = jnp.where(lane == face, -1.0, 0.0) + jnp.where(lane == face + 1, 1.0, 0.0)
    return jnp.where(row < 6, spread, 0.0).astype(jnp.bfloat16)


def spread_faces(faces):
    return lax.dot_general(
        split3(faces, 0), face_spread(), (((0,), (0,)), ((), ())), preferred_element_type=F32
    )


def edge_kernel(far_ref, near_ref, own_ref, sums_ref, dense_ref, state_ref, faces_ref, strip_ref):
    odd = lax.rem(lax.axis_index("gx"), 2) == 1
    near, far = near_ref[...], far_ref[...]
    left = jnp.where(odd, near, far)
    right = jnp.where(odd, far, near)
    strip_ref[...] = own_ref[...]
    for f in range(2):
        strip_ref[16 * f:16 * f + 3] = left[3 * f:3 * f + 3]
        strip_ref[16 * f + 13:16 * f + 16] = right[3 * f:3 * f + 3]
    for kind in range(2):
        strip_ref[32 + 8 * kind:33 + 8 * kind] = left[6 + kind:7 + kind]
        strip_ref[39 + 8 * kind:40 + 8 * kind] = right[6 + kind:7 + kind]
    faces_ref[...] = jnp.zeros(faces_ref.shape, F32)
    weight = dense_ref[4:5] * (2.0 / 3.0)
    for side in range(2):
        at = 32 + 4 * side
        speed = strip_ref[at:at + 3] + strip_ref[at + 1:at + 4]
        mixing = strip_ref[at + 8:at + 11] + strip_ref[at + 9:at + 12]
        for f in range(2):
            at = 16 * f + 8 * side
            qs = [strip_ref[at + s:at + s + 3] for s in range(6)]
            faces_ref[8 * f + 3 * side:8 * f + 3 * side + 3] = flux(qs, speed, mixing) * weight
    folds = []
    for part in range(2):
        for f in range(2):
            product = faces_ref[8 * f:8 * f + 8] * dense_ref[2 * f + 1 - part:2 * f + 2 - part]
            folded = product[:, :LANES]
            for i in range(1, CELLS // LANES):
                folded = folded + product[:, i * LANES:(i + 1) * LANES]
            folds.append(folded)
    total = spread_faces(jnp.concatenate(folds, axis=1)).reshape(4, LANES // ROWS, ROWS, LANES)
    state_ref[:4 * ROWS] = sums_ref[:4 * ROWS] + jnp.sum(total, axis=1).reshape(4 * ROWS, LANES)
    state_ref[4 * ROWS:] = sums_ref[4 * ROWS:]


def spread_coef(coef, f, i):
    at = 4 * f + i
    return jnp.concatenate([
        jnp.broadcast_to(coef[:, at:at + 1], (COEF, LANES)),
        jnp.broadcast_to(coef[:, at + LANES // 2:at + LANES // 2 + 1], (COEF, LANES)),
    ], axis=0)


def pack_coef(values):
    lane = iota((COEF, LANES), 1)
    coef = jnp.zeros((COEF, LANES), F32)
    for i, value in enumerate(values):
        coef = jnp.where(lane == i, value[:COEF], coef)
        coef = jnp.where(lane == i + LANES // 2, value[COEF:], coef)
    return coef


def unpack(state, f):
    yf = state[f * ROWS:(f + 1) * ROWS]
    yl = state[(2 + f) * ROWS:(3 + f) * ROWS]
    coef = state[4 * ROWS:]
    return (yf, yl, *(spread_coef(coef, f, i) for i in range(4)))


def join(lower, upper):
    yf_a, yl_a, z11_a, z12_a, z22_a, a_a = lower
    yf_b, yl_b, z11_b, z12_b, z22_b, a_b = upper
    g = a_b / (1.0 + a_b * (z22_a + z11_b))
    flow = g * (yl_a - yf_b)
    step_a, step_b = z12_a * g, z12_b * g
    return (
        yf_a - z12_a * flow, yl_b + z12_b * flow,
        z11_a - z12_a * step_a, z12_a * step_b, z22_b - z12_b * step_b, a_a,
    )


def bit(place):
    return lax.rem(lax.div(lax.axis_index("gz"), 1 << place), 2) == 1


def join_pair(own, other, place):
    high = bit(place)
    lower = tuple(jnp.where(high, y, x) for x, y in zip(own, other))
    upper = tuple(jnp.where(high, x, y) for x, y in zip(own, other))
    return join(lower, upper)


def store(state_ref, blocks):
    values = []
    for f, (yf, yl, *coefs) in enumerate(blocks):
        state_ref[f * ROWS:(f + 1) * ROWS] = yf
        state_ref[(2 + f) * ROWS:(3 + f) * ROWS] = yl
        values += coefs
    state_ref[4 * ROWS:] = pack_coef(values)


def four_kernel(own_ref, one_ref, two_ref, three_ref, pair_ref, total_ref):
    pairs, totals = [], []
    for f in range(2):
        own, one, two, three = (unpack(ref[...], f) for ref in (own_ref, one_ref, two_ref, three_ref))
        pairs.append(join_pair(two, three, 0))
        totals.append(join_pair(join_pair(own, one, 0), pairs[f], 1))
    store(total_ref, totals)
    store(pair_ref, pairs)


def local_kernel(
    rhs_ref, up_ref, down_ref, faces_ref, state_ref, one_ref, pair_ref, y_ref, above_ref, below_ref, b_ref
):
    aboves, belows = [], []
    for f in range(2):
        one, pair = unpack(one_ref[...], f), unpack(pair_ref[...], f)
        near, outer = bit(0), bit(1)
        both = join(one, pair)
        aboves.append(tuple(
            jnp.where(near, y, jnp.where(outer, x, z)) for x, y, z in zip(one, pair, both)
        ))
        both = join(pair, one)
        belows.append(tuple(
            jnp.where(near, jnp.where(outer, z, x), y) for x, y, z in zip(one, pair, both)
        ))
    store(above_ref, aboves)
    store(below_ref, belows)
    zero = jnp.zeros((ROWS, LANES), F32)
    coef = state_ref[4 * ROWS:]
    for f in range(2):
        inv = spread_coef(coef, f, 1)
        spread = spread_faces(faces_ref[8 * f:8 * f + 8]).reshape(LEVELS, ROWS, LANES)
        b_ref[f] = (rhs_ref[f] + spread) * inv[None]

    def upward(i, carry):
        carry = list(carry)
        for step in range(UNROLL):
            k = i * UNROLL + step
            for f in range(2):
                carry[f] = carry[f] + up_ref[f, k] * b_ref[f, k]
                y_ref[f, k] = carry[f] * down_ref[f, k]
        return tuple(carry)

    lax.fori_loop(0, LEVELS // UNROLL, upward, (zero, zero))

    def downward(i, carry):
        carry = list(carry)
        for step in range(UNROLL):
            k = LEVELS - 1 - (i * UNROLL + step)
            for f in range(2):
                y_ref[f, k] = y_ref[f, k] + up_ref[f, k] * carry[f]
                carry[f] = carry[f] + down_ref[f, k] * b_ref[f, k]
        return tuple(carry)

    lax.fori_loop(0, LEVELS // UNROLL, downward, (zero, zero))


def above(chain, block, here):
    y, z, a = chain
    yf, yl, z11, z12, z22, a_block = block
    g = a / (1.0 + a * (z + z22))
    new = (yf + z12 * (g * (y - yl)), z11 - z12 * z12 * g, a_block)
    return tuple(jnp.where(here, x, old) for x, old in zip(new, chain))


def below(chain, block, here):
    y, z = chain
    yf, yl, z11, z12, z22, a = block
    g = a / (1.0 + a * (z + z11))
    new = (yl + z12 * (g * (y - yf)), z22 - z12 * z12 * g)
    return tuple(jnp.where(here, x, old) for x, old in zip(new, chain))


def final_kernel(
    y_ref, up_ref, down_ref, own_ref, above_ref, below_ref, a_ref, b_ref, c_ref, w_hbm, t_hbm, out_ref, sem
):
    zero = jnp.zeros((ROWS, LANES), F32)
    own = own_ref[...]
    group = lax.div(lax.axis_index("gz"), 4)
    place = lax.rem(lax.axis_index("gz"), 4)
    others = (a_ref[...], c_ref[...], b_ref[...])
    groups = []
    for j in range(4):
        slot = lax.rem(group, 2) * (1 - 2 * (j % 2)) + j % 2
        slot = slot + 2 * (lax.div(group, 2) * (1 - 2 * (j // 2)) + j // 2)
        groups.append(jnp.where(slot == 1, others[0], jnp.where(slot == 2, others[1], others[2])))
    flows = []
    for f in range(2):
        blocks = [unpack(g, f) for g in groups]
        inner_above, inner_below = unpack(above_ref[...], f), unpack(below_ref[...], f)
        upper, lower = (zero, zero, zero), (zero, zero)
        for j in (3, 2, 1):
            upper = above(upper, blocks[j], j > group)
        for j in (0, 1, 2):
            lower = below(lower, blocks[j], j < group)
        upper = above(upper, inner_above, place < 3)
        lower = below(lower, inner_below, place > 0)
        yf_above, z_above, a_above = upper
        yl_below, z_below = lower
        yf, yl, z11, z12, z22, a = unpack(own, f)
        p = 1.0 + a * (z_below + z11)
        q = 1.0 + a_above * (z_above + z22)
        s_below = a * (yl_below - yf)
        s_above = a_above * (yf_above - yl)
        scale = z12 / (p * q - a * a_above * z12 * z12)
        flows.append((
            (s_below * q - a * z12 * s_above) * scale,
            (s_above * p - a_above * z12 * s_below) * scale,
        ))
    chunk = LEVELS // PARTS
    copies = []
    for part in range(PARTS):
        for f, out in enumerate((w_hbm, t_hbm)):
            for k in range(part * chunk, (part + 1) * chunk):
                out_ref[f, k] = y_ref[f, k] + (down_ref[f, k] * flows[f][0] + up_ref[f, k] * flows[f][1])
            levels = pl.ds(part * chunk, chunk)
            copies.append(pltpu.make_async_copy(
                out_ref.at[f, levels], out.at[levels], sem.at[2 * part + f]
            ))
            copies[-1].start()
    for copy in copies:
        copy.wait()


def call(kernel, shapes, in_specs, scratch=(), out_specs=None, flops=0):
    shapes = [s if isinstance(s, jax.ShapeDtypeStruct) else jax.ShapeDtypeStruct(s, F32) for s in shapes]
    return pl.pallas_call(
        kernel,
        out_shape=shapes,
        in_specs=in_specs,
        out_specs=out_specs or [VMEM] * len(shapes),
        scratch_shapes=list(scratch),
        compiler_params=PARAMS,
        cost_estimate=pl.CostEstimate(flops=flops, bytes_accessed=flops // 8, transcendentals=0),
    )


def shards(
    vertical_now, vertical_section, theta_now, theta_section,
    east_wind, north_wind, eddy_viscosity, density, coupling, cloud_top,
):
    strip = (8, CELLS)
    count = 16
    part = (LEVELS, ROWS, LANES)
    block = (2, *part)
    state_shape = (STATE, LANES)
    wide = jax.ShapeDtypeStruct(part, F32)
    half = jax.ShapeDtypeStruct(part, jnp.bfloat16)
    split = jax.ShapeDtypeStruct((2, CELLS, 2 * LANES), jnp.bfloat16)
    tall = jax.ShapeDtypeStruct((LEVELS, ROWS + 2 * PAD, LANES), F32)

    def in_hbm(*arrays):
        return [pltpu.with_memory_space_constraint(x, pltpu.HBM) for x in arrays]

    tile = (ROWS, LANES)
    ws, ts, east, visc, wn, tn, north, parts, far, near, own, up, down, rho, inv, coef = call(
        pack_kernel,
        [tall, tall, half, half, wide, wide, half, split, strip, strip, (48, CELLS), block, block, part, (2, *tile), (COEF, LANES)],
        [HBM] * 10,
        [
            pltpu.SMEM((LEVELS,), F32),
            pltpu.SMEM((LEVELS,), F32),
            pltpu.SMEM((1, ROWS), jnp.int32),
            pltpu.SemaphoreType.DMA((3,)),
            pltpu.SemaphoreType.DMA((11,)),
        ],
    )(*in_hbm(
        vertical_section, theta_section, east_wind, eddy_viscosity, vertical_now, theta_now, north_wind,
        density, coupling, cloud_top.reshape(1, ROWS),
    ))
    far = lax.ppermute(
        far, "gx", [(i, (i + 1) % count if i % 2 else (i - 1) % count) for i in range(count)]
    )
    near = lax.ppermute(near, "gx", [(i, i ^ 1) for i in range(count)])
    rhs, sums, dense = call(
        main_kernel,
        [block, state_shape, strip],
        [VMEM] * 13,
        [pltpu.VMEM(part, F32), pltpu.VMEM((4, *part), F32), pltpu.VMEM((2, 3, *part), F32)],
        flops=16_000_000,
    )(
        wn, tn, north, ws, ts, east, visc, parts, up, down, rho, inv, coef,
    )
    state, faces = call(
        edge_kernel, [state_shape, (16, CELLS)], [VMEM] * 5, [pltpu.VMEM((48, CELLS), F32)]
    )(far, near, own, sums, dense)

    def swap(x, partner):
        return lax.ppermute(x, "gz", [(i, partner(i)) for i in range(count)])

    three, two, one = (swap(state, lambda i, k=k: i ^ k) for k in (3, 2, 1))
    pair, four = call(four_kernel, [state_shape] * 2, [VMEM] * 4)(state, one, two, three)
    y, inner_above, inner_below = call(
        local_kernel, [block, state_shape, state_shape], [VMEM] * 7, [pltpu.VMEM(block, F32)], flops=4_000_000
    )(rhs, up, down, faces, state, one, pair)
    side_a = swap(four, lambda i: i ^ 4)
    side_b = swap(four, lambda i: (i + 4 if i & 4 else i - 4) % count)
    side_c = swap(four, lambda i: FAR_GROUP[i // 2] * 2 + i % 2)
    return tuple(call(
        final_kernel,
        [part, part],
        [VMEM] * 9,
        [pltpu.VMEM(block, F32), pltpu.SemaphoreType.DMA((2 * PARTS,))],
        [HBM] * 2,
    )(y, up, down, state, inner_above, inner_below, side_a, side_b, side_c))


def solution(mesh):
    wide = P("gz", None, "gx")
    return jax.shard_map(
        shards,
        mesh=mesh,
        in_specs=(wide,) * 7 + (P("gz"), P("gz"), P(None, "gx")),
        out_specs=(wide, wide),
        check_vma=False,
    )
```

```python
import jax
import jax.numpy as jnp
from jax import lax
from jax.experimental import pallas as pl
from jax.experimental.pallas import tpu as pltpu
from jax.sharding import PartitionSpec as P

COURANT = 0.25
MIXED_BOOST = 4.0
HEAT_RATIO = 3.0
RATIOS = (1.0, HEAT_RATIO)
LEVELS = 40
ROWS = 16
LANES = 128
CELLS = LEVELS * ROWS
COEF = 8
STATE = 4 * ROWS + COEF
PAD = 8
FAR_GROUP = (5, 4, 7, 6, 1, 0, 3, 2)
PARTS = 2
UNROLL = 8
HBM = pl.BlockSpec(memory_space=pltpu.HBM)
VMEM = pl.BlockSpec(memory_space=pltpu.VMEM)
SMEM = pl.BlockSpec(memory_space=pltpu.SMEM)
PARAMS = pltpu.CompilerParams(vmem_limit_bytes=32 * 1024 * 1024)
F32 = jnp.float32


def iota(shape, dim):
    return lax.broadcasted_iota(jnp.int32, shape, dim)


def split3(x, axis):
    high = x.astype(jnp.bfloat16)
    rest = x - high.astype(F32)
    mid = rest.astype(jnp.bfloat16)
    low = (rest - mid.astype(F32)).astype(jnp.bfloat16)
    return jnp.concatenate([high, mid, low], axis=axis)


MEAN = (1.0, -8.0, 37.0, 37.0, -8.0, 1.0)
SKEW = (1.0, -5.0, 10.0, -10.0, 5.0, -1.0)
STEP = (0.0, 0.0, 1.0, -1.0, 0.0, 0.0)


def face_flux(mean, skew, step, speed_sum, mixing_sum):
    speed = speed_sum * (0.5 * COURANT / 60.0)
    return speed * mean + jnp.abs(speed) * skew + (0.5 * mixing_sum) * step


def flux(qs, speed_sum, mixing_sum):
    qm2, qm1, q0, q1, q2, q3 = qs
    step = q0 - q1
    mean = (qm2 + q3) - 8.0 * (qm1 + q2) + 37.0 * (q0 + q1)
    skew = (qm2 - q3) - 5.0 * (qm1 - q2) + 10.0 * step
    return face_flux(mean, skew, step, speed_sum, mixing_sum)


def stencil(coefs, first):
    offset = iota((LANES, LANES), 0) - iota((LANES, LANES), 1) - first
    out = jnp.zeros((LANES, LANES), F32)
    for s, coef in enumerate(coefs):
        if coef:
            out = jnp.where(offset == s, coef, out)
    return out


def dot(x, y):
    return lax.dot_general(x, y, (((1,), (0,)), ((), ())), preferred_element_type=F32)


def strip_selectors():
    rows = [[-1] * 64 for _ in range(4)]
    for field in range(2):
        for cell in range(3):
            rows[field][3 * field + cell] = cell
            rows[field][8 + 3 * field + cell] = LANES - 3 + cell
        for cell in range(5):
            rows[field][16 + 16 * field + 3 + cell] = cell
            rows[field][24 + 16 * field + cell] = LANES - 5 + cell
    for kind in range(2):
        rows[2 + kind][6 + kind] = 0
        rows[2 + kind][14 + kind] = LANES - 1
        for cell in range(3):
            rows[2 + kind][48 + 8 * kind + 1 + cell] = cell
            rows[2 + kind][48 + 8 * kind + 4 + cell] = LANES - 3 + cell
    return rows


def lane_selector(lanes):
    row = iota((len(lanes), LANES), 0)
    lane = iota((len(lanes), LANES), 1)
    hit = jnp.zeros((len(lanes), LANES), jnp.bool_)
    start = 0
    while start < len(lanes):
        if lanes[start] < 0:
            start += 1
            continue
        stop = start + 1
        while stop < len(lanes) and lanes[stop] == lanes[stop - 1] + 1:
            stop += 1
        hit = hit | ((row >= start) & (row < stop) & (lane - row == lanes[start] - start))
        start = stop
    return jnp.where(hit, 1.0, 0.0).astype(jnp.bfloat16)


def pick_lanes(select, x):
    dims = (((1,), (1,)), ((), ()))
    if x.dtype == jnp.bfloat16:
        return lax.dot_general(select, x, dims, preferred_element_type=F32)
    high = x.astype(jnp.bfloat16)
    rest = x - high.astype(F32)
    mid = rest.astype(jnp.bfloat16)
    low = (rest - mid.astype(F32)).astype(jnp.bfloat16)
    parts = [lax.dot_general(select, p, dims, preferred_element_type=F32) for p in (high, mid, low)]
    return parts[0] + (parts[1] + parts[2])


def pack_kernel(
    ws_hbm, ts_hbm, east_hbm, visc_hbm, wn_hbm, tn_hbm, north_hbm, dens_hbm, coup_hbm, top_hbm,
    ws_ref, ts_ref, east_ref, visc_ref, wn_ref, tn_ref, north_ref, parts_ref, far_ref, near_ref, own_ref,
    up_ref, down_ref, rho_ref, inv_ref, coef_ref,
    dens_ref, coup_ref, top_ref, small_sem, sem,
):
    small = [
        pltpu.make_async_copy(src, dst, small_sem.at[i])
        for i, (src, dst) in enumerate(
            ((dens_hbm, dens_ref), (coup_hbm, coup_ref), (top_hbm, top_ref))
        )
    ]
    for copy in small:
        copy.start()
    refs = (ws_ref, ts_ref, east_ref, visc_ref)
    sources = (ws_hbm, ts_hbm, east_hbm, visc_hbm, wn_hbm, tn_hbm, north_hbm)
    targets = (*refs, wn_ref, tn_ref, north_ref)
    copies = [
        pltpu.make_async_copy(src, dst, sem.at[i]) for i, (src, dst) in enumerate(zip(sources, targets))
    ]
    for copy in copies:
        copy.start()
    selects = [lane_selector(lanes) for lanes in strip_selectors()]
    is_odd = lax.rem(lax.axis_index("gx"), 2) == 1
    for copy in small:
        copy.wait()

    first = lax.axis_index("gz") * LEVELS
    tile = (ROWS, LANES)
    row = iota(tile, 0)
    one = jnp.ones(tile, F32)
    top = jnp.zeros(tile, jnp.int32)
    for j in range(ROWS):
        top = jnp.where(row == j, top_ref[0, j], top)

    def resist(k):
        boost = jnp.where(first + k <= top, 1.0 / (1.0 + MIXED_BOOST), 1.0)
        return boost / (one * coup_ref[k])

    u = [one, one]
    v = [one, one]
    n = [one * dens_ref[0]] * 2
    m = [one * dens_ref[LEVELS - 1]] * 2
    rho_ref[0] = n[0]
    for f in range(2):
        up_ref[f, 0] = u[f]
        down_ref[f, LEVELS - 1] = v[f]
    for k in range(1, LEVELS):
        j = LEVELS - 1 - k
        res_u = resist(k)
        res_v = resist(j + 1)
        rho_ref[k] = one * dens_ref[k]
        for f in range(2):
            u[f] = u[f] + n[f] * (res_u * (1.0 / RATIOS[f]))
            n[f] = n[f] + dens_ref[k] * u[f]
            up_ref[f, k] = u[f]
            v[f] = v[f] + m[f] * (res_v * (1.0 / RATIOS[f]))
            m[f] = m[f] + dens_ref[j] * v[f]
            down_ref[f, j] = v[f]
    inv = [1.0 / n[f] for f in range(2)]

    boost = jnp.where(first <= top, 1.0 + MIXED_BOOST, 1.0)
    below = jnp.where(first >= 1, 1.0, 0.0)
    values = []
    for f in range(2):
        values += [
            down_ref[f, 0] * inv[f],
            inv[f],
            up_ref[f, LEVELS - 1] * inv[f],
            boost * (coup_ref[0] * RATIOS[f] * below),
        ]
    coef_ref[...] = pack_coef(values)
    for f in range(2):
        inv_ref[f] = inv[f]
    for copy in copies[:4]:
        copy.wait()
    left_parts, right_parts = [], []
    for index, (ref, select) in enumerate(zip(refs, selects)):
        x = ref[...].reshape(CELLS, LANES)
        parts = [x]
        if x.dtype == F32:
            high = x.astype(jnp.bfloat16)
            rest = x - high.astype(F32)
            mid = rest.astype(jnp.bfloat16)
            parts = [high, mid]
            for j, value in enumerate(parts):
                parts_ref[index, :, j * LANES:(j + 1) * LANES] = value
        left_parts += [select] * len(parts)
        right_parts += parts
    total = lax.dot_general(
        jnp.concatenate(left_parts, axis=1), jnp.concatenate(right_parts, axis=1),
        (((1,), (1,)), ((), ())), preferred_element_type=F32,
    )
    left, right = total[0:8], total[8:16]
    far_ref[...] = jnp.where(is_odd, right, left)
    near_ref[...] = jnp.where(is_odd, left, right)
    own_ref[...] = total[16:]
    for copy in copies[4:]:
        copy.wait()


def main_kernel(
    wn_ref, tn_ref, north_ref, w_ref, t_ref, east_ref, visc_ref, parts_ref,
    up_ref, down_ref, rho_ref, inv_ref, coef_ref,
    rhs_ref, sums_ref, dense_ref, packed_ref, face_ref, stencil_ref, ws_ref, ts_ref, sem,
):
    pairs = []
    for src, dst in ((w_ref, ws_ref), (t_ref, ts_ref)):
        pairs.append((src, dst.at[:, PAD:PAD + ROWS]))
        pairs.append((src.at[:, ROWS - PAD:], dst.at[:, :PAD]))
        pairs.append((src.at[:, :PAD], dst.at[:, PAD + ROWS:]))
    copies = [pltpu.make_async_copy(src, dst, sem.at[i]) for i, (src, dst) in enumerate(pairs)]
    for copy in copies:
        copy.start()
    tile = (ROWS, LANES)
    lane = iota(tile, 1)
    inv = [inv_ref[f] for f in range(2)]

    for k in range(LEVELS):
        packed = jnp.where(lane < 16, up_ref[0, k] * inv[0], down_ref[0, k] * inv[0])
        packed = jnp.where(lane < 32, packed, up_ref[1, k] * inv[1])
        packed = jnp.where(lane < 48, packed, down_ref[1, k] * inv[1])
        packed_ref[k] = jnp.where(lane < 64, packed, rho_ref[k])
    dense_ref[...] = pick_lanes(
        lane_selector([0, 16, 32, 48, 64, -1, -1, -1]), packed_ref[...].reshape(CELLS, LANES)
    )

    column = iota((LANES, LANES), 1)
    pair = jnp.where((column >= 2) & (column <= LANES - 4), stencil((1.0, 1.0), 0), 0.0).astype(jnp.bfloat16)
    row, column = iota((LANES, LANES), 0), iota((LANES, LANES), 1)
    near = (row == column) | ((row // ROWS == column // ROWS) & (lax.rem(row + 1, ROWS) == lax.rem(column, ROWS)))
    pair_y = jnp.where(near, 1.0, 0.0).astype(jnp.bfloat16)
    chunk = LANES // ROWS
    face_ref[0] = dot(east_ref[...].reshape(CELLS, LANES), pair).reshape(LEVELS, ROWS, LANES)
    face_ref[1] = dot(visc_ref[...].reshape(CELLS, LANES), pair).reshape(LEVELS, ROWS, LANES)
    for i, ref in enumerate((north_ref, visc_ref)):
        for k in range(0, LEVELS, chunk):
            x = ref[k:k + chunk].reshape(LANES, LANES)
            face_ref[2 + i, k:k + chunk] = dot(pair_y, x).reshape(chunk, ROWS, LANES)
    weights = jnp.concatenate([stencil(c, -2) for c in (MEAN, SKEW, STEP)], axis=1).astype(jnp.bfloat16)
    weights = jnp.concatenate([weights] * 2, axis=0)
    for f in range(2):
        product = dot(parts_ref[f], weights)
        for j in range(3):
            stencil_ref[f, j] = product[:, j * LANES:(j + 1) * LANES].reshape(LEVELS, ROWS, LANES)

    for copy in copies:
        copy.wait()

    def level(k, carry):
        weight = rho_ref[k]
        out = []
        for f, (now_ref, sec_ref) in enumerate(((wn_ref, ws_ref), (tn_ref, ts_ref))):
            fx = face_flux(*(stencil_ref[f, j, k] for j in range(3)), face_ref[0, k], face_ref[1, k])
            qy = [sec_ref[k, PAD + s:PAD + s + ROWS] for s in range(-2, 4)]
            fy = flux(qy, face_ref[2, k], face_ref[3, k])
            change = (pltpu.roll(fx, 1, 1) - fx) + (pltpu.roll(fy, 1, 0) - fy)
            explicit = now_ref[k] * (1.0 / 3.0) + (qy[2] + change) * (2.0 / 3.0)
            b = explicit * weight
            rhs_ref[f, k] = b
            out.append(carry[2 * f] + down_ref[f, k] * b)
            out.append(carry[2 * f + 1] + up_ref[f, k] * b)
        return tuple(out)

    def levels(i, carry):
        for step in range(UNROLL):
            carry = level(i * UNROLL + step, carry)
        return carry

    zero = jnp.zeros(tile, F32)
    sums = lax.fori_loop(0, LEVELS // UNROLL, levels, (zero,) * 4)
    for f in range(2):
        sums_ref[f * ROWS:(f + 1) * ROWS] = sums[2 * f] * inv[f]
        sums_ref[(2 + f) * ROWS:(3 + f) * ROWS] = sums[2 * f + 1] * inv[f]
    sums_ref[4 * ROWS:] = coef_ref[...]


def face_spread():
    row = lax.rem(iota((24, LANES), 0), 8)
    lane = iota((24, LANES), 1)
    face = jnp.where(row < 3, row - 1, LANES - 6 + row)
    spread = jnp.where(lane == face, -1.0, 0.0) + jnp.where(lane == face + 1, 1.0, 0.0)
    return jnp.where(row < 6, spread, 0.0).astype(jnp.bfloat16)


def spread_faces(faces):
    return lax.dot_general(
        split3(faces, 0), face_spread(), (((0,), (0,)), ((), ())), preferred_element_type=F32
    )


def edge_kernel(far_ref, near_ref, own_ref, sums_ref, dense_ref, state_ref, faces_ref, strip_ref):
    odd = lax.rem(lax.axis_index("gx"), 2) == 1
    near, far = near_ref[...], far_ref[...]
    left = jnp.where(odd, near, far)
    right = jnp.where(odd, far, near)
    strip_ref[...] = own_ref[...]
    for f in range(2):
        strip_ref[16 * f:16 * f + 3] = left[3 * f:3 * f + 3]
        strip_ref[16 * f + 13:16 * f + 16] = right[3 * f:3 * f + 3]
    for kind in range(2):
        strip_ref[32 + 8 * kind:33 + 8 * kind] = left[6 + kind:7 + kind]
        strip_ref[39 + 8 * kind:40 + 8 * kind] = right[6 + kind:7 + kind]
    faces_ref[...] = jnp.zeros(faces_ref.shape, F32)
    weight = dense_ref[4:5] * (2.0 / 3.0)
    for side in range(2):
        at = 32 + 4 * side
        speed = strip_ref[at:at + 3] + strip_ref[at + 1:at + 4]
        mixing = strip_ref[at + 8:at + 11] + strip_ref[at + 9:at + 12]
        for f in range(2):
            at = 16 * f + 8 * side
            qs = [strip_ref[at + s:at + s + 3] for s in range(6)]
            faces_ref[8 * f + 3 * side:8 * f + 3 * side + 3] = flux(qs, speed, mixing) * weight
    folds = []
    for part in range(2):
        for f in range(2):
            product = faces_ref[8 * f:8 * f + 8] * dense_ref[2 * f + 1 - part:2 * f + 2 - part]
            folded = product[:, :LANES]
            for i in range(1, CELLS // LANES):
                folded = folded + product[:, i * LANES:(i + 1) * LANES]
            folds.append(folded)
    total = spread_faces(jnp.concatenate(folds, axis=1)).reshape(4, LANES // ROWS, ROWS, LANES)
    state_ref[:4 * ROWS] = sums_ref[:4 * ROWS] + jnp.sum(total, axis=1).reshape(4 * ROWS, LANES)
    state_ref[4 * ROWS:] = sums_ref[4 * ROWS:]


def spread_coef(coef, f, i):
    at = 4 * f + i
    return jnp.concatenate([
        jnp.broadcast_to(coef[:, at:at + 1], (COEF, LANES)),
        jnp.broadcast_to(coef[:, at + LANES // 2:at + LANES // 2 + 1], (COEF, LANES)),
    ], axis=0)


def pack_coef(values):
    lane = iota((COEF, LANES), 1)
    coef = jnp.zeros((COEF, LANES), F32)
    for i, value in enumerate(values):
        coef = jnp.where(lane == i, value[:COEF], coef)
        coef = jnp.where(lane == i + LANES // 2, value[COEF:], coef)
    return coef


def unpack(state, f):
    yf = state[f * ROWS:(f + 1) * ROWS]
    yl = state[(2 + f) * ROWS:(3 + f) * ROWS]
    coef = state[4 * ROWS:]
    return (yf, yl, *(spread_coef(coef, f, i) for i in range(4)))


def join(lower, upper):
    yf_a, yl_a, z11_a, z12_a, z22_a, a_a = lower
    yf_b, yl_b, z11_b, z12_b, z22_b, a_b = upper
    g = a_b / (1.0 + a_b * (z22_a + z11_b))
    flow = g * (yl_a - yf_b)
    step_a, step_b = z12_a * g, z12_b * g
    return (
        yf_a - z12_a * flow, yl_b + z12_b * flow,
        z11_a - z12_a * step_a, z12_a * step_b, z22_b - z12_b * step_b, a_a,
    )


def bit(place):
    return lax.rem(lax.div(lax.axis_index("gz"), 1 << place), 2) == 1


def join_pair(own, other, place):
    high = bit(place)
    lower = tuple(jnp.where(high, y, x) for x, y in zip(own, other))
    upper = tuple(jnp.where(high, x, y) for x, y in zip(own, other))
    return join(lower, upper)


def store(state_ref, blocks):
    values = []
    for f, (yf, yl, *coefs) in enumerate(blocks):
        state_ref[f * ROWS:(f + 1) * ROWS] = yf
        state_ref[(2 + f) * ROWS:(3 + f) * ROWS] = yl
        values += coefs
    state_ref[4 * ROWS:] = pack_coef(values)


def four_kernel(own_ref, one_ref, two_ref, three_ref, pair_ref, total_ref):
    pairs, totals = [], []
    for f in range(2):
        own, one, two, three = (unpack(ref[...], f) for ref in (own_ref, one_ref, two_ref, three_ref))
        pairs.append(join_pair(two, three, 0))
        totals.append(join_pair(join_pair(own, one, 0), pairs[f], 1))
    store(total_ref, totals)
    store(pair_ref, pairs)


def local_kernel(
    rhs_ref, up_ref, down_ref, faces_ref, state_ref, one_ref, pair_ref, y_ref, above_ref, below_ref, b_ref
):
    aboves, belows = [], []
    for f in range(2):
        one, pair = unpack(one_ref[...], f), unpack(pair_ref[...], f)
        near, outer = bit(0), bit(1)
        both = join(one, pair)
        aboves.append(tuple(
            jnp.where(near, y, jnp.where(outer, x, z)) for x, y, z in zip(one, pair, both)
        ))
        both = join(pair, one)
        belows.append(tuple(
            jnp.where(near, jnp.where(outer, z, x), y) for x, y, z in zip(one, pair, both)
        ))
    store(above_ref, aboves)
    store(below_ref, belows)
    zero = jnp.zeros((ROWS, LANES), F32)
    coef = state_ref[4 * ROWS:]
    for f in range(2):
        inv = spread_coef(coef, f, 1)
        spread = spread_faces(faces_ref[8 * f:8 * f + 8]).reshape(LEVELS, ROWS, LANES)
        b_ref[f] = (rhs_ref[f] + spread) * inv[None]

    def upward(i, carry):
        carry = list(carry)
        for step in range(UNROLL):
            k = i * UNROLL + step
            for f in range(2):
                carry[f] = carry[f] + up_ref[f, k] * b_ref[f, k]
                y_ref[f, k] = carry[f] * down_ref[f, k]
        return tuple(carry)

    lax.fori_loop(0, LEVELS // UNROLL, upward, (zero, zero))

    def downward(i, carry):
        carry = list(carry)
        for step in range(UNROLL):
            k = LEVELS - 1 - (i * UNROLL + step)
            for f in range(2):
                y_ref[f, k] = y_ref[f, k] + up_ref[f, k] * carry[f]
                carry[f] = carry[f] + down_ref[f, k] * b_ref[f, k]
        return tuple(carry)

    lax.fori_loop(0, LEVELS // UNROLL, downward, (zero, zero))


def above(chain, block, here):
    y, z, a = chain
    yf, yl, z11, z12, z22, a_block = block
    g = a / (1.0 + a * (z + z22))
    new = (yf + z12 * (g * (y - yl)), z11 - z12 * z12 * g, a_block)
    return tuple(jnp.where(here, x, old) for x, old in zip(new, chain))


def below(chain, block, here):
    y, z = chain
    yf, yl, z11, z12, z22, a = block
    g = a / (1.0 + a * (z + z11))
    new = (yl + z12 * (g * (y - yf)), z22 - z12 * z12 * g)
    return tuple(jnp.where(here, x, old) for x, old in zip(new, chain))


def final_kernel(
    y_ref, up_ref, down_ref, own_ref, above_ref, below_ref, a_ref, b_ref, c_ref, w_hbm, t_hbm, out_ref, sem
):
    zero = jnp.zeros((ROWS, LANES), F32)
    own = own_ref[...]
    group = lax.div(lax.axis_index("gz"), 4)
    place = lax.rem(lax.axis_index("gz"), 4)
    others = (a_ref[...], c_ref[...], b_ref[...])
    groups = []
    for j in range(4):
        slot = lax.rem(group, 2) * (1 - 2 * (j % 2)) + j % 2
        slot = slot + 2 * (lax.div(group, 2) * (1 - 2 * (j // 2)) + j // 2)
        groups.append(jnp.where(slot == 1, others[0], jnp.where(slot == 2, others[1], others[2])))
    flows = []
    for f in range(2):
        blocks = [unpack(g, f) for g in groups]
        inner_above, inner_below = unpack(above_ref[...], f), unpack(below_ref[...], f)
        upper, lower = (zero, zero, zero), (zero, zero)
        for j in (3, 2, 1):
            upper = above(upper, blocks[j], j > group)
        for j in (0, 1, 2):
            lower = below(lower, blocks[j], j < group)
        upper = above(upper, inner_above, place < 3)
        lower = below(lower, inner_below, place > 0)
        yf_above, z_above, a_above = upper
        yl_below, z_below = lower
        yf, yl, z11, z12, z22, a = unpack(own, f)
        p = 1.0 + a * (z_below + z11)
        q = 1.0 + a_above * (z_above + z22)
        s_below = a * (yl_below - yf)
        s_above = a_above * (yf_above - yl)
        scale = z12 / (p * q - a * a_above * z12 * z12)
        flows.append((
            (s_below * q - a * z12 * s_above) * scale,
            (s_above * p - a_above * z12 * s_below) * scale,
        ))
    chunk = LEVELS // PARTS
    copies = []
    for part in range(PARTS):
        for f, out in enumerate((w_hbm, t_hbm)):
            for k in range(part * chunk, (part + 1) * chunk):
                out_ref[f, k] = y_ref[f, k] + (down_ref[f, k] * flows[f][0] + up_ref[f, k] * flows[f][1])
            levels = pl.ds(part * chunk, chunk)
            copies.append(pltpu.make_async_copy(
                out_ref.at[f, levels], out.at[levels], sem.at[2 * part + f]
            ))
            copies[-1].start()
    for copy in copies:
        copy.wait()


def call(kernel, shapes, in_specs, scratch=(), out_specs=None, flops=0):
    shapes = [s if isinstance(s, jax.ShapeDtypeStruct) else jax.ShapeDtypeStruct(s, F32) for s in shapes]
    return pl.pallas_call(
        kernel,
        out_shape=shapes,
        in_specs=in_specs,
        out_specs=out_specs or [VMEM] * len(shapes),
        scratch_shapes=list(scratch),
        compiler_params=PARAMS,
        cost_estimate=pl.CostEstimate(flops=flops, bytes_accessed=flops // 8, transcendentals=0),
    )


def shards(
    vertical_now, vertical_section, theta_now, theta_section,
    east_wind, north_wind, eddy_viscosity, density, coupling, cloud_top,
):
    strip = (8, CELLS)
    count = 16
    part = (LEVELS, ROWS, LANES)
    block = (2, *part)
    state_shape = (STATE, LANES)
    wide = jax.ShapeDtypeStruct(part, F32)
    half = jax.ShapeDtypeStruct(part, jnp.bfloat16)
    split = jax.ShapeDtypeStruct((2, CELLS, 2 * LANES), jnp.bfloat16)
    tall = (LEVELS, ROWS + 2 * PAD, LANES)

    def in_hbm(*arrays):
        return [pltpu.with_memory_space_constraint(x, pltpu.HBM) for x in arrays]

    tile = (ROWS, LANES)
    ws, ts, east, visc, wn, tn, north, parts, far, near, own, up, down, rho, inv, coef = call(
        pack_kernel,
        [wide, wide, half, half, wide, wide, half, split, strip, strip, (48, CELLS), block, block, part, (2, *tile), (COEF, LANES)],
        [HBM] * 10,
        [
            pltpu.SMEM((LEVELS,), F32),
            pltpu.SMEM((LEVELS,), F32),
            pltpu.SMEM((1, ROWS), jnp.int32),
            pltpu.SemaphoreType.DMA((3,)),
            pltpu.SemaphoreType.DMA((7,)),
        ],
    )(*in_hbm(
        vertical_section, theta_section, east_wind, eddy_viscosity, vertical_now, theta_now, north_wind,
        density, coupling, cloud_top.reshape(1, ROWS),
    ))
    far = lax.ppermute(
        far, "gx", [(i, (i + 1) % count if i % 2 else (i - 1) % count) for i in range(count)]
    )
    near = lax.ppermute(near, "gx", [(i, i ^ 1) for i in range(count)])
    rhs, sums, dense = call(
        main_kernel,
        [block, state_shape, strip],
        [VMEM] * 13,
        [
            pltpu.VMEM(part, F32),
            pltpu.VMEM((4, *part), F32),
            pltpu.VMEM((2, 3, *part), F32),
            pltpu.VMEM(tall, F32),
            pltpu.VMEM(tall, F32),
            pltpu.SemaphoreType.DMA((6,)),
        ],
        flops=16_000_000,
    )(
        wn, tn, north, ws, ts, east, visc, parts, up, down, rho, inv, coef,
    )
    state, faces = call(
        edge_kernel, [state_shape, (16, CELLS)], [VMEM] * 5, [pltpu.VMEM((48, CELLS), F32)]
    )(far, near, own, sums, dense)

    def swap(x, partner):
        return lax.ppermute(x, "gz", [(i, partner(i)) for i in range(count)])

    three, two, one = (swap(state, lambda i, k=k: i ^ k) for k in (3, 2, 1))
    pair, four = call(four_kernel, [state_shape] * 2, [VMEM] * 4)(state, one, two, three)
    y, inner_above, inner_below = call(
        local_kernel, [block, state_shape, state_shape], [VMEM] * 7, [pltpu.VMEM(block, F32)], flops=4_000_000
    )(rhs, up, down, faces, state, one, pair)
    side_a = swap(four, lambda i: i ^ 4)
    side_b = swap(four, lambda i: (i + 4 if i & 4 else i - 4) % count)
    side_c = swap(four, lambda i: FAR_GROUP[i // 2] * 2 + i % 2)
    return tuple(call(
        final_kernel,
        [part, part],
        [VMEM] * 9,
        [pltpu.VMEM(block, F32), pltpu.SemaphoreType.DMA((2 * PARTS,))],
        [HBM] * 2,
    )(y, up, down, state, inner_above, inner_below, side_a, side_b, side_c))


def solution(mesh):
    wide = P("gz", None, "gx")
    return jax.shard_map(
        shards,
        mesh=mesh,
        in_specs=(wide,) * 7 + (P("gz"), P("gz"), P(None, "gx")),
        out_specs=(wide, wide),
        check_vma=False,
    )
```

```python
import jax
import jax.numpy as jnp
from jax import lax
from jax.experimental import pallas as pl
from jax.experimental.pallas import tpu as pltpu
from jax.sharding import PartitionSpec as P

COURANT = 0.25
MIXED_BOOST = 4.0
HEAT_RATIO = 3.0
RATIOS = (1.0, HEAT_RATIO)
LEVELS = 40
ROWS = 16
LANES = 128
CELLS = LEVELS * ROWS
COEF = 8
STATE = 4 * ROWS + COEF
PAD = 8
FAR_GROUP = (5, 4, 7, 6, 1, 0, 3, 2)
PARTS = 2
UNROLL = 20
HBM = pl.BlockSpec(memory_space=pltpu.HBM)
VMEM = pl.BlockSpec(memory_space=pltpu.VMEM)
SMEM = pl.BlockSpec(memory_space=pltpu.SMEM)
PARAMS = pltpu.CompilerParams(vmem_limit_bytes=32 * 1024 * 1024)
F32 = jnp.float32


def iota(shape, dim):
    return lax.broadcasted_iota(jnp.int32, shape, dim)


def split3(x, axis):
    high = x.astype(jnp.bfloat16)
    rest = x - high.astype(F32)
    mid = rest.astype(jnp.bfloat16)
    low = (rest - mid.astype(F32)).astype(jnp.bfloat16)
    return jnp.concatenate([high, mid, low], axis=axis)


MEAN = (1.0, -8.0, 37.0, 37.0, -8.0, 1.0)
SKEW = (1.0, -5.0, 10.0, -10.0, 5.0, -1.0)
STEP = (0.0, 0.0, 1.0, -1.0, 0.0, 0.0)


def face_flux(mean, skew, step, speed_sum, mixing_sum):
    speed = speed_sum * (0.5 * COURANT / 60.0)
    return speed * mean + jnp.abs(speed) * skew + (0.5 * mixing_sum) * step


def flux(qs, speed_sum, mixing_sum):
    qm2, qm1, q0, q1, q2, q3 = qs
    step = q0 - q1
    mean = (qm2 + q3) - 8.0 * (qm1 + q2) + 37.0 * (q0 + q1)
    skew = (qm2 - q3) - 5.0 * (qm1 - q2) + 10.0 * step
    return face_flux(mean, skew, step, speed_sum, mixing_sum)


def stencil(coefs, first):
    offset = iota((LANES, LANES), 0) - iota((LANES, LANES), 1) - first
    out = jnp.zeros((LANES, LANES), F32)
    for s, coef in enumerate(coefs):
        if coef:
            out = jnp.where(offset == s, coef, out)
    return out


def dot(x, y):
    return lax.dot_general(x, y, (((1,), (0,)), ((), ())), preferred_element_type=F32)


def strip_selectors():
    rows = [[-1] * 64 for _ in range(4)]
    for field in range(2):
        for cell in range(3):
            rows[field][3 * field + cell] = cell
            rows[field][8 + 3 * field + cell] = LANES - 3 + cell
        for cell in range(5):
            rows[field][16 + 16 * field + 3 + cell] = cell
            rows[field][24 + 16 * field + cell] = LANES - 5 + cell
    for kind in range(2):
        rows[2 + kind][6 + kind] = 0
        rows[2 + kind][14 + kind] = LANES - 1
        for cell in range(3):
            rows[2 + kind][48 + 8 * kind + 1 + cell] = cell
            rows[2 + kind][48 + 8 * kind + 4 + cell] = LANES - 3 + cell
    return rows


def lane_selector(lanes):
    row = iota((len(lanes), LANES), 0)
    lane = iota((len(lanes), LANES), 1)
    hit = jnp.zeros((len(lanes), LANES), jnp.bool_)
    start = 0
    while start < len(lanes):
        if lanes[start] < 0:
            start += 1
            continue
        stop = start + 1
        while stop < len(lanes) and lanes[stop] == lanes[stop - 1] + 1:
            stop += 1
        hit = hit | ((row >= start) & (row < stop) & (lane - row == lanes[start] - start))
        start = stop
    return jnp.where(hit, 1.0, 0.0).astype(jnp.bfloat16)


def pick_lanes(select, x):
    dims = (((1,), (1,)), ((), ()))
    if x.dtype == jnp.bfloat16:
        return lax.dot_general(select, x, dims, preferred_element_type=F32)
    high = x.astype(jnp.bfloat16)
    rest = x - high.astype(F32)
    mid = rest.astype(jnp.bfloat16)
    low = (rest - mid.astype(F32)).astype(jnp.bfloat16)
    parts = [lax.dot_general(select, p, dims, preferred_element_type=F32) for p in (high, mid, low)]
    return parts[0] + (parts[1] + parts[2])


def pack_kernel(
    ws_hbm, ts_hbm, east_hbm, visc_hbm, wn_hbm, tn_hbm, north_hbm, dens_hbm, coup_hbm, top_hbm,
    ws_ref, ts_ref, east_ref, visc_ref, wn_ref, tn_ref, north_ref, far_ref, near_ref, own_ref,
    up_ref, down_ref, rho_ref, inv_ref, coef_ref,
    dens_ref, coup_ref, top_ref, small_sem, sem,
):
    small = [
        pltpu.make_async_copy(src, dst, small_sem.at[i])
        for i, (src, dst) in enumerate(
            ((dens_hbm, dens_ref), (coup_hbm, coup_ref), (top_hbm, top_ref))
        )
    ]
    for copy in small:
        copy.start()
    refs = (ws_ref, ts_ref, east_ref, visc_ref)
    sources = (ws_hbm, ts_hbm, east_hbm, visc_hbm, wn_hbm, tn_hbm, north_hbm)
    targets = (*refs, wn_ref, tn_ref, north_ref)
    copies = [
        pltpu.make_async_copy(src, dst, sem.at[i]) for i, (src, dst) in enumerate(zip(sources, targets))
    ]
    for copy in copies:
        copy.start()
    selects = [lane_selector(lanes) for lanes in strip_selectors()]
    is_odd = lax.rem(lax.axis_index("gx"), 2) == 1
    for copy in small:
        copy.wait()

    first = lax.axis_index("gz") * LEVELS
    tile = (ROWS, LANES)
    row = iota(tile, 0)
    one = jnp.ones(tile, F32)
    top = jnp.zeros(tile, jnp.int32)
    for j in range(ROWS):
        top = jnp.where(row == j, top_ref[0, j], top)

    def resist(k):
        boost = jnp.where(first + k <= top, 1.0 / (1.0 + MIXED_BOOST), 1.0)
        return boost / (one * coup_ref[k])

    u = [one, one]
    v = [one, one]
    n = [one * dens_ref[0]] * 2
    m = [one * dens_ref[LEVELS - 1]] * 2
    rho_ref[0] = n[0]
    for f in range(2):
        up_ref[f, 0] = u[f]
        down_ref[f, LEVELS - 1] = v[f]
    for k in range(1, LEVELS):
        j = LEVELS - 1 - k
        res_u = resist(k)
        res_v = resist(j + 1)
        rho_ref[k] = one * dens_ref[k]
        for f in range(2):
            u[f] = u[f] + n[f] * (res_u * (1.0 / RATIOS[f]))
            n[f] = n[f] + dens_ref[k] * u[f]
            up_ref[f, k] = u[f]
            v[f] = v[f] + m[f] * (res_v * (1.0 / RATIOS[f]))
            m[f] = m[f] + dens_ref[j] * v[f]
            down_ref[f, j] = v[f]
    inv = [1.0 / n[f] for f in range(2)]

    boost = jnp.where(first <= top, 1.0 + MIXED_BOOST, 1.0)
    below = jnp.where(first >= 1, 1.0, 0.0)
    values = []
    for f in range(2):
        values += [
            down_ref[f, 0] * inv[f],
            inv[f],
            up_ref[f, LEVELS - 1] * inv[f],
            boost * (coup_ref[0] * RATIOS[f] * below),
        ]
    coef_ref[...] = pack_coef(values)
    for f in range(2):
        inv_ref[f] = inv[f]
    for copy in copies[:4]:
        copy.wait()
    left_parts, right_parts = [], []
    for index, (ref, select) in enumerate(zip(refs, selects)):
        x = ref[...].reshape(CELLS, LANES)
        parts = [x]
        if x.dtype == F32:
            high = x.astype(jnp.bfloat16)
            rest = x - high.astype(F32)
            mid = rest.astype(jnp.bfloat16)
            parts = [high, mid]
        left_parts += [select] * len(parts)
        right_parts += parts
    total = lax.dot_general(
        jnp.concatenate(left_parts, axis=1), jnp.concatenate(right_parts, axis=1),
        (((1,), (1,)), ((), ())), preferred_element_type=F32,
    )
    left, right = total[0:8], total[8:16]
    far_ref[...] = jnp.where(is_odd, right, left)
    near_ref[...] = jnp.where(is_odd, left, right)
    own_ref[...] = total[16:]
    for copy in copies[4:]:
        copy.wait()


def main_kernel(
    wn_ref, tn_ref, north_ref, w_ref, t_ref, east_ref, visc_ref,
    up_ref, down_ref, rho_ref, inv_ref, coef_ref,
    rhs_ref, sums_ref, dense_ref, packed_ref, face_ref, stencil_ref, ws_ref, ts_ref, sem,
):
    pairs = []
    for src, dst in ((w_ref, ws_ref), (t_ref, ts_ref)):
        pairs.append((src, dst.at[:, PAD:PAD + ROWS]))
        pairs.append((src.at[:, ROWS - PAD:], dst.at[:, :PAD]))
        pairs.append((src.at[:, :PAD], dst.at[:, PAD + ROWS:]))
    copies = [pltpu.make_async_copy(src, dst, sem.at[i]) for i, (src, dst) in enumerate(pairs)]
    for copy in copies:
        copy.start()
    tile = (ROWS, LANES)
    lane = iota(tile, 1)
    inv = [inv_ref[f] for f in range(2)]

    for k in range(LEVELS):
        packed = jnp.where(lane < 16, up_ref[0, k] * inv[0], down_ref[0, k] * inv[0])
        packed = jnp.where(lane < 32, packed, up_ref[1, k] * inv[1])
        packed = jnp.where(lane < 48, packed, down_ref[1, k] * inv[1])
        packed_ref[k] = jnp.where(lane < 64, packed, rho_ref[k])
    dense_ref[...] = pick_lanes(
        lane_selector([0, 16, 32, 48, 64, -1, -1, -1]), packed_ref[...].reshape(CELLS, LANES)
    )

    column = iota((LANES, LANES), 1)
    pair = jnp.where((column >= 2) & (column <= LANES - 4), stencil((1.0, 1.0), 0), 0.0).astype(jnp.bfloat16)
    row, column = iota((LANES, LANES), 0), iota((LANES, LANES), 1)
    near = (row == column) | ((row // ROWS == column // ROWS) & (lax.rem(row + 1, ROWS) == lax.rem(column, ROWS)))
    pair_y = jnp.where(near, 1.0, 0.0).astype(jnp.bfloat16)
    chunk = LANES // ROWS
    face_ref[0] = dot(east_ref[...].reshape(CELLS, LANES), pair).reshape(LEVELS, ROWS, LANES)
    face_ref[1] = dot(visc_ref[...].reshape(CELLS, LANES), pair).reshape(LEVELS, ROWS, LANES)
    for i, ref in enumerate((north_ref, visc_ref)):
        for k in range(0, LEVELS, chunk):
            x = ref[k:k + chunk].reshape(LANES, LANES)
            face_ref[2 + i, k:k + chunk] = dot(pair_y, x).reshape(chunk, ROWS, LANES)
    weights = jnp.concatenate([stencil(c, -2) for c in (MEAN, SKEW, STEP)], axis=1).astype(jnp.bfloat16)
    weights = jnp.concatenate([weights] * 2, axis=0)
    for f, ref in enumerate((w_ref, t_ref)):
        x = ref[...].reshape(CELLS, LANES)
        high = x.astype(jnp.bfloat16)
        low = (x - high.astype(F32)).astype(jnp.bfloat16)
        product = dot(jnp.concatenate([high, low], axis=1), weights)
        for j in range(3):
            stencil_ref[f, j] = product[:, j * LANES:(j + 1) * LANES].reshape(LEVELS, ROWS, LANES)

    for copy in copies:
        copy.wait()

    def level(k, carry):
        weight = rho_ref[k]
        out = []
        for f, (now_ref, sec_ref) in enumerate(((wn_ref, ws_ref), (tn_ref, ts_ref))):
            fx = face_flux(*(stencil_ref[f, j, k] for j in range(3)), face_ref[0, k], face_ref[1, k])
            qy = [sec_ref[k, PAD + s:PAD + s + ROWS] for s in range(-2, 4)]
            fy = flux(qy, face_ref[2, k], face_ref[3, k])
            change = (pltpu.roll(fx, 1, 1) - fx) + (pltpu.roll(fy, 1, 0) - fy)
            explicit = now_ref[k] * (1.0 / 3.0) + (qy[2] + change) * (2.0 / 3.0)
            b = explicit * weight
            rhs_ref[f, k] = b
            out.append(carry[2 * f] + down_ref[f, k] * b)
            out.append(carry[2 * f + 1] + up_ref[f, k] * b)
        return tuple(out)

    def levels(i, carry):
        for step in range(UNROLL):
            carry = level(i * UNROLL + step, carry)
        return carry

    zero = jnp.zeros(tile, F32)
    sums = lax.fori_loop(0, LEVELS // UNROLL, levels, (zero,) * 4)
    for f in range(2):
        sums_ref[f * ROWS:(f + 1) * ROWS] = sums[2 * f] * inv[f]
        sums_ref[(2 + f) * ROWS:(3 + f) * ROWS] = sums[2 * f + 1] * inv[f]
    sums_ref[4 * ROWS:] = coef_ref[...]


def face_spread():
    row = lax.rem(iota((24, LANES), 0), 8)
    lane = iota((24, LANES), 1)
    face = jnp.where(row < 3, row - 1, LANES - 6 + row)
    spread = jnp.where(lane == face, -1.0, 0.0) + jnp.where(lane == face + 1, 1.0, 0.0)
    return jnp.where(row < 6, spread, 0.0).astype(jnp.bfloat16)


def spread_faces(faces):
    return lax.dot_general(
        split3(faces, 0), face_spread(), (((0,), (0,)), ((), ())), preferred_element_type=F32
    )


def edge_kernel(far_ref, near_ref, own_ref, sums_ref, dense_ref, state_ref, faces_ref, strip_ref):
    odd = lax.rem(lax.axis_index("gx"), 2) == 1
    near, far = near_ref[...], far_ref[...]
    left = jnp.where(odd, near, far)
    right = jnp.where(odd, far, near)
    strip_ref[...] = own_ref[...]
    for f in range(2):
        strip_ref[16 * f:16 * f + 3] = left[3 * f:3 * f + 3]
        strip_ref[16 * f + 13:16 * f + 16] = right[3 * f:3 * f + 3]
    for kind in range(2):
        strip_ref[32 + 8 * kind:33 + 8 * kind] = left[6 + kind:7 + kind]
        strip_ref[39 + 8 * kind:40 + 8 * kind] = right[6 + kind:7 + kind]
    faces_ref[...] = jnp.zeros(faces_ref.shape, F32)
    weight = dense_ref[4:5] * (2.0 / 3.0)
    for side in range(2):
        at = 32 + 4 * side
        speed = strip_ref[at:at + 3] + strip_ref[at + 1:at + 4]
        mixing = strip_ref[at + 8:at + 11] + strip_ref[at + 9:at + 12]
        for f in range(2):
            at = 16 * f + 8 * side
            qs = [strip_ref[at + s:at + s + 3] for s in range(6)]
            faces_ref[8 * f + 3 * side:8 * f + 3 * side + 3] = flux(qs, speed, mixing) * weight
    folds = []
    for part in range(2):
        for f in range(2):
            product = faces_ref[8 * f:8 * f + 8] * dense_ref[2 * f + 1 - part:2 * f + 2 - part]
            folded = product[:, :LANES]
            for i in range(1, CELLS // LANES):
                folded = folded + product[:, i * LANES:(i + 1) * LANES]
            folds.append(folded)
    total = spread_faces(jnp.concatenate(folds, axis=1)).reshape(4, LANES // ROWS, ROWS, LANES)
    state_ref[:4 * ROWS] = sums_ref[:4 * ROWS] + jnp.sum(total, axis=1).reshape(4 * ROWS, LANES)
    state_ref[4 * ROWS:] = sums_ref[4 * ROWS:]


def spread_coef(coef, f, i):
    at = 4 * f + i
    return jnp.concatenate([
        jnp.broadcast_to(coef[:, at:at + 1], (COEF, LANES)),
        jnp.broadcast_to(coef[:, at + LANES // 2:at + LANES // 2 + 1], (COEF, LANES)),
    ], axis=0)


def pack_coef(values):
    lane = iota((COEF, LANES), 1)
    coef = jnp.zeros((COEF, LANES), F32)
    for i, value in enumerate(values):
        coef = jnp.where(lane == i, value[:COEF], coef)
        coef = jnp.where(lane == i + LANES // 2, value[COEF:], coef)
    return coef


def unpack(state, f):
    yf = state[f * ROWS:(f + 1) * ROWS]
    yl = state[(2 + f) * ROWS:(3 + f) * ROWS]
    coef = state[4 * ROWS:]
    return (yf, yl, *(spread_coef(coef, f, i) for i in range(4)))


def join(lower, upper):
    yf_a, yl_a, z11_a, z12_a, z22_a, a_a = lower
    yf_b, yl_b, z11_b, z12_b, z22_b, a_b = upper
    g = a_b / (1.0 + a_b * (z22_a + z11_b))
    flow = g * (yl_a - yf_b)
    step_a, step_b = z12_a * g, z12_b * g
    return (
        yf_a - z12_a * flow, yl_b + z12_b * flow,
        z11_a - z12_a * step_a, z12_a * step_b, z22_b - z12_b * step_b, a_a,
    )


def bit(place):
    return lax.rem(lax.div(lax.axis_index("gz"), 1 << place), 2) == 1


def join_pair(own, other, place):
    high = bit(place)
    lower = tuple(jnp.where(high, y, x) for x, y in zip(own, other))
    upper = tuple(jnp.where(high, x, y) for x, y in zip(own, other))
    return join(lower, upper)


def store(state_ref, blocks):
    values = []
    for f, (yf, yl, *coefs) in enumerate(blocks):
        state_ref[f * ROWS:(f + 1) * ROWS] = yf
        state_ref[(2 + f) * ROWS:(3 + f) * ROWS] = yl
        values += coefs
    state_ref[4 * ROWS:] = pack_coef(values)


def four_kernel(own_ref, one_ref, two_ref, three_ref, pair_ref, total_ref):
    pairs, totals = [], []
    for f in range(2):
        own, one, two, three = (unpack(ref[...], f) for ref in (own_ref, one_ref, two_ref, three_ref))
        pairs.append(join_pair(two, three, 0))
        totals.append(join_pair(join_pair(own, one, 0), pairs[f], 1))
    store(total_ref, totals)
    store(pair_ref, pairs)


def local_kernel(
    rhs_ref, up_ref, down_ref, faces_ref, state_ref, one_ref, pair_ref, y_ref, above_ref, below_ref, b_ref
):
    aboves, belows = [], []
    for f in range(2):
        one, pair = unpack(one_ref[...], f), unpack(pair_ref[...], f)
        near, outer = bit(0), bit(1)
        both = join(one, pair)
        aboves.append(tuple(
            jnp.where(near, y, jnp.where(outer, x, z)) for x, y, z in zip(one, pair, both)
        ))
        both = join(pair, one)
        belows.append(tuple(
            jnp.where(near, jnp.where(outer, z, x), y) for x, y, z in zip(one, pair, both)
        ))
    store(above_ref, aboves)
    store(below_ref, belows)
    zero = jnp.zeros((ROWS, LANES), F32)
    coef = state_ref[4 * ROWS:]
    for f in range(2):
        inv = spread_coef(coef, f, 1)
        spread = spread_faces(faces_ref[8 * f:8 * f + 8]).reshape(LEVELS, ROWS, LANES)
        b_ref[f] = (rhs_ref[f] + spread) * inv[None]

    def upward(i, carry):
        carry = list(carry)
        for step in range(UNROLL):
            k = i * UNROLL + step
            for f in range(2):
                carry[f] = carry[f] + up_ref[f, k] * b_ref[f, k]
                y_ref[f, k] = carry[f] * down_ref[f, k]
        return tuple(carry)

    lax.fori_loop(0, LEVELS // UNROLL, upward, (zero, zero))

    def downward(i, carry):
        carry = list(carry)
        for step in range(UNROLL):
            k = LEVELS - 1 - (i * UNROLL + step)
            for f in range(2):
                y_ref[f, k] = y_ref[f, k] + up_ref[f, k] * carry[f]
                carry[f] = carry[f] + down_ref[f, k] * b_ref[f, k]
        return tuple(carry)

    lax.fori_loop(0, LEVELS // UNROLL, downward, (zero, zero))


def above(chain, block, here):
    y, z, a = chain
    yf, yl, z11, z12, z22, a_block = block
    g = a / (1.0 + a * (z + z22))
    new = (yf + z12 * (g * (y - yl)), z11 - z12 * z12 * g, a_block)
    return tuple(jnp.where(here, x, old) for x, old in zip(new, chain))


def below(chain, block, here):
    y, z = chain
    yf, yl, z11, z12, z22, a = block
    g = a / (1.0 + a * (z + z11))
    new = (yl + z12 * (g * (y - yf)), z22 - z12 * z12 * g)
    return tuple(jnp.where(here, x, old) for x, old in zip(new, chain))


def final_kernel(
    y_ref, up_ref, down_ref, own_ref, above_ref, below_ref, a_ref, b_ref, c_ref, w_hbm, t_hbm, out_ref, sem
):
    zero = jnp.zeros((ROWS, LANES), F32)
    own = own_ref[...]
    group = lax.div(lax.axis_index("gz"), 4)
    place = lax.rem(lax.axis_index("gz"), 4)
    others = (a_ref[...], c_ref[...], b_ref[...])
    groups = []
    for j in range(4):
        slot = lax.rem(group, 2) * (1 - 2 * (j % 2)) + j % 2
        slot = slot + 2 * (lax.div(group, 2) * (1 - 2 * (j // 2)) + j // 2)
        groups.append(jnp.where(slot == 1, others[0], jnp.where(slot == 2, others[1], others[2])))
    flows = []
    for f in range(2):
        blocks = [unpack(g, f) for g in groups]
        inner_above, inner_below = unpack(above_ref[...], f), unpack(below_ref[...], f)
        upper, lower = (zero, zero, zero), (zero, zero)
        for j in (3, 2, 1):
            upper = above(upper, blocks[j], j > group)
        for j in (0, 1, 2):
            lower = below(lower, blocks[j], j < group)
        upper = above(upper, inner_above, place < 3)
        lower = below(lower, inner_below, place > 0)
        yf_above, z_above, a_above = upper
        yl_below, z_below = lower
        yf, yl, z11, z12, z22, a = unpack(own, f)
        p = 1.0 + a * (z_below + z11)
        q = 1.0 + a_above * (z_above + z22)
        s_below = a * (yl_below - yf)
        s_above = a_above * (yf_above - yl)
        scale = z12 / (p * q - a * a_above * z12 * z12)
        flows.append((
            (s_below * q - a * z12 * s_above) * scale,
            (s_above * p - a_above * z12 * s_below) * scale,
        ))
    chunk = LEVELS // PARTS
    copies = []
    for part in range(PARTS):
        for f, out in enumerate((w_hbm, t_hbm)):
            for k in range(part * chunk, (part + 1) * chunk):
                out_ref[f, k] = y_ref[f, k] + (down_ref[f, k] * flows[f][0] + up_ref[f, k] * flows[f][1])
            levels = pl.ds(part * chunk, chunk)
            copies.append(pltpu.make_async_copy(
                out_ref.at[f, levels], out.at[levels], sem.at[2 * part + f]
            ))
            copies[-1].start()
    for copy in copies:
        copy.wait()


def call(kernel, shapes, in_specs, scratch=(), out_specs=None, flops=0):
    shapes = [s if isinstance(s, jax.ShapeDtypeStruct) else jax.ShapeDtypeStruct(s, F32) for s in shapes]
    return pl.pallas_call(
        kernel,
        out_shape=shapes,
        in_specs=in_specs,
        out_specs=out_specs or [VMEM] * len(shapes),
        scratch_shapes=list(scratch),
        compiler_params=PARAMS,
        cost_estimate=pl.CostEstimate(flops=flops, bytes_accessed=flops // 8, transcendentals=0),
    )


def shards(
    vertical_now, vertical_section, theta_now, theta_section,
    east_wind, north_wind, eddy_viscosity, density, coupling, cloud_top,
):
    strip = (8, CELLS)
    count = 16
    part = (LEVELS, ROWS, LANES)
    block = (2, *part)
    state_shape = (STATE, LANES)
    wide = jax.ShapeDtypeStruct(part, F32)
    half = jax.ShapeDtypeStruct(part, jnp.bfloat16)
    tall = (LEVELS, ROWS + 2 * PAD, LANES)

    def in_hbm(*arrays):
        return [pltpu.with_memory_space_constraint(x, pltpu.HBM) for x in arrays]

    tile = (ROWS, LANES)
    ws, ts, east, visc, wn, tn, north, far, near, own, up, down, rho, inv, coef = call(
        pack_kernel,
        [wide, wide, half, half, wide, wide, half, strip, strip, (48, CELLS), block, block, part, (2, *tile), (COEF, LANES)],
        [HBM] * 10,
        [
            pltpu.SMEM((LEVELS,), F32),
            pltpu.SMEM((LEVELS,), F32),
            pltpu.SMEM((1, ROWS), jnp.int32),
            pltpu.SemaphoreType.DMA((3,)),
            pltpu.SemaphoreType.DMA((7,)),
        ],
    )(*in_hbm(
        vertical_section, theta_section, east_wind, eddy_viscosity, vertical_now, theta_now, north_wind,
        density, coupling, cloud_top.reshape(1, ROWS),
    ))
    far = lax.ppermute(
        far, "gx", [(i, (i + 1) % count if i % 2 else (i - 1) % count) for i in range(count)]
    )
    near = lax.ppermute(near, "gx", [(i, i ^ 1) for i in range(count)])
    rhs, sums, dense = call(
        main_kernel,
        [block, state_shape, strip],
        [VMEM] * 12,
        [
            pltpu.VMEM(part, F32),
            pltpu.VMEM((4, *part), F32),
            pltpu.VMEM((2, 3, *part), F32),
            pltpu.VMEM(tall, F32),
            pltpu.VMEM(tall, F32),
            pltpu.SemaphoreType.DMA((6,)),
        ],
        flops=16_000_000,
    )(
        wn, tn, north, ws, ts, east, visc, up, down, rho, inv, coef,
    )
    state, faces = call(
        edge_kernel, [state_shape, (16, CELLS)], [VMEM] * 5, [pltpu.VMEM((48, CELLS), F32)]
    )(far, near, own, sums, dense)

    def swap(x, partner):
        return lax.ppermute(x, "gz", [(i, partner(i)) for i in range(count)])

    three, two, one = (swap(state, lambda i, k=k: i ^ k) for k in (3, 2, 1))
    pair, four = call(four_kernel, [state_shape] * 2, [VMEM] * 4)(state, one, two, three)
    y, inner_above, inner_below = call(
        local_kernel, [block, state_shape, state_shape], [VMEM] * 7, [pltpu.VMEM(block, F32)], flops=4_000_000
    )(rhs, up, down, faces, state, one, pair)
    side_a = swap(four, lambda i: i ^ 4)
    side_b = swap(four, lambda i: (i + 4 if i & 4 else i - 4) % count)
    side_c = swap(four, lambda i: FAR_GROUP[i // 2] * 2 + i % 2)
    return tuple(call(
        final_kernel,
        [part, part],
        [VMEM] * 9,
        [pltpu.VMEM(block, F32), pltpu.SemaphoreType.DMA((2 * PARTS,))],
        [HBM] * 2,
    )(y, up, down, state, inner_above, inner_below, side_a, side_b, side_c))


def solution(mesh):
    wide = P("gz", None, "gx")
    return jax.shard_map(
        shards,
        mesh=mesh,
        in_specs=(wide,) * 7 + (P("gz"), P("gz"), P(None, "gx")),
        out_specs=(wide, wide),
        check_vma=False,
    )
```

```python
import jax
import jax.numpy as jnp
from jax import lax
from jax.experimental import pallas as pl
from jax.experimental.pallas import tpu as pltpu
from jax.sharding import PartitionSpec as P

COURANT = 0.25
MIXED_BOOST = 4.0
HEAT_RATIO = 3.0
RATIOS = (1.0, HEAT_RATIO)
LEVELS = 40
ROWS = 16
LANES = 128
CELLS = LEVELS * ROWS
COEF = 8
STATE = 4 * ROWS + COEF
PAD = 8
FAR_GROUP = (5, 4, 7, 6, 1, 0, 3, 2)
PARTS = 2
UNROLL = 20
HBM = pl.BlockSpec(memory_space=pltpu.HBM)
VMEM = pl.BlockSpec(memory_space=pltpu.VMEM)
SMEM = pl.BlockSpec(memory_space=pltpu.SMEM)
PARAMS = pltpu.CompilerParams(vmem_limit_bytes=32 * 1024 * 1024)
F32 = jnp.float32


def iota(shape, dim):
    return lax.broadcasted_iota(jnp.int32, shape, dim)


def split3(x, axis):
    high = x.astype(jnp.bfloat16)
    rest = x - high.astype(F32)
    mid = rest.astype(jnp.bfloat16)
    low = (rest - mid.astype(F32)).astype(jnp.bfloat16)
    return jnp.concatenate([high, mid, low], axis=axis)


MEAN = (1.0, -8.0, 37.0, 37.0, -8.0, 1.0)
SKEW = (1.0, -5.0, 10.0, -10.0, 5.0, -1.0)
STEP = (0.0, 0.0, 1.0, -1.0, 0.0, 0.0)


def face_flux(mean, skew, step, speed_sum, mixing_sum):
    speed = speed_sum * (0.5 * COURANT / 60.0)
    return speed * mean + jnp.abs(speed) * skew + (0.5 * mixing_sum) * step


def flux(qs, speed_sum, mixing_sum):
    qm2, qm1, q0, q1, q2, q3 = qs
    step = q0 - q1
    mean = (qm2 + q3) - 8.0 * (qm1 + q2) + 37.0 * (q0 + q1)
    skew = (qm2 - q3) - 5.0 * (qm1 - q2) + 10.0 * step
    return face_flux(mean, skew, step, speed_sum, mixing_sum)


def stencil(coefs, first):
    offset = iota((LANES, LANES), 0) - iota((LANES, LANES), 1) - first
    out = jnp.zeros((LANES, LANES), F32)
    for s, coef in enumerate(coefs):
        if coef:
            out = jnp.where(offset == s, coef, out)
    return out


def dot(x, y):
    return lax.dot_general(x, y, (((1,), (0,)), ((), ())), preferred_element_type=F32)


def strip_selectors():
    rows = [[-1] * 64 for _ in range(4)]
    for field in range(2):
        for cell in range(3):
            rows[field][3 * field + cell] = cell
            rows[field][8 + 3 * field + cell] = LANES - 3 + cell
        for cell in range(5):
            rows[field][16 + 16 * field + 3 + cell] = cell
            rows[field][24 + 16 * field + cell] = LANES - 5 + cell
    for kind in range(2):
        rows[2 + kind][6 + kind] = 0
        rows[2 + kind][14 + kind] = LANES - 1
        for cell in range(3):
            rows[2 + kind][48 + 8 * kind + 1 + cell] = cell
            rows[2 + kind][48 + 8 * kind + 4 + cell] = LANES - 3 + cell
    return rows


def lane_selector(lanes):
    row = iota((len(lanes), LANES), 0)
    lane = iota((len(lanes), LANES), 1)
    hit = jnp.zeros((len(lanes), LANES), jnp.bool_)
    start = 0
    while start < len(lanes):
        if lanes[start] < 0:
            start += 1
            continue
        stop = start + 1
        while stop < len(lanes) and lanes[stop] == lanes[stop - 1] + 1:
            stop += 1
        hit = hit | ((row >= start) & (row < stop) & (lane - row == lanes[start] - start))
        start = stop
    return jnp.where(hit, 1.0, 0.0).astype(jnp.bfloat16)


def pick_lanes(select, x):
    dims = (((1,), (1,)), ((), ()))
    if x.dtype == jnp.bfloat16:
        return lax.dot_general(select, x, dims, preferred_element_type=F32)
    high = x.astype(jnp.bfloat16)
    rest = x - high.astype(F32)
    mid = rest.astype(jnp.bfloat16)
    low = (rest - mid.astype(F32)).astype(jnp.bfloat16)
    parts = [lax.dot_general(select, p, dims, preferred_element_type=F32) for p in (high, mid, low)]
    return parts[0] + (parts[1] + parts[2])


def pack_kernel(
    ws_hbm, ts_hbm, east_hbm, visc_hbm, wn_hbm, tn_hbm, north_hbm, dens_hbm, coup_hbm, top_hbm,
    ws_ref, ts_ref, east_ref, visc_ref, wn_ref, tn_ref, north_ref, parts_ref, far_ref, near_ref, own_ref,
    up_ref, down_ref, rho_ref, inv_ref, coef_ref,
    dens_ref, coup_ref, top_ref, small_sem, sem,
):
    small = [
        pltpu.make_async_copy(src, dst, small_sem.at[i])
        for i, (src, dst) in enumerate(
            ((dens_hbm, dens_ref), (coup_hbm, coup_ref), (top_hbm, top_ref))
        )
    ]
    for copy in small:
        copy.start()
    refs = (ws_ref, ts_ref, east_ref, visc_ref)
    sources = (ws_hbm, ts_hbm, east_hbm, visc_hbm, wn_hbm, tn_hbm, north_hbm)
    targets = (*refs, wn_ref, tn_ref, north_ref)
    copies = [
        pltpu.make_async_copy(src, dst, sem.at[i]) for i, (src, dst) in enumerate(zip(sources, targets))
    ]
    for copy in copies:
        copy.start()
    selects = [lane_selector(lanes) for lanes in strip_selectors()]
    is_odd = lax.rem(lax.axis_index("gx"), 2) == 1
    for copy in small:
        copy.wait()

    first = lax.axis_index("gz") * LEVELS
    tile = (ROWS, LANES)
    row = iota(tile, 0)
    one = jnp.ones(tile, F32)
    top = jnp.zeros(tile, jnp.int32)
    for j in range(ROWS):
        top = jnp.where(row == j, top_ref[0, j], top)

    def resist(k):
        boost = jnp.where(first + k <= top, 1.0 / (1.0 + MIXED_BOOST), 1.0)
        return boost / (one * coup_ref[k])

    u = [one, one]
    v = [one, one]
    n = [one * dens_ref[0]] * 2
    m = [one * dens_ref[LEVELS - 1]] * 2
    rho_ref[0] = n[0]
    for f in range(2):
        up_ref[f, 0] = u[f]
        down_ref[f, LEVELS - 1] = v[f]
    for k in range(1, LEVELS):
        j = LEVELS - 1 - k
        res_u = resist(k)
        res_v = resist(j + 1)
        rho_ref[k] = one * dens_ref[k]
        for f in range(2):
            u[f] = u[f] + n[f] * (res_u * (1.0 / RATIOS[f]))
            n[f] = n[f] + dens_ref[k] * u[f]
            up_ref[f, k] = u[f]
            v[f] = v[f] + m[f] * (res_v * (1.0 / RATIOS[f]))
            m[f] = m[f] + dens_ref[j] * v[f]
            down_ref[f, j] = v[f]
    inv = [1.0 / n[f] for f in range(2)]

    boost = jnp.where(first <= top, 1.0 + MIXED_BOOST, 1.0)
    below = jnp.where(first >= 1, 1.0, 0.0)
    values = []
    for f in range(2):
        values += [
            down_ref[f, 0] * inv[f],
            inv[f],
            up_ref[f, LEVELS - 1] * inv[f],
            boost * (coup_ref[0] * RATIOS[f] * below),
        ]
    coef_ref[...] = pack_coef(values)
    for f in range(2):
        inv_ref[f] = inv[f]
    for copy in copies[:4]:
        copy.wait()
    left_parts, right_parts = [], []
    for index, (ref, select) in enumerate(zip(refs, selects)):
        x = ref[...].reshape(CELLS, LANES)
        parts = [x]
        if x.dtype == F32:
            high = x.astype(jnp.bfloat16)
            rest = x - high.astype(F32)
            mid = rest.astype(jnp.bfloat16)
            parts = [high, mid]
            for j, value in enumerate(parts):
                parts_ref[index, :, j * LANES:(j + 1) * LANES] = value
        left_parts += [select] * len(parts)
        right_parts += parts
    total = lax.dot_general(
        jnp.concatenate(left_parts, axis=1), jnp.concatenate(right_parts, axis=1),
        (((1,), (1,)), ((), ())), preferred_element_type=F32,
    )
    left, right = total[0:8], total[8:16]
    far_ref[...] = jnp.where(is_odd, right, left)
    near_ref[...] = jnp.where(is_odd, left, right)
    own_ref[...] = total[16:]
    for copy in copies[4:]:
        copy.wait()


def main_kernel(
    wn_ref, tn_ref, north_ref, w_ref, t_ref, east_ref, visc_ref, parts_ref,
    up_ref, down_ref, rho_ref, inv_ref, coef_ref,
    rhs_ref, sums_ref, dense_ref, packed_ref, face_ref, stencil_ref, ws_ref, ts_ref, sem,
):
    pairs = []
    for src, dst in ((w_ref, ws_ref), (t_ref, ts_ref)):
        pairs.append((src, dst.at[:, PAD:PAD + ROWS]))
        pairs.append((src.at[:, ROWS - PAD:], dst.at[:, :PAD]))
        pairs.append((src.at[:, :PAD], dst.at[:, PAD + ROWS:]))
    copies = [pltpu.make_async_copy(src, dst, sem.at[i]) for i, (src, dst) in enumerate(pairs)]
    for copy in copies:
        copy.start()
    tile = (ROWS, LANES)
    lane = iota(tile, 1)
    inv = [inv_ref[f] for f in range(2)]

    for k in range(LEVELS):
        packed = jnp.where(lane < 16, up_ref[0, k] * inv[0], down_ref[0, k] * inv[0])
        packed = jnp.where(lane < 32, packed, up_ref[1, k] * inv[1])
        packed = jnp.where(lane < 48, packed, down_ref[1, k] * inv[1])
        packed_ref[k] = jnp.where(lane < 64, packed, rho_ref[k])
    dense_ref[...] = pick_lanes(
        lane_selector([0, 16, 32, 48, 64, -1, -1, -1]), packed_ref[...].reshape(CELLS, LANES)
    )

    column = iota((LANES, LANES), 1)
    pair = jnp.where((column >= 2) & (column <= LANES - 4), stencil((1.0, 1.0), 0), 0.0).astype(jnp.bfloat16)
    row, column = iota((LANES, LANES), 0), iota((LANES, LANES), 1)
    near = (row == column) | ((row // ROWS == column // ROWS) & (lax.rem(row + 1, ROWS) == lax.rem(column, ROWS)))
    pair_y = jnp.where(near, 1.0, 0.0).astype(jnp.bfloat16)
    chunk = LANES // ROWS
    face_ref[0] = dot(east_ref[...].reshape(CELLS, LANES), pair).reshape(LEVELS, ROWS, LANES)
    face_ref[1] = dot(visc_ref[...].reshape(CELLS, LANES), pair).reshape(LEVELS, ROWS, LANES)
    for i, ref in enumerate((north_ref, visc_ref)):
        for k in range(0, LEVELS, chunk):
            x = ref[k:k + chunk].reshape(LANES, LANES)
            face_ref[2 + i, k:k + chunk] = dot(pair_y, x).reshape(chunk, ROWS, LANES)
    weights = jnp.concatenate([stencil(c, -2) for c in (MEAN, SKEW, STEP)], axis=1).astype(jnp.bfloat16)
    weights = jnp.concatenate([weights] * 2, axis=0)
    for f in range(2):
        product = dot(parts_ref[f], weights)
        for j in range(3):
            stencil_ref[f, j] = product[:, j * LANES:(j + 1) * LANES].reshape(LEVELS, ROWS, LANES)

    for copy in copies:
        copy.wait()

    def level(k, carry):
        weight = rho_ref[k]
        out = []
        for f, (now_ref, sec_ref) in enumerate(((wn_ref, ws_ref), (tn_ref, ts_ref))):
            fx = face_flux(*(stencil_ref[f, j, k] for j in range(3)), face_ref[0, k], face_ref[1, k])
            qy = [sec_ref[k, PAD + s:PAD + s + ROWS] for s in range(-2, 4)]
            fy = flux(qy, face_ref[2, k], face_ref[3, k])
            change = (pltpu.roll(fx, 1, 1) - fx) + (pltpu.roll(fy, 1, 0) - fy)
            explicit = now_ref[k] * (1.0 / 3.0) + (qy[2] + change) * (2.0 / 3.0)
            b = explicit * weight
            rhs_ref[f, k] = b
            out.append(carry[2 * f] + down_ref[f, k] * b)
            out.append(carry[2 * f + 1] + up_ref[f, k] * b)
        return tuple(out)

    def levels(i, carry):
        for step in range(UNROLL):
            carry = level(i * UNROLL + step, carry)
        return carry

    zero = jnp.zeros(tile, F32)
    sums = lax.fori_loop(0, LEVELS // UNROLL, levels, (zero,) * 4)
    for f in range(2):
        sums_ref[f * ROWS:(f + 1) * ROWS] = sums[2 * f] * inv[f]
        sums_ref[(2 + f) * ROWS:(3 + f) * ROWS] = sums[2 * f + 1] * inv[f]
    sums_ref[4 * ROWS:] = coef_ref[...]


def face_spread():
    row = lax.rem(iota((24, LANES), 0), 8)
    lane = iota((24, LANES), 1)
    face = jnp.where(row < 3, row - 1, LANES - 6 + row)
    spread = jnp.where(lane == face, -1.0, 0.0) + jnp.where(lane == face + 1, 1.0, 0.0)
    return jnp.where(row < 6, spread, 0.0).astype(jnp.bfloat16)


def spread_faces(faces):
    return lax.dot_general(
        split3(faces, 0), face_spread(), (((0,), (0,)), ((), ())), preferred_element_type=F32
    )


def edge_kernel(far_ref, near_ref, own_ref, sums_ref, dense_ref, state_ref, faces_ref, strip_ref):
    odd = lax.rem(lax.axis_index("gx"), 2) == 1
    near, far = near_ref[...], far_ref[...]
    left = jnp.where(odd, near, far)
    right = jnp.where(odd, far, near)
    strip_ref[...] = own_ref[...]
    for f in range(2):
        strip_ref[16 * f:16 * f + 3] = left[3 * f:3 * f + 3]
        strip_ref[16 * f + 13:16 * f + 16] = right[3 * f:3 * f + 3]
    for kind in range(2):
        strip_ref[32 + 8 * kind:33 + 8 * kind] = left[6 + kind:7 + kind]
        strip_ref[39 + 8 * kind:40 + 8 * kind] = right[6 + kind:7 + kind]
    faces_ref[...] = jnp.zeros(faces_ref.shape, F32)
    weight = dense_ref[4:5] * (2.0 / 3.0)
    for side in range(2):
        at = 32 + 4 * side
        speed = strip_ref[at:at + 3] + strip_ref[at + 1:at + 4]
        mixing = strip_ref[at + 8:at + 11] + strip_ref[at + 9:at + 12]
        for f in range(2):
            at = 16 * f + 8 * side
            qs = [strip_ref[at + s:at + s + 3] for s in range(6)]
            faces_ref[8 * f + 3 * side:8 * f + 3 * side + 3] = flux(qs, speed, mixing) * weight
    folds = []
    for part in range(2):
        for f in range(2):
            product = faces_ref[8 * f:8 * f + 8] * dense_ref[2 * f + 1 - part:2 * f + 2 - part]
            folded = product[:, :LANES]
            for i in range(1, CELLS // LANES):
                folded = folded + product[:, i * LANES:(i + 1) * LANES]
            folds.append(folded)
    total = spread_faces(jnp.concatenate(folds, axis=1)).reshape(4, LANES // ROWS, ROWS, LANES)
    state_ref[:4 * ROWS] = sums_ref[:4 * ROWS] + jnp.sum(total, axis=1).reshape(4 * ROWS, LANES)
    state_ref[4 * ROWS:] = sums_ref[4 * ROWS:]


def spread_coef(coef, f, i):
    at = 4 * f + i
    return jnp.concatenate([
        jnp.broadcast_to(coef[:, at:at + 1], (COEF, LANES)),
        jnp.broadcast_to(coef[:, at + LANES // 2:at + LANES // 2 + 1], (COEF, LANES)),
    ], axis=0)


def pack_coef(values):
    lane = iota((COEF, LANES), 1)
    coef = jnp.zeros((COEF, LANES), F32)
    for i, value in enumerate(values):
        coef = jnp.where(lane == i, value[:COEF], coef)
        coef = jnp.where(lane == i + LANES // 2, value[COEF:], coef)
    return coef


def unpack(state, f):
    yf = state[f * ROWS:(f + 1) * ROWS]
    yl = state[(2 + f) * ROWS:(3 + f) * ROWS]
    coef = state[4 * ROWS:]
    return (yf, yl, *(spread_coef(coef, f, i) for i in range(4)))


def join(lower, upper):
    yf_a, yl_a, z11_a, z12_a, z22_a, a_a = lower
    yf_b, yl_b, z11_b, z12_b, z22_b, a_b = upper
    g = a_b / (1.0 + a_b * (z22_a + z11_b))
    flow = g * (yl_a - yf_b)
    step_a, step_b = z12_a * g, z12_b * g
    return (
        yf_a - z12_a * flow, yl_b + z12_b * flow,
        z11_a - z12_a * step_a, z12_a * step_b, z22_b - z12_b * step_b, a_a,
    )


def bit(place):
    return lax.rem(lax.div(lax.axis_index("gz"), 1 << place), 2) == 1


def join_pair(own, other, place):
    high = bit(place)
    lower = tuple(jnp.where(high, y, x) for x, y in zip(own, other))
    upper = tuple(jnp.where(high, x, y) for x, y in zip(own, other))
    return join(lower, upper)


def store(state_ref, blocks):
    values = []
    for f, (yf, yl, *coefs) in enumerate(blocks):
        state_ref[f * ROWS:(f + 1) * ROWS] = yf
        state_ref[(2 + f) * ROWS:(3 + f) * ROWS] = yl
        values += coefs
    state_ref[4 * ROWS:] = pack_coef(values)


def four_kernel(own_ref, one_ref, two_ref, three_ref, pair_ref, total_ref):
    pairs, totals = [], []
    for f in range(2):
        own, one, two, three = (unpack(ref[...], f) for ref in (own_ref, one_ref, two_ref, three_ref))
        pairs.append(join_pair(two, three, 0))
        totals.append(join_pair(join_pair(own, one, 0), pairs[f], 1))
    store(total_ref, totals)
    store(pair_ref, pairs)


def local_kernel(
    rhs_ref, up_ref, down_ref, faces_ref, state_ref, one_ref, pair_ref, y_ref, above_ref, below_ref, own_ref, b_ref
):
    aboves, belows = [], []
    for f in range(2):
        one, pair = unpack(one_ref[...], f), unpack(pair_ref[...], f)
        near, outer = bit(0), bit(1)
        both = join(one, pair)
        aboves.append(tuple(
            jnp.where(near, y, jnp.where(outer, x, z)) for x, y, z in zip(one, pair, both)
        ))
        both = join(pair, one)
        belows.append(tuple(
            jnp.where(near, jnp.where(outer, z, x), y) for x, y, z in zip(one, pair, both)
        ))
    owns = [unpack(state_ref[...], f) for f in range(2)]
    for ref, blocks in ((above_ref, aboves), (below_ref, belows), (own_ref, owns)):
        for f in range(2):
            for i in range(6):
                ref[f, i] = blocks[f][i]
    zero = jnp.zeros((ROWS, LANES), F32)
    coef = state_ref[4 * ROWS:]
    for f in range(2):
        inv = spread_coef(coef, f, 1)
        spread = spread_faces(faces_ref[8 * f:8 * f + 8]).reshape(LEVELS, ROWS, LANES)
        b_ref[f] = (rhs_ref[f] + spread) * inv[None]

    def upward(i, carry):
        carry = list(carry)
        for step in range(UNROLL):
            k = i * UNROLL + step
            for f in range(2):
                carry[f] = carry[f] + up_ref[f, k] * b_ref[f, k]
                y_ref[f, k] = carry[f] * down_ref[f, k]
        return tuple(carry)

    lax.fori_loop(0, LEVELS // UNROLL, upward, (zero, zero))

    def downward(i, carry):
        carry = list(carry)
        for step in range(UNROLL):
            k = LEVELS - 1 - (i * UNROLL + step)
            for f in range(2):
                y_ref[f, k] = y_ref[f, k] + up_ref[f, k] * carry[f]
                carry[f] = carry[f] + down_ref[f, k] * b_ref[f, k]
        return tuple(carry)

    lax.fori_loop(0, LEVELS // UNROLL, downward, (zero, zero))


def above(chain, block, here):
    y, z, a = chain
    yf, yl, z11, z12, z22, a_block = block
    g = a / (1.0 + a * (z + z22))
    new = (yf + z12 * (g * (y - yl)), z11 - z12 * z12 * g, a_block)
    return tuple(jnp.where(here, x, old) for x, old in zip(new, chain))


def below(chain, block, here):
    y, z = chain
    yf, yl, z11, z12, z22, a = block
    g = a / (1.0 + a * (z + z11))
    new = (yl + z12 * (g * (y - yf)), z22 - z12 * z12 * g)
    return tuple(jnp.where(here, x, old) for x, old in zip(new, chain))


def final_kernel(
    y_ref, up_ref, down_ref, own_ref, above_ref, below_ref, a_ref, b_ref, c_ref, w_hbm, t_hbm, out_ref, sem
):
    zero = jnp.zeros((ROWS, LANES), F32)
    group = lax.div(lax.axis_index("gz"), 4)
    place = lax.rem(lax.axis_index("gz"), 4)
    slots = []
    for j in range(4):
        slot = lax.rem(group, 2) * (1 - 2 * (j % 2)) + j % 2
        slots.append(slot + 2 * (lax.div(group, 2) * (1 - 2 * (j // 2)) + j // 2))
    flows = []
    for f in range(2):
        others = [unpack(ref[...], f) for ref in (a_ref, c_ref, b_ref)]
        blocks = [
            tuple(jnp.where(slot == 1, x, jnp.where(slot == 2, y, z)) for x, y, z in zip(*others))
            for slot in slots
        ]
        inner_above, inner_below = (tuple(ref[f, i] for i in range(6)) for ref in (above_ref, below_ref))
        upper, lower = (zero, zero, zero), (zero, zero)
        for j in (3, 2, 1):
            upper = above(upper, blocks[j], j > group)
        for j in (0, 1, 2):
            lower = below(lower, blocks[j], j < group)
        upper = above(upper, inner_above, place < 3)
        lower = below(lower, inner_below, place > 0)
        yf_above, z_above, a_above = upper
        yl_below, z_below = lower
        yf, yl, z11, z12, z22, a = (own_ref[f, i] for i in range(6))
        p = 1.0 + a * (z_below + z11)
        q = 1.0 + a_above * (z_above + z22)
        s_below = a * (yl_below - yf)
        s_above = a_above * (yf_above - yl)
        scale = z12 / (p * q - a * a_above * z12 * z12)
        flows.append((
            (s_below * q - a * z12 * s_above) * scale,
            (s_above * p - a_above * z12 * s_below) * scale,
        ))
    chunk = LEVELS // PARTS
    copies = []
    for part in range(PARTS):
        for f, out in enumerate((w_hbm, t_hbm)):
            for k in range(part * chunk, (part + 1) * chunk):
                out_ref[f, k] = y_ref[f, k] + (down_ref[f, k] * flows[f][0] + up_ref[f, k] * flows[f][1])
            levels = pl.ds(part * chunk, chunk)
            copies.append(pltpu.make_async_copy(
                out_ref.at[f, levels], out.at[levels], sem.at[2 * part + f]
            ))
            copies[-1].start()
    for copy in copies:
        copy.wait()


def call(kernel, shapes, in_specs, scratch=(), out_specs=None, flops=0):
    shapes = [s if isinstance(s, jax.ShapeDtypeStruct) else jax.ShapeDtypeStruct(s, F32) for s in shapes]
    return pl.pallas_call(
        kernel,
        out_shape=shapes,
        in_specs=in_specs,
        out_specs=out_specs or [VMEM] * len(shapes),
        scratch_shapes=list(scratch),
        compiler_params=PARAMS,
        cost_estimate=pl.CostEstimate(flops=flops, bytes_accessed=flops // 8, transcendentals=0),
    )


def shards(
    vertical_now, vertical_section, theta_now, theta_section,
    east_wind, north_wind, eddy_viscosity, density, coupling, cloud_top,
):
    strip = (8, CELLS)
    count = 16
    part = (LEVELS, ROWS, LANES)
    block = (2, *part)
    state_shape = (STATE, LANES)
    wide = jax.ShapeDtypeStruct(part, F32)
    half = jax.ShapeDtypeStruct(part, jnp.bfloat16)
    split = jax.ShapeDtypeStruct((2, CELLS, 2 * LANES), jnp.bfloat16)
    tall = (LEVELS, ROWS + 2 * PAD, LANES)

    def in_hbm(*arrays):
        return [pltpu.with_memory_space_constraint(x, pltpu.HBM) for x in arrays]

    tile = (ROWS, LANES)
    ws, ts, east, visc, wn, tn, north, parts, far, near, own, up, down, rho, inv, coef = call(
        pack_kernel,
        [wide, wide, half, half, wide, wide, half, split, strip, strip, (48, CELLS), block, block, part, (2, *tile), (COEF, LANES)],
        [HBM] * 10,
        [
            pltpu.SMEM((LEVELS,), F32),
            pltpu.SMEM((LEVELS,), F32),
            pltpu.SMEM((1, ROWS), jnp.int32),
            pltpu.SemaphoreType.DMA((3,)),
            pltpu.SemaphoreType.DMA((7,)),
        ],
    )(*in_hbm(
        vertical_section, theta_section, east_wind, eddy_viscosity, vertical_now, theta_now, north_wind,
        density, coupling, cloud_top.reshape(1, ROWS),
    ))
    far = lax.ppermute(
        far, "gx", [(i, (i + 1) % count if i % 2 else (i - 1) % count) for i in range(count)]
    )
    near = lax.ppermute(near, "gx", [(i, i ^ 1) for i in range(count)])
    rhs, sums, dense = call(
        main_kernel,
        [block, state_shape, strip],
        [VMEM] * 13,
        [
            pltpu.VMEM(part, F32),
            pltpu.VMEM((4, *part), F32),
            pltpu.VMEM((2, 3, *part), F32),
            pltpu.VMEM(tall, F32),
            pltpu.VMEM(tall, F32),
            pltpu.SemaphoreType.DMA((6,)),
        ],
        flops=16_000_000,
    )(
        wn, tn, north, ws, ts, east, visc, parts, up, down, rho, inv, coef,
    )
    state, faces = call(
        edge_kernel, [state_shape, (16, CELLS)], [VMEM] * 5, [pltpu.VMEM((48, CELLS), F32)]
    )(far, near, own, sums, dense)

    def swap(x, partner):
        return lax.ppermute(x, "gz", [(i, partner(i)) for i in range(count)])

    three, two, one = (swap(state, lambda i, k=k: i ^ k) for k in (3, 2, 1))
    pair, four = call(four_kernel, [state_shape] * 2, [VMEM] * 4)(state, one, two, three)
    spread = (2, 6, ROWS, LANES)
    y, inner_above, inner_below, own_spread = call(
        local_kernel, [block, spread, spread, spread], [VMEM] * 7, [pltpu.VMEM(block, F32)], flops=4_000_000
    )(rhs, up, down, faces, state, one, pair)
    side_a = swap(four, lambda i: i ^ 4)
    side_b = swap(four, lambda i: (i + 4 if i & 4 else i - 4) % count)
    side_c = swap(four, lambda i: FAR_GROUP[i // 2] * 2 + i % 2)
    return tuple(call(
        final_kernel,
        [part, part],
        [VMEM] * 9,
        [pltpu.VMEM(block, F32), pltpu.SemaphoreType.DMA((2 * PARTS,))],
        [HBM] * 2,
    )(y, up, down, own_spread, inner_above, inner_below, side_a, side_b, side_c))


def solution(mesh):
    wide = P("gz", None, "gx")
    return jax.shard_map(
        shards,
        mesh=mesh,
        in_specs=(wide,) * 7 + (P("gz"), P("gz"), P(None, "gx")),
        out_specs=(wide, wide),
        check_vma=False,
    )
```
